32 devices in a mesh: ctx: 16 (over z, y, x), wt: 2 (over core).
Axes of the slice: x: 2, y: 2, z: 4, core: 2. Of those that a mesh axis runs over, the one named last changes fastest.
Arguments:
- inputs: bfloat16 [16, 256, 4, 768], P('ctx'), may hold values from -6 to 6
- cotangent: bfloat16 [16, 256, 4, 768], P('ctx'), may hold values from -6 to 6
- lengths: int32 [4], replicated, may hold values from 1024 to 4096, as said below
- block_pairs: int32 [16], replicated, may hold values from 0 to 15, each once
- routes: int32 [16, 256, 4, 2], P('ctx'), may hold values from 0 to 15, all different within a row; in each aligned block of 1024 rows (0 to 1023, 1024 to 2047, ..., all dimensions but the last counted through in order) at most 160 rows name the same one
- attn_gain: float32 [768], replicated, may hold values from 0.25 to 1.75
- query_weight: bfloat16 [768, 768], P(None, 'wt'), may hold values from -0.21875 to 0.21875
- key_weight: bfloat16 [768, 768], P(None, 'wt'), may hold values from -0.21875 to 0.21875
- value_weight: bfloat16 [768, 768], P(None, 'wt'), may hold values from -0.21875 to 0.21875
- out_weight: bfloat16 [768, 768], P('wt'), may hold values from -1.75 to 1.75
- ffn_gain: float32 [768], replicated, may hold values from 0.25 to 1.75
- router_weight: bfloat16 [768, 16], replicated, may hold values from -0.15625 to 0.15625
- expert_gate: bfloat16 [16, 768, 2048], P(None, None, 'wt'), may hold values from -0.21875 to 0.21875
- expert_up: bfloat16 [16, 768, 2048], P(None, None, 'wt'), may hold values from -0.21875 to 0.21875
- expert_down: bfloat16 [16, 2048, 768], P(None, 'wt'), may hold values from -0.125 to 0.125
- dense_gate: bfloat16 [768, 2048], P(None, 'wt'), may hold values from -0.21875 to 0.21875
- dense_up: bfloat16 [768, 2048], P(None, 'wt'), may hold values from -0.21875 to 0.21875
- dense_down: bfloat16 [2048, 768], P('wt'), may hold values from -0.125 to 0.125
Outputs:
- output: bfloat16 [16, 256, 4, 768], P('ctx')
- grad_inputs: bfloat16 [16, 256, 4, 768], P('ctx')
- grad_attn_gain: float32 [768], P('ctx')
- grad_query: float32 [768, 768], P('ctx', 'wt')
- grad_key: float32 [768, 768], P('ctx', 'wt')
- grad_value: float32 [768, 768], P('ctx', 'wt')
- grad_out: float32 [768, 768], P('wt', 'ctx')
- grad_ffn_gain: float32 [768], P('ctx')
- grad_router: float32 [768, 16], P('ctx')
- grad_expert_gate: float32 [16, 768, 2048], P(None, 'ctx', 'wt')
- grad_expert_up: float32 [16, 768, 2048], P(None, 'ctx', 'wt')
- grad_expert_down: float32 [16, 2048, 768], P(None, 'wt', 'ctx')
- grad_dense_gate: float32 [768, 2048], P('ctx', 'wt')
- grad_dense_up: float32 [768, 2048], P('ctx', 'wt')
- grad_dense_down: float32 [2048, 768], P('wt', 'ctx')
The draws below stay inside these ranges and needn't reach their ends.
Inputs may be any that keep to these rules, and one draw needn't show every extreme that they name: `lengths`: one slot chosen by the seed is 4096 tokens long and another one 4096 // 4. `block_pairs`: every pair number once. `routes`: two different experts a token; among the 1024 tokens of one ctx index no expert is named more than 160 times, a bound that some block reaches.
All inputs are finite; a program needn't handle non-finite values.
Results may differ from the reference program's by a relative error of at most 0.015.
Values may be sent and summed in bfloat16 or wider, within the bound.
No kernel may reach another device: no remote copies, remote signals or barrier semaphores. Data moves between devices by JAX's collectives and lax.ppermute only.
A program may use at most 448 MiB of HBM per device.

```python
import math
import jax
import jax.numpy as jnp
import numpy as np
from jax import lax

D = 768
HEADS = 12
HEAD_DIM = 64
EXPERT_FF = 2048
DENSE_FF = 2048
EXPERTS = 16
BLOCK = 128
SEQS = 4
PAIR = 256
SLOT = 4096
TOK_DEV = 1024
CAPACITY = 160
N_CTX = 16


def draw_lengths(key, part):
    key = jax.random.fold_in(key, 11)
    first_key, second_key = jax.random.split(key)
    drawn = jax.random.randint(first_key, (SEQS,), SLOT // 4, SLOT + 1)
    order = jax.random.permutation(second_key, SEQS)
    indices = jnp.arange(SEQS)
    drawn = jnp.where(indices == order[0], SLOT, drawn)
    drawn = jnp.where(indices == order[1], SLOT // 4, drawn)
    return drawn.astype(jnp.int32)


def block_levels(rng, shape, cuts, smallest, largest):
    def one(axis_at, shards_of):
        steps = jax.random.uniform(jax.random.fold_in(jax.random.fold_in(rng, 6), axis_at), (shards_of,), jnp.float32, smallest / len(cuts), largest / len(cuts))
        return jnp.repeat(jnp.exp(steps), shape[axis_at] // shards_of).reshape((-1,) + (1,) * (len(shape) - axis_at - 1))

    level = one(*cuts[0])
    for cut in cuts[1:]:
        level = level * one(*cut)
    return level


def deal_out(stream_key, own, number, rows, count, top, bound, slope):
    ranking = jax.random.permutation(stream_key, count)
    packed, common = shares(count, rows * top, bound, slope, True), shares(count, rows * top, bound, slope, False)
    places = jnp.arange(count)

    def named(sizes, rotation):
        used = int((sizes > 0).sum())
        fixed = max(1, used // 4)
        shifted = fixed + (places - fixed + rotation * (used - fixed)) % max(1, count - fixed)
        return jnp.zeros((count,), jnp.int32).at[ranking[jnp.where(places < fixed, places, shifted)]].set(jnp.asarray(sizes, jnp.int32))

    sizes = jnp.where(number % 4 == 0, named(packed, number // 4), named(common, number - number // 4 - 1))
    mixed = jax.random.permutation(jax.random.fold_in(own, 3), count)
    source_of, sink = mixed[0:count // 2 * 2:2], mixed[1:count // 2 * 2:2]
    margin = jnp.minimum(sizes[source_of] - 1, bound - sizes[sink]) // 2
    margin = jnp.where((source_of == ranking[0]) | (sink == ranking[0]) | (sizes[sink] == 0), 0, jnp.maximum(margin, 0))
    shifted = jax.random.randint(jax.random.fold_in(own, 4), (count // 2,), 0, 1 << 20) % (margin + 1)
    sizes = sizes.at[source_of].add(-shifted).at[sink].add(shifted)
    items = jnp.searchsorted(jnp.cumsum(sizes), jnp.arange(rows * top), side="right").astype(jnp.int32)
    table = items.reshape(top, rows).T
    table = table[jax.random.permutation(jax.random.fold_in(own, 1), rows)]
    rotation = jax.random.randint(jax.random.fold_in(own, 2), (rows, 1), 0, top)
    return jnp.take_along_axis(table, (jnp.arange(top)[None, :] + rotation) % top, axis=1)


def shares(number_of, total, reach, lean, full):
    loads = [(1 << 20) // math.isqrt(grade ** lean) + 1 for grade in range(1, number_of + 1)]
    largest = reach if full else min(reach, max(-(-total // number_of), total * loads[0] // sum(loads)))
    least = 1 if total - largest >= number_of - 1 else 0
    counts, rest = [largest] + [least] * (number_of - 1), total - largest - least * (number_of - 1)
    while rest > 0:
        candidates = [i for i in range(1, number_of) if counts[i] < largest] or [i for i in range(1, number_of) if counts[i] < reach]
        mass, left = sum([loads[i] for i in candidates]), rest
        for i in candidates:
            addition = min(reach - counts[i], max(1, left * loads[i] // mass), rest)
            counts[i] = counts[i] + addition
            rest = rest - addition
    return np.array(counts)


def centred(rng, extent, deviation, reach, cuts=(), held_as=jnp.bfloat16):
    array = deviation * jax.random.normal(rng, extent, jnp.float32)
    if cuts:
        array = array * block_levels(rng, extent, cuts, -0.22, 0.18)
    return jnp.clip(array, -reach, reach).astype(held_as)


def setup_inputs(seed: int = 0) -> dict:
    seeds = jax.random.split(jax.random.key(seed), 19)
    inputs = centred(seeds[0], (N_CTX, PAIR, SEQS, D), 1.0, 6.0, ((0, 16),))
    cotangent = centred(seeds[1], (N_CTX, PAIR, SEQS, D), 1.0, 6.0, ((0, 16),))
    lengths = draw_lengths(jax.random.fold_in(seeds[18], 71), 0)
    block_pairs = jax.random.permutation(seeds[3], N_CTX).astype(jnp.int32)
    routes_keys = jax.random.split(jax.random.fold_in(seeds[4], 1), N_CTX * PAIR * SEQS // TOK_DEV)
    routes_turns = jax.random.permutation(jax.random.fold_in(seeds[4], 3), N_CTX * PAIR * SEQS // TOK_DEV)
    routes = jax.vmap(lambda own, number: deal_out(jax.random.fold_in(seeds[4], 2), own, number, TOK_DEV, EXPERTS, 2, CAPACITY, 1))(routes_keys, routes_turns).reshape((N_CTX, PAIR, SEQS, 2))
    attn_gain = jnp.clip(1.0 + 0.15 * jax.random.normal(seeds[5], (D,), jnp.float32), 0.25, 1.75)
    query_weight = centred(seeds[6], (D, HEADS * HEAD_DIM), D ** -0.5, 0.21875, ((1, 2),))
    key_weight = centred(seeds[7], (D, HEADS * HEAD_DIM), D ** -0.5, 0.21875, ((1, 2),))
    value_weight = centred(seeds[8], (D, HEADS * HEAD_DIM), D ** -0.5, 0.21875, ((1, 2),))
    out_weight = centred(seeds[9], (HEADS * HEAD_DIM, D), (HEADS * HEAD_DIM // 64) ** -0.5, 1.75, ((0, 2),))
    ffn_gain = jnp.clip(1.0 + 0.15 * jax.random.normal(seeds[10], (D,), jnp.float32), 0.25, 1.75)
    router_weight = centred(seeds[11], (D, EXPERTS), (2 * D) ** -0.5, 0.15625)
    expert_gate = centred(seeds[12], (EXPERTS, D, EXPERT_FF), D ** -0.5, 0.21875, ((2, 2),))
    expert_up = centred(seeds[13], (EXPERTS, D, EXPERT_FF), D ** -0.5, 0.21875, ((2, 2),))
    expert_down = centred(seeds[14], (EXPERTS, EXPERT_FF, D), EXPERT_FF ** -0.5, 0.125, ((1, 2),))
    dense_gate = centred(seeds[15], (D, DENSE_FF), D ** -0.5, 0.21875, ((1, 2),))
    dense_up = centred(seeds[16], (D, DENSE_FF), D ** -0.5, 0.21875, ((1, 2),))
    dense_down = centred(seeds[17], (DENSE_FF, D), DENSE_FF ** -0.5, 0.125, ((0, 2),))
    return dict(inputs=inputs, cotangent=cotangent, lengths=lengths, block_pairs=block_pairs, routes=routes, attn_gain=attn_gain, query_weight=query_weight, key_weight=key_weight, value_weight=value_weight, out_weight=out_weight, ffn_gain=ffn_gain, router_weight=router_weight, expert_gate=expert_gate, expert_up=expert_up, expert_down=expert_down, dense_gate=dense_gate, dense_up=dense_up, dense_down=dense_down)


EPS = 1e-06
THETA = 10000.0
HIGH = lax.Precision.HIGHEST

@jax.custom_vjp
def low(v):
    return lax.optimization_barrier(v.astype(jnp.bfloat16)).astype(jnp.float32)

@jax.custom_vjp
def low_back(v):
    return v

def low_keep(v):
    return (low(v), None)

def low_pass(kept, grad):
    return (grad,)

def back_keep(v):
    return (v, None)

def back_low(kept, grad):
    return (low(grad),)
low.defvjp(low_keep, low_pass)
low_back.defvjp(back_keep, back_low)

def mult(left, right):
    return jnp.dot(left, right, precision=HIGH)

def normalize(values, gain):
    return values * lax.rsqrt(lax.optimization_barrier(jnp.mean(values * values, axis=-1, keepdims=True)) + EPS) * gain

def place_table(block_pairs):
    within = jnp.arange(PAIR, dtype=jnp.int32)
    which = jnp.where(within[None, :] < BLOCK, block_pairs[:, None], 2 * N_CTX - 1 - block_pairs[:, None])
    return (which * BLOCK + within[None, :] % BLOCK).reshape(-1)

def rotary(values, places):
    half = values.shape[-1] // 2
    freqs = THETA ** (-jnp.arange(half, dtype=jnp.float32) / half)
    angles = places.astype(jnp.float32)[:, None] * freqs[None, :]
    extra = tuple(range(1, values.ndim - 1))
    cosine = jnp.expand_dims(jnp.concatenate([jnp.cos(angles), jnp.cos(angles)], axis=-1), extra)
    sine = jnp.expand_dims(jnp.concatenate([jnp.sin(angles), jnp.sin(angles)], axis=-1), extra)
    turned = jnp.concatenate([-values[..., half:], values[..., :half]], axis=-1)
    return values * cosine + turned * sine

def attend_block(queries, query_places, keys, values, key_places, length):
    scores = jnp.einsum('qhd,khd->hqk', queries, keys, precision=HIGH) * HEAD_DIM ** (-0.5)
    scores = low_back(scores)
    allowed = (key_places[None, :] <= query_places[:, None]) & (key_places[None, :] < length)
    scores = jnp.where(allowed[None], scores, -1e+30)
    top = lax.optimization_barrier(jnp.max(scores, axis=-1, keepdims=True))
    weights = jnp.exp(scores - top)
    weights = weights / lax.optimization_barrier(jnp.sum(weights, axis=-1, keepdims=True))
    return jnp.einsum('hqk,khd->qhd', low(weights), values, precision=HIGH)

def attend_slot(queries, keys, values, length, places):
    query_block = min(512, SLOT)
    blocks = SLOT // query_block
    stepper = jax.checkpoint(attend_block)

    def single(item):
        return stepper(item[0], item[1], keys, values, places, length)
    results = lax.map(single, (queries.reshape(blocks, query_block, HEADS, HEAD_DIM), places.reshape(blocks, query_block)))
    return results.reshape(SLOT, HEADS, HEAD_DIM)

def expert_block(normed, chosen, gates, expert_gate, expert_up, expert_down):
    flat = chosen.reshape(-1)
    marks = (flat[:, None] == jnp.arange(EXPERTS, dtype=jnp.int32)[None, :]).astype(jnp.int32)
    order = lax.optimization_barrier(jnp.sum((jnp.cumsum(marks, axis=0, dtype=jnp.int32) - 1) * marks, axis=1, dtype=jnp.int32))
    target = (flat * CAPACITY + order).reshape(-1, 2)
    slots = jnp.arange(EXPERTS * CAPACITY, dtype=jnp.int32)[:, None]
    spread = ((slots == target[None, :, 0]) | (slots == target[None, :, 1])).astype(jnp.float32)
    routed = mult(spread, normed).reshape(EXPERTS, CAPACITY, D)
    gate_part = low_back(jnp.einsum('ecd,edf->ecf', routed, expert_gate, precision=HIGH))
    up_part = low_back(jnp.einsum('ecd,edf->ecf', routed, expert_up, precision=HIGH))
    hidden = low(jax.nn.silu(gate_part) * up_part)
    produced = low_back(jnp.einsum('ecf,efd->ecd', hidden, expert_down, precision=HIGH)).reshape(-1, D)
    picked = produced[target.reshape(-1)].reshape(-1, 2, D)
    return lax.optimization_barrier(jnp.sum(picked * gates[:, :, None], axis=1))

def forward(inputs, attn_gain, query_weight, key_weight, value_weight, out_weight, ffn_gain, router_weight, expert_gate, expert_up, expert_down, dense_gate, dense_up, dense_down, lengths, block_pairs, routes):
    places = place_table(block_pairs)
    tokens = inputs.reshape(-1, D)
    first = low(normalize(tokens, attn_gain))
    head_shape = (SLOT, SEQS, HEADS, HEAD_DIM)
    queries = low(rotary(low_back(mult(first, query_weight)).reshape(head_shape), places))
    keys = low(rotary(low_back(mult(first, key_weight)).reshape(head_shape), places))
    values = low(low_back(mult(first, value_weight))).reshape(head_shape)

    def one_slot(item):
        return attend_slot(item[0], item[1], item[2], item[3], places)
    mixed = lax.map(one_slot, (jnp.moveaxis(queries, 1, 0), jnp.moveaxis(keys, 1, 0), jnp.moveaxis(values, 1, 0), lengths))
    mixed = jnp.moveaxis(mixed, 0, 1).reshape(-1, HEADS * HEAD_DIM)
    mixed = low(low_back(mixed))
    state = tokens + low_back(mult(mixed, out_weight))
    second = low(normalize(state, ffn_gain))
    logits = low_back(mult(second, router_weight))
    chosen = routes.reshape(-1, 2)
    selected = jnp.take_along_axis(logits, chosen, axis=1)
    weights = jnp.exp(selected - lax.optimization_barrier(jnp.max(selected, axis=-1, keepdims=True)))
    gates = weights / lax.optimization_barrier(jnp.sum(weights, axis=-1, keepdims=True))
    expert_step = jax.checkpoint(expert_block)

    def one_device(item):
        return expert_step(item[0], item[1], item[2], expert_gate, expert_up, expert_down)
    mixture = lax.map(one_device, (second.reshape(N_CTX, TOK_DEV, D), chosen.reshape(N_CTX, TOK_DEV, 2), gates.reshape(N_CTX, TOK_DEV, 2))).reshape(-1, D)
    dense_hidden = low(jax.nn.silu(low_back(mult(second, dense_gate))) * low_back(mult(second, dense_up)))
    dense_out = mult(dense_hidden, dense_down)
    return (state + mixture + dense_out).reshape(inputs.shape)

def reference(inputs, cotangent, lengths, block_pairs, routes, attn_gain, query_weight, key_weight, value_weight, out_weight, ffn_gain, router_weight, expert_gate, expert_up, expert_down, dense_gate, dense_up, dense_down):
    floats = tuple((item.astype(jnp.float32) for item in (inputs, attn_gain, query_weight, key_weight, value_weight, out_weight, ffn_gain, router_weight, expert_gate, expert_up, expert_down, dense_gate, dense_up, dense_down)))

    def closed(*weights):
        return forward(*weights, lengths, block_pairs, routes)
    output, pull = jax.vjp(closed, *floats)
    places = place_table(block_pairs).reshape(N_CTX, PAIR)
    valid = (places[:, :, None] < lengths[None, None, :]).astype(jnp.float32)
    grads = pull(cotangent.astype(jnp.float32) * valid[..., None])
    return (output.astype(jnp.bfloat16), grads[0].astype(jnp.bfloat16), grads[1], grads[2], grads[3], grads[4], grads[5], grads[6], grads[7], grads[8], grads[9], grads[10], grads[11], grads[12], grads[13])
```

```python
import functools

import jax
import jax.numpy as jnp
from jax import lax
from jax.experimental import pallas as pl
from jax.experimental.pallas import tpu as pltpu
from jax.sharding import PartitionSpec as P

HEAD_DIM = 64
CAPACITY = 160
EPS = 1e-06
THETA = 10000.0
LANES = 128
BF = jnp.bfloat16
F4 = jnp.float32
TQ = 256
TK = 512
VMEM_LIMIT = 56 * 1024 * 1024


def dot(a, b):
    return jnp.dot(a, b, preferred_element_type=F4)


def dot_nt(a, b):
    return lax.dot_general(a, b, (((1,), (1,)), ((), ())), preferred_element_type=F4)


def dot_tn(a, b):
    return lax.dot_general(a, b, (((0,), (0,)), ((), ())), preferred_element_type=F4)


def wt_gather(x):
    size = lax.axis_size("wt")
    return [x] + [
        lax.ppermute(x, "wt", [(i, (i - k) % size) for i in range(size)]) for k in range(1, size)
    ]


def wt_scatter(pieces):
    size = lax.axis_size("wt")
    total = pieces[0]
    for k in range(1, size):
        moved = lax.ppermute(pieces[k], "wt", [(i, (i + k) % size) for i in range(size)])
        total = total + moved.astype(total.dtype)
    return total


def wt_sum(x):
    if lax.axis_size("wt") == 2:
        return x + lax.ppermute(x, "wt", [(0, 1), (1, 0)])
    return lax.psum(x, "wt")


def in_order(parts):
    size = len(parts)
    start = (size - lax.axis_index("wt")) % size
    return lax.dynamic_slice_in_dim(jnp.stack(parts + parts[:-1]), start, size, 0)


def lane_of(shape):
    return lax.broadcasted_iota(jnp.int32, shape, len(shape) - 1)


def pair_swap(a, b):
    low = lane_of(a.shape) < HEAD_DIM
    return (
        jnp.where(low, a, pltpu.roll(b, HEAD_DIM, 1)),
        jnp.where(low, pltpu.roll(a, HEAD_DIM, 1), b),
    )


def turn_halves(t):
    first = lane_of(t.shape) % HEAD_DIM < HEAD_DIM // 2
    return jnp.where(
        first,
        pltpu.roll(t, LANES - HEAD_DIM // 2, 1),
        pltpu.roll(t, HEAD_DIM // 2, 1),
    )


def params(count):
    return pltpu.CompilerParams(
        vmem_limit_bytes=VMEM_LIMIT, dimension_semantics=("arbitrary",) * count
    )


def whole(shape):
    return pl.BlockSpec(shape, lambda *i: (0,) * len(shape))


def project_kernel(members, heads, units, x_ref, gain_ref, w_ref, cos_ref, sin_ref, msg_ref, a1_ref):
    s = pl.program_id(0)
    rows = x_ref.shape[1]
    chunk = rows // 2
    width = heads * HEAD_DIM
    x = x_ref[0].astype(F4)
    scale = lax.rsqrt(jnp.mean(x * x, axis=-1, keepdims=True) + EPS)
    a1 = (x * scale * gain_ref[...]).astype(BF)
    a1_ref[0] = a1
    cosine, sine = cos_ref[...], sin_ref[...]
    query = dot(a1, w_ref[:, :width])
    key = dot(a1, w_ref[:, width : 2 * width])
    value = dot(a1, w_ref[:, 2 * width :])
    if units * members > (heads * pl.num_programs(0)):

        @pl.when(s == 0)
        def _():
            msg_ref[...] = jnp.zeros_like(msg_ref)

    def rope(t):
        return t * cosine + turn_halves(t) * sine

    for g in range(heads // 2):
        part = slice(g * LANES, (g + 1) * LANES)
        pairs = pair_swap(rope(key[:, part]), value[:, part])
        turned = rope(query[:, part])
        asked = pair_swap(turned[:chunk], turned[chunk:])
        for c in range(2):
            unit = s * heads + 2 * g + c
            chip, u = unit % members, unit // members
            msg_ref[chip, 3 * u] = pairs[c][:chunk].astype(BF)
            msg_ref[chip, 3 * u + 1] = pairs[c][chunk:].astype(BF)
            msg_ref[chip, 3 * u + 2] = asked[c].astype(BF)


def project(x, gain, weights, cosine, sine, members, units):
    seqs, rows, width = x.shape
    heads = weights.shape[1] // 3 // HEAD_DIM
    msg = (members, 3 * units, rows // 2, LANES)
    return pl.pallas_call(
        functools.partial(project_kernel, members, heads, units),
        grid=(seqs,),
        in_specs=[
            pl.BlockSpec((1, rows, width), lambda s: (s, 0, 0)),
            whole((1, width)),
            whole(weights.shape),
            whole(cosine.shape),
            whole(sine.shape),
        ],
        out_specs=[whole(msg), pl.BlockSpec((1, rows, width), lambda s: (s, 0, 0))],
        out_shape=[
            jax.ShapeDtypeStruct(msg, BF),
            jax.ShapeDtypeStruct((seqs, rows, width), BF),
        ],
        compiler_params=params(1),
        name="project",
    )(x, gain, weights, cosine, sine)


def gather_keys(inv_ref, w, kv_refs, kv_s, members, chunk):
    size = len(kv_refs)
    for block in range(2 * members):
        half = 0 if block < members else 1
        chip = inv_ref[block if half == 0 else 2 * members - 1 - block]
        for k, ref in enumerate(kv_refs):
            core = lax.rem(w + k, size)
            start = pl.multiple_of(block * size * chunk + core * chunk, chunk)
            kv_s[pl.ds(start, chunk), :] = ref[chip, half]


def gather_rows(inv_ref, read, put, members, to_high):
    for block in range(2 * members):
        half = 0 if block < members else 1
        chip = inv_ref[block if half == 0 else 2 * members - 1 - block]
        rows = read(chip).astype(F4)
        if (half == 1) != to_high:
            rows = pltpu.roll(rows, HEAD_DIM, 1)
        low = lane_of(rows.shape) < HEAD_DIM
        rows = jnp.where(low, 0.0, rows) if to_high else jnp.where(low, rows, 0.0)
        put(block, rows)


def attend_kernel(members, size, inv_ref, len_ref, w_ref, *refs):
    kv_refs = refs[:size]
    o_ref, of_ref, lse_ref = refs[size : size + 3]
    kv_s, vt_s, q_s, o_s = refs[size + 3 :]
    u = pl.program_id(0)
    chunk = kv_refs[0].shape[2]
    own_rows = q_s.shape[0]
    slot = kv_s.shape[0]
    w = w_ref[0]
    length = len_ref[u]
    gather_keys(inv_ref, w, kv_refs, kv_s, members, chunk)

    def put(block, rows):
        q_s[block * chunk : (block + 1) * chunk, :] = rows * HEAD_DIM ** (-0.5)

    gather_rows(inv_ref, lambda chip: kv_refs[0][chip, 2], put, members, False)

    def flip(i, carry):
        tile = kv_s[pl.ds(pl.multiple_of(i * TK, TK), TK), :].astype(F4)
        vt_s[i] = tile.T[HEAD_DIM:].astype(BF)
        return carry

    lax.fori_loop(0, slot // TK, flip, 0)
    span = TQ * size

    def row_tile(t, carry):
        row = pl.multiple_of(t * TQ, TQ)
        qt = q_s[pl.ds(row, TQ), :].T.astype(BF)
        index = lax.broadcasted_iota(jnp.int32, (1, TQ), 1)
        place = t * span + (index // chunk) * (size * chunk) + w * chunk + index % chunk
        limit = jnp.minimum(place, length - 1)

        def step(masked, kt, state):
            top, total, acc = state
            start = pl.multiple_of(kt * TK, TK)
            scores = dot(kv_s[pl.ds(start, TK), :], qt)
            if masked:
                keys = kt * TK + lax.broadcasted_iota(jnp.int32, (TK, 1), 0)
                scores = jnp.where(keys <= limit, scores, -1e30)
            new_top = jnp.maximum(top, jnp.max(scores, axis=0, keepdims=True))
            weights = jnp.exp(scores - new_top)
            fade = jnp.exp(top - new_top)
            total = total * fade + jnp.sum(weights, axis=0, keepdims=True)
            acc = acc * fade + dot(vt_s[kt], weights.astype(BF))
            return new_top, total, acc

        clear = jnp.minimum(t * span, length) // TK
        last = jnp.minimum(pl.cdiv((t + 1) * span, TK), pl.cdiv(length, TK))
        state = (
            jnp.full((1, TQ), -1e30, F4),
            jnp.zeros((1, TQ), F4),
            jnp.zeros((HEAD_DIM, TQ), F4),
        )
        state = lax.fori_loop(0, clear, functools.partial(step, False), state)
        top, total, acc = lax.fori_loop(clear, last, functools.partial(step, True), state)
        result = acc / total
        of_ref[0, t] = result
        lse_ref[0, t] = top + jnp.log(total)
        blank = jnp.zeros_like(result)
        first = 2 * t * TQ < own_rows
        both = jnp.concatenate(
            [jnp.where(first, result, blank), jnp.where(first, blank, result)], axis=0
        )
        o_s[pl.ds(row, TQ), :] = both.T
        return carry

    lax.fori_loop(0, own_rows // TQ, row_tile, 0)
    for b in range(members):
        other = 2 * members - 1 - b
        rows = (
            o_s[b * chunk : (b + 1) * chunk, :] + o_s[other * chunk : (other + 1) * chunk, :]
        )
        o_ref[inv_ref[b], 0] = rows.astype(BF)


def attend(inv, lengths, w, blocks, units):
    members, _, chunk, _ = blocks[0].shape
    size = len(blocks)
    slot = 2 * members * chunk * size
    rows = 2 * members * chunk
    spec = pl.BlockSpec((members, 3, chunk, LANES), lambda u, *_: (0, u, 0, 0))
    return pl.pallas_call(
        functools.partial(attend_kernel, members, size),
        grid_spec=pltpu.PrefetchScalarGridSpec(
            num_scalar_prefetch=3,
            grid=(units,),
            in_specs=[spec] * size,
            out_specs=[
                pl.BlockSpec((members, 1, chunk, LANES), lambda u, *_: (0, u, 0, 0)),
                pl.BlockSpec((1, rows // TQ, HEAD_DIM, TQ), lambda u, *_: (u, 0, 0, 0)),
                pl.BlockSpec((1, rows // TQ, 1, TQ), lambda u, *_: (u, 0, 0, 0)),
            ],
            scratch_shapes=[
                pltpu.VMEM((slot, LANES), BF),
                pltpu.VMEM((slot // TK, HEAD_DIM, TK), BF),
                pltpu.VMEM((rows, LANES), F4),
                pltpu.VMEM((rows, LANES), F4),
            ],
        ),
        out_shape=[
            jax.ShapeDtypeStruct((members, units, chunk, LANES), BF),
            jax.ShapeDtypeStruct((units, rows // TQ, HEAD_DIM, TQ), F4),
            jax.ShapeDtypeStruct((units, rows // TQ, 1, TQ), F4),
        ],
        compiler_params=params(1),
        name="attend",
    )(inv, lengths, w, *blocks)


def attend_back_kernel(members, size, inv_ref, len_ref, w_ref, *refs):
    kv_refs = refs[:size]
    do_ref, of_ref, lse_ref = refs[size : size + 3]
    dq_ref = refs[size + 3]
    dkv_refs = refs[size + 4 : 2 * size + 4]
    kv_s, kt_s, q_s, do_s, dq_s, dkv_s = refs[2 * size + 4 :]
    u = pl.program_id(0)
    chunk = kv_refs[0].shape[2]
    own_rows = q_s.shape[0]
    slot = kv_s.shape[0]
    w = w_ref[0]
    length = len_ref[u]
    gather_keys(inv_ref, w, kv_refs, kv_s, members, chunk)

    def put_q(block, rows):
        q_s[block * chunk : (block + 1) * chunk, :] = rows * HEAD_DIM ** (-0.5)

    def put_do(block, rows):
        do_s[block * chunk : (block + 1) * chunk, :] = rows

    gather_rows(inv_ref, lambda chip: kv_refs[0][chip, 2], put_q, members, False)
    gather_rows(inv_ref, lambda chip: do_ref[chip, 0], put_do, members, True)

    def flip(i, carry):
        tile = kv_s[pl.ds(pl.multiple_of(i * TK, TK), TK), :].astype(F4)
        kt_s[i] = tile.T[:HEAD_DIM].astype(BF)
        return carry

    lax.fori_loop(0, slot // TK, flip, 0)
    dkv_s[...] = jnp.zeros_like(dkv_s)
    dq_s[...] = jnp.zeros_like(dq_s)
    span = TQ * size

    def row_tile(t, carry):
        row = pl.multiple_of(t * TQ, TQ)
        q_rows = q_s[pl.ds(row, TQ), :]
        do_rows = do_s[pl.ds(row, TQ), :]
        qt, dot_ = q_rows.T, do_rows.T
        delta = jnp.sum(dot_[HEAD_DIM:] * of_ref[0, t], axis=0, keepdims=True)
        qt, dot_ = qt.astype(BF), dot_.astype(BF)
        stacked = jnp.concatenate([do_rows.astype(BF), q_rows.astype(BF)], axis=0)
        lse = lse_ref[0, t]
        index = lax.broadcasted_iota(jnp.int32, (1, TQ), 1)
        place = t * span + (index // chunk) * (size * chunk) + w * chunk + index % chunk
        limit = jnp.minimum(place, length - 1)

        def step(masked, kt, dqt):
            start = pl.multiple_of(kt * TK, TK)
            kv = kv_s[pl.ds(start, TK), :]
            weights = jnp.exp(dot(kv, qt) - lse)
            if masked:
                keys = kt * TK + lax.broadcasted_iota(jnp.int32, (TK, 1), 0)
                weights = jnp.where(keys <= limit, weights, 0.0)
            pulled = dot(kv, dot_)
            back = (weights * (pulled - delta)).astype(BF)
            dkv_s[pl.ds(start, TK), :] += dot(
                jnp.concatenate([weights.astype(BF), back], axis=1), stacked
            )
            return dqt + dot(kt_s[kt], back)

        clear = jnp.minimum(t * span, length) // TK
        last = jnp.minimum(pl.cdiv((t + 1) * span, TK), pl.cdiv(length, TK))
        dqt = jnp.zeros((HEAD_DIM, TQ), F4)
        dqt = lax.fori_loop(0, clear, functools.partial(step, False), dqt)
        dqt = lax.fori_loop(clear, last, functools.partial(step, True), dqt)
        dqt = dqt * HEAD_DIM ** (-0.5)
        blank = jnp.zeros_like(dqt)
        first = 2 * t * TQ < own_rows
        both = jnp.concatenate(
            [jnp.where(first, dqt, blank), jnp.where(first, blank, dqt)], axis=0
        )
        dq_s[pl.ds(row, TQ), :] = both.T
        return carry

    lax.fori_loop(0, jnp.minimum(pl.cdiv(length, span), own_rows // TQ), row_tile, 0)
    for b in range(members):
        other = 2 * members - 1 - b
        chip = inv_ref[b]
        rows = (
            dq_s[b * chunk : (b + 1) * chunk, :] + dq_s[other * chunk : (other + 1) * chunk, :]
        )
        dq_ref[chip, 0] = rows.astype(BF)
        for half, block in ((0, b), (1, other)):
            for k, ref in enumerate(dkv_refs):
                core = lax.rem(w + k, size)
                start = pl.multiple_of(block * size * chunk + core * chunk, chunk)
                ref[chip, half] = dkv_s[pl.ds(start, chunk), :]


def attend_back(inv, lengths, w, blocks, do_msg, kept, lse, units):
    members, _, chunk, _ = blocks[0].shape
    size = len(blocks)
    slot = 2 * members * chunk * size
    rows = 2 * members * chunk
    spec = pl.BlockSpec((members, 3, chunk, LANES), lambda u, *_: (0, u, 0, 0))
    one = pl.BlockSpec((members, 1, chunk, LANES), lambda u, *_: (0, u, 0, 0))
    two = pl.BlockSpec((members, 2, chunk, LANES), lambda u, *_: (0, u, 0, 0))
    return pl.pallas_call(
        functools.partial(attend_back_kernel, members, size),
        grid_spec=pltpu.PrefetchScalarGridSpec(
            num_scalar_prefetch=3,
            grid=(units,),
            in_specs=[spec] * size
            + [
                one,
                pl.BlockSpec((1, rows // TQ, HEAD_DIM, TQ), lambda u, *_: (u, 0, 0, 0)),
                pl.BlockSpec((1, rows // TQ, 1, TQ), lambda u, *_: (u, 0, 0, 0)),
            ],
            out_specs=[one] + [two] * size,
            scratch_shapes=[
                pltpu.VMEM((slot, LANES), BF),
                pltpu.VMEM((slot // TK, HEAD_DIM, TK), BF),
                pltpu.VMEM((rows, LANES), F4),
                pltpu.VMEM((rows, LANES), F4),
                pltpu.VMEM((rows, LANES), F4),
                pltpu.VMEM((slot, LANES), F4),
            ],
        ),
        out_shape=[jax.ShapeDtypeStruct((members, units, chunk, LANES), BF)]
        + [jax.ShapeDtypeStruct((members, 2 * units, chunk, LANES), F4)] * size,
        compiler_params=params(1),
        name="attend_back",
    )(inv, lengths, w, *blocks, do_msg, kept, lse)


def mix_kernel(members, heads, o_ref, x_ref, w_ref, gain_ref, mixed_ref, state_ref, a2_ref):
    s = pl.program_id(0)
    chunk = o_ref.shape[2]
    for g in range(heads // 2):
        pair = []
        for c in range(2):
            unit = s * heads + 2 * g + c
            pair.append(o_ref[unit % members, unit // members].astype(F4))
        early, late = pair_swap(*pair)
        part = slice(g * LANES, (g + 1) * LANES)
        mixed_ref[0, :chunk, part] = early.astype(BF)
        mixed_ref[0, chunk:, part] = late.astype(BF)
    state = x_ref[0].astype(F4) + dot(mixed_ref[0], w_ref[...])
    state_ref[0] = state
    scale = lax.rsqrt(jnp.mean(state * state, axis=-1, keepdims=True) + EPS)
    a2_ref[0] = (state * scale * gain_ref[...]).astype(BF)


def mix(o_msg, x, out_weight, gain):
    members, units, chunk, _ = o_msg.shape
    seqs, rows, width = x.shape
    inner = out_weight.shape[0]
    per_slot = pl.BlockSpec((1, rows, width), lambda s: (s, 0, 0))
    return pl.pallas_call(
        functools.partial(mix_kernel, members, inner // HEAD_DIM),
        grid=(seqs,),
        in_specs=[whole(o_msg.shape), per_slot, whole(out_weight.shape), whole((1, width))],
        out_specs=[pl.BlockSpec((1, rows, inner), lambda s: (s, 0, 0)), per_slot, per_slot],
        out_shape=[
            jax.ShapeDtypeStruct((seqs, rows, inner), BF),
            jax.ShapeDtypeStruct((seqs, rows, width), F4),
            jax.ShapeDtypeStruct((seqs, rows, width), BF),
        ],
        compiler_params=params(1),
        name="mix",
    )(o_msg, x, out_weight, gain)


def norm_back(values, gain, upstream):
    scale = lax.rsqrt(jnp.mean(values * values, axis=-1, keepdims=True) + EPS)
    unit = values * scale
    pulled = upstream * gain
    result = scale * (pulled - unit * jnp.mean(pulled * unit, axis=-1, keepdims=True))
    return result, jnp.sum(upstream * unit, axis=0, keepdims=True)


def unmix_kernel(members, heads, state_ref, da2_ref, cot_ref, gain_ref, w_ref, *outs):
    dstate_ref, low_ref, msg_ref, dgain_ref = outs
    s = pl.program_id(0)
    rows = state_ref.shape[1]
    chunk = rows // 2
    pulled, dgain = norm_back(state_ref[0], gain_ref[...], da2_ref[0])
    dstate = cot_ref[0].astype(F4) + pulled
    dstate_ref[0] = dstate
    low = dstate.astype(BF)
    low_ref[0] = low

    @pl.when(s == 0)
    def _():
        dgain_ref[...] = jnp.zeros_like(dgain_ref)
        if msg_ref.shape[0] * msg_ref.shape[1] > heads * pl.num_programs(0):
            msg_ref[...] = jnp.zeros_like(msg_ref)

    dgain_ref[...] += dgain
    mixed_back = dot_nt(low, w_ref[...])
    for g in range(heads // 2):
        part = mixed_back[:, g * LANES : (g + 1) * LANES]
        pair = pair_swap(part[:chunk], part[chunk:])
        for c in range(2):
            unit = s * heads + 2 * g + c
            msg_ref[unit % members, unit // members] = pair[c].astype(BF)


def unmix(state, da2, cot, gain, out_weight, members, units):
    seqs, rows, width = state.shape
    inner = out_weight.shape[0]
    msg = (members, units, rows // 2, LANES)
    per_slot = pl.BlockSpec((1, rows, width), lambda s: (s, 0, 0))
    return pl.pallas_call(
        functools.partial(unmix_kernel, members, inner // HEAD_DIM),
        grid=(seqs,),
        in_specs=[per_slot, per_slot, per_slot, whole((1, width)), whole(out_weight.shape)],
        out_specs=[per_slot, per_slot, whole(msg), whole((1, width))],
        out_shape=[
            jax.ShapeDtypeStruct((seqs, rows, width), F4),
            jax.ShapeDtypeStruct((seqs, rows, width), BF),
            jax.ShapeDtypeStruct(msg, BF),
            jax.ShapeDtypeStruct((1, width), F4),
        ],
        compiler_params=params(1),
        name="unmix",
    )(state, da2, cot, gain, out_weight)


def unproject_kernel(
    members, heads, units, msg_ref, x_ref, dstate_ref, gain_ref, w_ref, cos_ref, sin_ref, *outs
):
    dqkv_ref, dx_ref, dgain_ref = outs
    s = pl.program_id(0)
    width = heads * HEAD_DIM
    cosine, sine = cos_ref[...], sin_ref[...]

    def rope_back(grad):
        return grad * cosine - turn_halves(grad) * sine

    for g in range(heads // 2):
        pair, early, late = [], [], []
        for c in range(2):
            unit = s * heads + 2 * g + c
            chip, u = unit % members, unit // members
            pair.append(
                jnp.concatenate([msg_ref[chip, 2 * u], msg_ref[chip, 2 * u + 1]], axis=0).astype(F4)
            )
            early.append(msg_ref[chip, 2 * units + u].astype(F4))
        key, value = pair_swap(*pair)
        query = jnp.concatenate(pair_swap(*early), axis=0)
        at = g * LANES
        dqkv_ref[0, :, at : at + LANES] = rope_back(query).astype(BF)
        dqkv_ref[0, :, width + at : width + at + LANES] = rope_back(key).astype(BF)
        dqkv_ref[0, :, 2 * width + at : 2 * width + at + LANES] = value.astype(BF)
    da1 = dot_nt(dqkv_ref[0], w_ref[...])
    pulled, dgain = norm_back(x_ref[0].astype(F4), gain_ref[...], da1)
    dx_ref[0] = (dstate_ref[0] + pulled).astype(BF)

    @pl.when(s == 0)
    def _():
        dgain_ref[...] = jnp.zeros_like(dgain_ref)

    dgain_ref[...] += dgain


def unproject(msg, x, dstate, gain, weights, cosine, sine):
    members, triple, chunk, _ = msg.shape
    seqs, rows, width = x.shape
    inner = weights.shape[1]
    per_slot = pl.BlockSpec((1, rows, width), lambda s: (s, 0, 0))
    return pl.pallas_call(
        functools.partial(unproject_kernel, members, inner // 3 // HEAD_DIM, triple // 3),
        grid=(seqs,),
        in_specs=[
            whole(msg.shape),
            per_slot,
            per_slot,
            whole((1, width)),
            whole(weights.shape),
            whole(cosine.shape),
            whole(sine.shape),
        ],
        out_specs=[
            pl.BlockSpec((1, rows, inner), lambda s: (s, 0, 0)),
            per_slot,
            whole((1, width)),
        ],
        out_shape=[
            jax.ShapeDtypeStruct((seqs, rows, inner), BF),
            jax.ShapeDtypeStruct((seqs, rows, width), BF),
            jax.ShapeDtypeStruct((1, width), F4),
        ],
        compiler_params=params(1),
        name="unproject",
    )(msg, x, dstate, gain, weights, cosine, sine)


def swiglu(gate_part, up_part):
    return jax.nn.silu(gate_part) * up_part


def swiglu_back(gate_part, up_part, hidden_back):
    unused, pull = jax.vjp(swiglu, gate_part, up_part)
    dgate, dup = pull(hidden_back)
    return dgate.astype(BF), dup.astype(BF)


def per_device(
    inputs,
    cotangent,
    lengths,
    block_pairs,
    routes,
    attn_gain,
    query_weight,
    key_weight,
    value_weight,
    out_weight,
    ffn_gain,
    router_weight,
    expert_gate,
    expert_up,
    expert_down,
    dense_gate,
    dense_up,
    dense_down,
):
    pair_rows, seqs, width = inputs.shape[1:]
    members, size = lax.axis_size("ctx"), lax.axis_size("wt")
    ctx, w = lax.axis_index("ctx"), lax.axis_index("wt")
    experts = expert_gate.shape[0]
    block = pair_rows // 2
    chunk = block // size
    rows = 2 * chunk * seqs
    inner = query_weight.shape[1] * size
    heads = inner // HEAD_DIM
    units = -(-(seqs * heads) // members)

    def rows_of(array, k):
        parted = array.reshape(2, size, chunk, seqs, -1)
        mine = lax.dynamic_index_in_dim(parted, (w + k) % size, 1, False)
        return mine.transpose(2, 0, 1, 3).reshape(seqs, 2 * chunk, -1)

    def places_of(k):
        pair = lax.dynamic_index_in_dim(block_pairs, ctx, 0, False)
        blocks = jnp.stack([pair, 2 * members - 1 - pair])
        core = (w + k) % size
        return (blocks[:, None] * block + core * chunk + jnp.arange(chunk)[None, :]).reshape(-1)

    x = rows_of(inputs[0], 0)
    half = HEAD_DIM // 2
    freqs = THETA ** (-jnp.arange(half, dtype=F4) / half)
    angles = places_of(0).astype(F4)[:, None] * freqs[None, :]
    cosine = jnp.tile(jnp.cos(angles), (1, LANES // half))
    sine = jnp.tile(
        jnp.concatenate([-jnp.sin(angles), jnp.sin(angles)], axis=1), (1, LANES // HEAD_DIM)
    )

    local = inner // size
    packed = jnp.concatenate([query_weight, key_weight, value_weight, out_weight.T], axis=1)
    packed = in_order(wt_gather(packed)).reshape(size, width, 4, local)
    packed = packed.transpose(1, 2, 0, 3).reshape(width, 4 * inner)
    qkv_weight = packed[:, : 3 * inner]
    out_full = packed[:, 3 * inner :].T

    msg, a1 = project(x, attn_gain[None], qkv_weight, cosine, sine, members, units)
    got = lax.all_to_all(msg, "ctx", 0, 0, tiled=True)
    blocks = wt_gather(got)
    inv = jnp.argsort(block_pairs).astype(jnp.int32)
    unit_slots = jnp.minimum((ctx + members * jnp.arange(units)) // heads, seqs - 1)
    unit_lengths = lengths[unit_slots]
    w_arg = w.astype(jnp.int32)[None]
    o_msg, kept, lse = attend(inv, unit_lengths, w_arg, blocks, units)
    o_got = lax.all_to_all(o_msg, "ctx", 0, 0, tiled=True)
    mixed, state, second_own = mix(o_got, x, out_full, ffn_gain[None])

    total_rows = rows * size
    second = jnp.concatenate(wt_gather(second_own.reshape(rows, width)))
    cots = []
    for k in range(size):
        valid = places_of(k)[None, :] < lengths[:, None]
        cots.append(
            jnp.where(valid[:, :, None], rows_of(cotangent[0], k), jnp.zeros((), BF)).reshape(
                rows, width
            )
        )
    cot = jnp.concatenate(cots)
    cot_float = cot.astype(F4)

    parted = routes[0].reshape(2, size, chunk, seqs, 2).transpose(1, 3, 0, 2, 4)
    chosen_all = parted.reshape(total_rows, 2)
    names = jnp.arange(experts, dtype=jnp.int32)
    picks_all = chosen_all[:, :, None] == names
    marks = jnp.any(picks_all, axis=1).astype(BF)
    index = jnp.arange(total_rows)
    before = dot((index[None, :] < index[:, None]).astype(BF), marks)
    order_all = jnp.sum(jnp.where(picks_all, before[:, None, :], 0.0), axis=-1).astype(jnp.int32)
    share = -(-CAPACITY // size)
    held = -(-share // 16) * 16
    inside = (order_all >= w * held) & (order_all < (w + 1) * held)
    target_all = jnp.where(inside, chosen_all * held + order_all - w * held, -1)

    def own_first(array):
        parts = array.reshape(size, rows, 2)
        parts = jnp.concatenate([parts, parts[:-1]]) if size > 1 else parts
        return lax.dynamic_slice_in_dim(parts, w, size, 0).reshape(total_rows, 2)

    chosen, target = own_first(chosen_all), own_first(target_all)
    picks = chosen[:, :, None] == names

    logits = dot(second, router_weight)
    selected = jnp.sum(jnp.where(picks, logits[:, None, :], 0.0), axis=-1)
    raised = jnp.exp(selected - jnp.max(selected, axis=-1, keepdims=True))
    gates = raised / jnp.sum(raised, axis=-1, keepdims=True)

    slot_ids = jnp.arange(experts * held, dtype=jnp.int32)
    hit_one = slot_ids[:, None] == target[None, :, 0]
    hit_two = slot_ids[:, None] == target[None, :, 1]
    spread = (hit_one | hit_two).astype(BF)
    slot_gate = jnp.sum(
        jnp.where(hit_one, gates[None, :, 0], 0.0) + jnp.where(hit_two, gates[None, :, 1], 0.0),
        axis=1,
    )
    routed = dot(spread, second).astype(BF)
    routed_cot = (dot(spread, cot) * slot_gate[:, None]).astype(BF)
    sent = jnp.concatenate([routed, routed_cot], axis=1).reshape(experts, held, 2 * width)
    groups = None
    if members != experts:
        groups = [[g * experts + e for e in range(experts)] for g in range(members // experts)]
    swap = functools.partial(
        lax.all_to_all,
        axis_name="ctx",
        split_axis=0,
        concat_axis=0,
        axis_index_groups=groups,
        tiled=True,
    )
    arrived = swap(sent).reshape(experts * held, 2 * width)
    xe, dye = arrived[:, :width], arrived[:, width:]

    expert = ctx % experts

    def whole_expert(weights):
        return wt_gather(lax.dynamic_index_in_dim(weights, expert, 0, False))

    gate_parts, up_parts, down_parts = (
        whole_expert(expert_gate),
        whole_expert(expert_up),
        whole_expert(expert_down),
    )
    ye, dxe = 0.0, 0.0
    expert_grads = []
    for k in range(size):
        ge, ue = dot(xe, gate_parts[k]), dot(xe, up_parts[k])
        he = swiglu(ge, ue).astype(BF)
        ye = ye + dot(he, down_parts[k])
        dhe = dot_nt(dye, down_parts[k])
        dge, due = swiglu_back(ge, ue, dhe)
        dxe = dxe + dot_nt(dge, gate_parts[k]) + dot_nt(due, up_parts[k])
        expert_grads.append((dge, due, he))
    returned = jnp.concatenate([ye.astype(BF), dxe.astype(BF)], axis=1)
    home = swap(returned.reshape(experts, held, 2 * width)).reshape(experts * held, 2 * width)

    gd, ud = dot(second, dense_gate), dot(second, dense_up)
    hd = swiglu(gd, ud).astype(BF)
    dense = dot(hd, dense_down)
    dgd, dud = swiglu_back(gd, ud, dot_nt(cot, dense_down))
    dense_back = dot_nt(dgd, dense_gate) + dot_nt(dud, dense_up)
    dense_grads = jnp.concatenate(
        [dot_tn(second, dgd), dot_tn(second, dud), dot_tn(cot, hd)], axis=1
    )
    dense_sum = lax.psum_scatter(dense_grads, "ctx", scatter_dimension=0, tiled=True)

    hits = target[:, :, None] == slot_ids
    picked = [dot(hits[:, c].astype(BF), home[:, :width]) for c in range(2)]
    moe = picked[0] * gates[:, :1] + picked[1] * gates[:, 1:]
    routed_back = dot(jnp.any(hits, axis=1).astype(BF), home[:, width:])
    gate_back = jnp.stack([jnp.sum(p * cot_float, axis=-1) for p in picked], axis=1)
    select_back = gates * (gate_back - jnp.sum(gates * gate_back, axis=-1, keepdims=True))
    logit_back = jnp.sum(jnp.where(picks, select_back[:, :, None], 0.0), axis=1)
    logit_high = logit_back.astype(BF)
    logit_low = (logit_back - logit_high.astype(F4)).astype(BF)
    logit_both = jnp.concatenate([logit_high, logit_low], axis=1)
    router_both = jnp.concatenate([router_weight, router_weight], axis=1)
    part_back = dense_back + routed_back + dot_nt(logit_both, router_both)
    router_grad = dot_tn(second, logit_both)
    router_grad = router_grad[:, :experts] + router_grad[:, experts:]
    both = jnp.stack([moe + dense, part_back], axis=1).reshape(size, rows, 2, width)
    both = wt_scatter([both[k] for k in range(size)])
    output = (state.reshape(rows, width) + both[:, 0]).astype(BF)
    da2 = both[:, 1].reshape(seqs, 2 * chunk, width)

    dstate, dstate_low, do_msg, ffn_grad = unmix(
        state, da2, cots[0].reshape(seqs, 2 * chunk, width), ffn_gain[None], out_full, members, units
    )
    do_got = lax.all_to_all(do_msg, "ctx", 0, 0, tiled=True)
    dq, *dkv = attend_back(inv, unit_lengths, w_arg, blocks, do_got, kept, lse, units)
    dkv = wt_scatter(dkv).astype(BF)
    grad_msg = jnp.concatenate([dkv, dq], axis=1)
    grad_got = lax.all_to_all(grad_msg, "ctx", 0, 0, tiled=True)
    dqkv, dx, attn_grad = unproject(grad_got, x, dstate, attn_gain[None], qkv_weight, cosine, sine)

    def split_wt(left, right, parts):
        cols = right.reshape(rows, parts, size, -1)
        pieces = []
        for k in range(size):
            mine = lax.dynamic_index_in_dim(cols, (w + k) % size, 2, False).reshape(rows, -1)
            made = dot_tn(left.reshape(rows, -1), mine)
            pieces.append(made if k == 0 else made.astype(BF))
        return wt_scatter(pieces)

    qkv_grad = split_wt(a1, dqkv, 3)
    out_grad = split_wt(dstate_low, mixed, 1)
    small = jnp.concatenate([attn_grad.T, ffn_grad.T, router_grad], axis=1)
    small = wt_sum(small)
    small_high = small.astype(BF)
    small_low = (small - small_high.astype(F4)).astype(BF)
    small = jnp.concatenate([small_high, small_low], axis=1)
    few = experts + 2
    small = jnp.pad(small, ((0, 0), (0, -(2 * few) % LANES)))
    mine_msg = jnp.concatenate([qkv_grad.astype(BF), out_grad.astype(BF), small], axis=1)
    mine_msg = mine_msg.reshape(members, width // members, -1)
    mine_got = lax.all_to_all(mine_msg, "ctx", 0, 0, tiled=True).astype(F4)
    mine_sum = jnp.sum(mine_got, axis=0)
    tail = mine_sum[:, 4 * local :]
    tail = tail[:, :few] + tail[:, few : 2 * few]

    expert_pieces = []
    for k in range(size):
        dge, due, he = expert_grads[k]
        made = jnp.stack([dot_tn(xe, dge), dot_tn(xe, due), dot_tn(dye, he)], axis=1)
        expert_pieces.append(made if k == 0 else made.astype(BF))
    expert_sum = wt_scatter(expert_pieces).astype(BF)
    hidden = expert_gate.shape[2]
    expert_msg = expert_sum.reshape(members, width // members, 3 * hidden)
    expert_got = lax.all_to_all(expert_msg, "ctx", 0, 0, tiled=True).astype(F4)
    expert_got = expert_got.reshape(members // experts, experts, width // members, 3, hidden)
    expert_got = jnp.sum(expert_got, axis=0)

    def to_tokens(own):
        array = in_order(wt_gather(own)).reshape(size, seqs, 2, chunk, width)
        return array.transpose(2, 0, 3, 1, 4).reshape(inputs.shape)

    dense_hidden = dense_gate.shape[1]
    return (
        to_tokens(output),
        to_tokens(dx),
        tail[:, 0],
        mine_sum[:, :local],
        mine_sum[:, local : 2 * local],
        mine_sum[:, 2 * local : 3 * local],
        mine_sum[:, 3 * local : 4 * local].T,
        tail[:, 1],
        tail[:, 2:],
        expert_got[:, :, 0],
        expert_got[:, :, 1],
        expert_got[:, :, 2].transpose(0, 2, 1),
        dense_sum[:, :dense_hidden],
        dense_sum[:, dense_hidden : 2 * dense_hidden],
        dense_sum[:, 2 * dense_hidden :].T,
    )


def solution(mesh):
    placed = (
        P("ctx", None, None, None),
        P("ctx", None, None, None),
        P(),
        P(),
        P("ctx", None, None, None),
        P(),
        P(None, "wt"),
        P(None, "wt"),
        P(None, "wt"),
        P("wt", None),
        P(),
        P(),
        P(None, None, "wt"),
        P(None, None, "wt"),
        P(None, "wt", None),
        P(None, "wt"),
        P(None, "wt"),
        P("wt", None),
    )
    return jax.shard_map(
        per_device,
        mesh=mesh,
        in_specs=placed,
        out_specs=(
            P("ctx", None, None, None),
            P("ctx", None, None, None),
            P("ctx"),
            P("ctx", "wt"),
            P("ctx", "wt"),
            P("ctx", "wt"),
            P("wt", "ctx"),
            P("ctx"),
            P("ctx", None),
            P(None, "ctx", "wt"),
            P(None, "ctx", "wt"),
            P(None, "wt", "ctx"),
            P("ctx", "wt"),
            P("ctx", "wt"),
            P("wt", "ctx"),
        ),
        check_vma=False,
    )
```

```python
import functools

import jax
import jax.numpy as jnp
from jax import lax
from jax.experimental import pallas as pl
from jax.experimental.pallas import tpu as pltpu
from jax.sharding import PartitionSpec as P

HEAD_DIM = 64
CAPACITY = 160
EPS = 1e-06
THETA = 10000.0
LANES = 128
BF = jnp.bfloat16
F4 = jnp.float32
TQ = 256
TK = 512
VMEM_LIMIT = 56 * 1024 * 1024


def dot(a, b):
    return jnp.dot(a, b, preferred_element_type=F4)


def dot_nt(a, b):
    return lax.dot_general(a, b, (((1,), (1,)), ((), ())), preferred_element_type=F4)


def dot_tn(a, b):
    return lax.dot_general(a, b, (((0,), (0,)), ((), ())), preferred_element_type=F4)


def wt_gather(x):
    size = lax.axis_size("wt")
    return [x] + [
        lax.ppermute(x, "wt", [(i, (i - k) % size) for i in range(size)]) for k in range(1, size)
    ]


def wt_scatter(pieces):
    size = lax.axis_size("wt")
    total = pieces[0]
    for k in range(1, size):
        moved = lax.ppermute(pieces[k], "wt", [(i, (i + k) % size) for i in range(size)])
        total = total + moved.astype(total.dtype)
    return total


def wt_sum(x):
    if lax.axis_size("wt") == 2:
        return x + lax.ppermute(x, "wt", [(0, 1), (1, 0)])
    return lax.psum(x, "wt")


def in_order(parts):
    size = len(parts)
    start = (size - lax.axis_index("wt")) % size
    return lax.dynamic_slice_in_dim(jnp.stack(parts + parts[:-1]), start, size, 0)


def lane_of(shape):
    return lax.broadcasted_iota(jnp.int32, shape, len(shape) - 1)


def pair_swap(a, b):
    low = lane_of(a.shape) < HEAD_DIM
    return (
        jnp.where(low, a, pltpu.roll(b, HEAD_DIM, 1)),
        jnp.where(low, pltpu.roll(a, HEAD_DIM, 1), b),
    )


def turn_halves(t):
    first = lane_of(t.shape) % HEAD_DIM < HEAD_DIM // 2
    return jnp.where(
        first,
        pltpu.roll(t, LANES - HEAD_DIM // 2, 1),
        pltpu.roll(t, HEAD_DIM // 2, 1),
    )


def params(count):
    return pltpu.CompilerParams(
        vmem_limit_bytes=VMEM_LIMIT, dimension_semantics=("arbitrary",) * count
    )


def whole(shape):
    return pl.BlockSpec(shape, lambda *i: (0,) * len(shape))


def head_units(seqs, heads, members, shift, s, rel):
    unit = s * heads + lax.rem(rel + shift, heads)
    return lax.rem(unit, members), lax.div(unit, members)


def project_kernel(heads, units, members, count, shift_ref, x_ref, gain_ref, cos_ref, sin_ref, *refs):
    w_refs = refs[: 3 * count]
    msg_ref, a1_ref = refs[3 * count :]
    seqs, rows, width = x_ref.shape
    chunk = rows // 2
    for s in range(seqs):
        x = x_ref[s].astype(F4)
        scale = lax.rsqrt(jnp.mean(x * x, axis=-1, keepdims=True) + EPS)
        a1_ref[s] = (x * scale * gain_ref[...]).astype(BF)
    if units * members > heads * seqs:
        msg_ref[...] = jnp.zeros_like(msg_ref)
    a1 = a1_ref[...].reshape(seqs * rows, width)
    cosine, sine = cos_ref[...], sin_ref[...]

    def rope(t):
        return t * cosine + turn_halves(t) * sine

    per = heads // count
    for k in range(count):
        query, key, value = (dot(a1, ref[...]) for ref in w_refs[3 * k : 3 * k + 3])
        for s in range(seqs):
            mine = slice(s * rows, (s + 1) * rows)
            for g in range(per // 2):
                part = slice(g * LANES, (g + 1) * LANES)
                pairs = pair_swap(rope(key[mine, part]), value[mine, part])
                turned = rope(query[mine, part])
                asked = pair_swap(turned[:chunk], turned[chunk:])
                for c in range(2):
                    chip, u = head_units(
                        seqs, heads, members, shift_ref[0], s, k * per + 2 * g + c
                    )
                    msg_ref[chip, 3 * u] = pairs[c][:chunk].astype(BF)
                    msg_ref[chip, 3 * u + 1] = pairs[c][chunk:].astype(BF)
                    msg_ref[chip, 3 * u + 2] = asked[c].astype(BF)


SMEM = pl.BlockSpec(memory_space=pltpu.SMEM)
VMEM = pl.BlockSpec(memory_space=pltpu.VMEM)


def project(shift, x, gain, cosine, sine, parts, members, units):
    seqs, rows, width = x.shape
    count = len(parts)
    heads = sum(part[0].shape[1] for part in parts) // HEAD_DIM
    flat = [w for part in parts for w in part]
    return pl.pallas_call(
        functools.partial(project_kernel, heads, units, members, count),
        in_specs=[SMEM] + [VMEM] * (4 + len(flat)),
        out_specs=[VMEM, VMEM],
        out_shape=[
            jax.ShapeDtypeStruct((members, 3 * units, rows // 2, LANES), BF),
            jax.ShapeDtypeStruct((seqs, rows, width), BF),
        ],
        compiler_params=params(0),
        name="project",
    )(shift, x, gain, cosine, sine, *flat)


def gather_keys(inv_ref, w, kv_refs, kv_s, members, chunk):
    size = len(kv_refs)
    for block in range(2 * members):
        half = 0 if block < members else 1
        chip = inv_ref[block if half == 0 else 2 * members - 1 - block]
        for k, ref in enumerate(kv_refs):
            core = lax.rem(w + k, size)
            start = pl.multiple_of(block * size * chunk + core * chunk, chunk)
            kv_s[pl.ds(start, chunk), :] = ref[chip, half]


def gather_rows(inv_ref, read, put, members, to_high):
    for block in range(2 * members):
        half = 0 if block < members else 1
        chip = inv_ref[block if half == 0 else 2 * members - 1 - block]
        rows = read(chip).astype(F4)
        if (half == 1) != to_high:
            rows = pltpu.roll(rows, HEAD_DIM, 1)
        low = lane_of(rows.shape) < HEAD_DIM
        rows = jnp.where(low, 0.0, rows) if to_high else jnp.where(low, rows, 0.0)
        put(block, rows)


def attend_kernel(members, size, inv_ref, len_ref, w_ref, *refs):
    kv_refs = refs[:size]
    o_ref, of_ref, lse_ref = refs[size : size + 3]
    kv_s, vt_s, q_s, o_s = refs[size + 3 :]
    u = pl.program_id(0)
    chunk = kv_refs[0].shape[2]
    own_rows = q_s.shape[0]
    slot = kv_s.shape[0]
    w = w_ref[0]
    length = len_ref[u]
    gather_keys(inv_ref, w, kv_refs, kv_s, members, chunk)

    def put(block, rows):
        q_s[block * chunk : (block + 1) * chunk, :] = rows * HEAD_DIM ** (-0.5)

    gather_rows(inv_ref, lambda chip: kv_refs[0][chip, 2], put, members, False)

    def flip(i, carry):
        tile = kv_s[pl.ds(pl.multiple_of(i * TK, TK), TK), :].astype(F4)
        vt_s[i] = tile.T[HEAD_DIM:].astype(BF)
        return carry

    lax.fori_loop(0, slot // TK, flip, 0)
    span = TQ * size

    def row_tile(t, carry):
        row = pl.multiple_of(t * TQ, TQ)
        qt = q_s[pl.ds(row, TQ), :].T.astype(BF)
        index = lax.broadcasted_iota(jnp.int32, (1, TQ), 1)
        place = t * span + (index // chunk) * (size * chunk) + w * chunk + index % chunk
        limit = jnp.minimum(place, length - 1)

        def step(masked, kt, state):
            top, total, acc = state
            start = pl.multiple_of(kt * TK, TK)
            scores = dot(kv_s[pl.ds(start, TK), :], qt)
            if masked:
                keys = kt * TK + lax.broadcasted_iota(jnp.int32, (TK, 1), 0)
                scores = jnp.where(keys <= limit, scores, -1e30)
            new_top = jnp.maximum(top, jnp.max(scores, axis=0, keepdims=True))
            weights = jnp.exp(scores - new_top)
            fade = jnp.exp(top - new_top)
            total = total * fade + jnp.sum(weights, axis=0, keepdims=True)
            acc = acc * fade + dot(vt_s[kt], weights.astype(BF))
            return new_top, total, acc

        clear = jnp.minimum(t * span, length) // TK
        last = jnp.minimum(pl.cdiv((t + 1) * span, TK), pl.cdiv(length, TK))
        state = (
            jnp.full((1, TQ), -1e30, F4),
            jnp.zeros((1, TQ), F4),
            jnp.zeros((HEAD_DIM, TQ), F4),
        )
        state = lax.fori_loop(0, clear, functools.partial(step, False), state)
        top, total, acc = lax.fori_loop(clear, last, functools.partial(step, True), state)
        result = acc / total
        of_ref[0, t] = result
        lse_ref[0, t] = top + jnp.log(total)
        blank = jnp.zeros_like(result)
        first = 2 * t * TQ < own_rows
        both = jnp.concatenate(
            [jnp.where(first, result, blank), jnp.where(first, blank, result)], axis=0
        )
        o_s[pl.ds(row, TQ), :] = both.T
        return carry

    lax.fori_loop(0, own_rows // TQ, row_tile, 0)
    for b in range(members):
        other = 2 * members - 1 - b
        rows = (
            o_s[b * chunk : (b + 1) * chunk, :] + o_s[other * chunk : (other + 1) * chunk, :]
        )
        o_ref[inv_ref[b], 0] = rows.astype(BF)


def attend(inv, lengths, w, blocks, units):
    members, _, chunk, _ = blocks[0].shape
    size = len(blocks)
    slot = 2 * members * chunk * size
    rows = 2 * members * chunk
    spec = pl.BlockSpec((members, 3, chunk, LANES), lambda u, *_: (0, u, 0, 0))
    return pl.pallas_call(
        functools.partial(attend_kernel, members, size),
        grid_spec=pltpu.PrefetchScalarGridSpec(
            num_scalar_prefetch=3,
            grid=(units,),
            in_specs=[spec] * size,
            out_specs=[
                pl.BlockSpec((members, 1, chunk, LANES), lambda u, *_: (0, u, 0, 0)),
                pl.BlockSpec((1, rows // TQ, HEAD_DIM, TQ), lambda u, *_: (u, 0, 0, 0)),
                pl.BlockSpec((1, rows // TQ, 1, TQ), lambda u, *_: (u, 0, 0, 0)),
            ],
            scratch_shapes=[
                pltpu.VMEM((slot, LANES), BF),
                pltpu.VMEM((slot // TK, HEAD_DIM, TK), BF),
                pltpu.VMEM((rows, LANES), F4),
                pltpu.VMEM((rows, LANES), F4),
            ],
        ),
        out_shape=[
            jax.ShapeDtypeStruct((members, units, chunk, LANES), BF),
            jax.ShapeDtypeStruct((units, rows // TQ, HEAD_DIM, TQ), F4),
            jax.ShapeDtypeStruct((units, rows // TQ, 1, TQ), F4),
        ],
        compiler_params=params(1),
        name="attend",
    )(inv, lengths, w, *blocks)


def attend_back_kernel(members, size, inv_ref, len_ref, w_ref, *refs):
    kv_refs = refs[:size]
    do_ref, of_ref, lse_ref = refs[size : size + 3]
    dq_ref = refs[size + 3]
    dkv_refs = refs[size + 4 : 2 * size + 4]
    kv_s, kt_s, q_s, do_s, dq_s, dkv_s = refs[2 * size + 4 :]
    u = pl.program_id(0)
    chunk = kv_refs[0].shape[2]
    own_rows = q_s.shape[0]
    slot = kv_s.shape[0]
    w = w_ref[0]
    length = len_ref[u]
    gather_keys(inv_ref, w, kv_refs, kv_s, members, chunk)

    def put_q(block, rows):
        q_s[block * chunk : (block + 1) * chunk, :] = rows * HEAD_DIM ** (-0.5)

    def put_do(block, rows):
        do_s[block * chunk : (block + 1) * chunk, :] = rows

    gather_rows(inv_ref, lambda chip: kv_refs[0][chip, 2], put_q, members, False)
    gather_rows(inv_ref, lambda chip: do_ref[chip, 0], put_do, members, True)

    def flip(i, carry):
        tile = kv_s[pl.ds(pl.multiple_of(i * TK, TK), TK), :].astype(F4)
        kt_s[i] = tile.T[:HEAD_DIM].astype(BF)
        return carry

    lax.fori_loop(0, slot // TK, flip, 0)
    dkv_s[...] = jnp.zeros_like(dkv_s)
    dq_s[...] = jnp.zeros_like(dq_s)
    span = TQ * size

    def row_tile(t, carry):
        row = pl.multiple_of(t * TQ, TQ)
        q_rows = q_s[pl.ds(row, TQ), :]
        do_rows = do_s[pl.ds(row, TQ), :]
        qt, dot_ = q_rows.T, do_rows.T
        delta = jnp.sum(dot_[HEAD_DIM:] * of_ref[0, t], axis=0, keepdims=True)
        qt, dot_ = qt.astype(BF), dot_.astype(BF)
        stacked = jnp.concatenate([do_rows.astype(BF), q_rows.astype(BF)], axis=0)
        lse = lse_ref[0, t]
        index = lax.broadcasted_iota(jnp.int32, (1, TQ), 1)
        place = t * span + (index // chunk) * (size * chunk) + w * chunk + index % chunk
        limit = jnp.minimum(place, length - 1)

        def step(masked, kt, dqt):
            start = pl.multiple_of(kt * TK, TK)
            kv = kv_s[pl.ds(start, TK), :]
            weights = jnp.exp(dot(kv, qt) - lse)
            if masked:
                keys = kt * TK + lax.broadcasted_iota(jnp.int32, (TK, 1), 0)
                weights = jnp.where(keys <= limit, weights, 0.0)
            pulled = dot(kv, dot_)
            back = (weights * (pulled - delta)).astype(BF)
            dkv_s[pl.ds(start, TK), :] += dot(
                jnp.concatenate([weights.astype(BF), back], axis=1), stacked
            )
            return dqt + dot(kt_s[kt], back)

        clear = jnp.minimum(t * span, length) // TK
        last = jnp.minimum(pl.cdiv((t + 1) * span, TK), pl.cdiv(length, TK))
        dqt = jnp.zeros((HEAD_DIM, TQ), F4)
        dqt = lax.fori_loop(0, clear, functools.partial(step, False), dqt)
        dqt = lax.fori_loop(clear, last, functools.partial(step, True), dqt)
        dqt = dqt * HEAD_DIM ** (-0.5)
        blank = jnp.zeros_like(dqt)
        first = 2 * t * TQ < own_rows
        both = jnp.concatenate(
            [jnp.where(first, dqt, blank), jnp.where(first, blank, dqt)], axis=0
        )
        dq_s[pl.ds(row, TQ), :] = both.T
        return carry

    lax.fori_loop(0, jnp.minimum(pl.cdiv(length, span), own_rows // TQ), row_tile, 0)
    for b in range(members):
        other = 2 * members - 1 - b
        chip = inv_ref[b]
        rows = (
            dq_s[b * chunk : (b + 1) * chunk, :] + dq_s[other * chunk : (other + 1) * chunk, :]
        )
        dq_ref[chip, 0] = rows.astype(BF)
        for half, block in ((0, b), (1, other)):
            for k, ref in enumerate(dkv_refs):
                core = lax.rem(w + k, size)
                start = pl.multiple_of(block * size * chunk + core * chunk, chunk)
                ref[chip, half] = dkv_s[pl.ds(start, chunk), :]


def attend_back(inv, lengths, w, blocks, do_msg, kept, lse, units):
    members, _, chunk, _ = blocks[0].shape
    size = len(blocks)
    slot = 2 * members * chunk * size
    rows = 2 * members * chunk
    spec = pl.BlockSpec((members, 3, chunk, LANES), lambda u, *_: (0, u, 0, 0))
    one = pl.BlockSpec((members, 1, chunk, LANES), lambda u, *_: (0, u, 0, 0))
    two = pl.BlockSpec((members, 2, chunk, LANES), lambda u, *_: (0, u, 0, 0))
    return pl.pallas_call(
        functools.partial(attend_back_kernel, members, size),
        grid_spec=pltpu.PrefetchScalarGridSpec(
            num_scalar_prefetch=3,
            grid=(units,),
            in_specs=[spec] * size
            + [
                one,
                pl.BlockSpec((1, rows // TQ, HEAD_DIM, TQ), lambda u, *_: (u, 0, 0, 0)),
                pl.BlockSpec((1, rows // TQ, 1, TQ), lambda u, *_: (u, 0, 0, 0)),
            ],
            out_specs=[one] + [two] * size,
            scratch_shapes=[
                pltpu.VMEM((slot, LANES), BF),
                pltpu.VMEM((slot // TK, HEAD_DIM, TK), BF),
                pltpu.VMEM((rows, LANES), F4),
                pltpu.VMEM((rows, LANES), F4),
                pltpu.VMEM((rows, LANES), F4),
                pltpu.VMEM((slot, LANES), F4),
            ],
        ),
        out_shape=[jax.ShapeDtypeStruct((members, units, chunk, LANES), BF)]
        + [jax.ShapeDtypeStruct((members, 2 * units, chunk, LANES), F4)] * size,
        compiler_params=params(1),
        name="attend_back",
    )(inv, lengths, w, *blocks, do_msg, kept, lse)


def mix_kernel(heads, count, shift_ref, o_ref, x_ref, gain_ref, *refs):
    w_refs = refs[:count]
    mixed_ref, state_ref, a2_ref = refs[count:]
    members, _, chunk, _ = o_ref.shape
    seqs, rows, width = x_ref.shape
    for s in range(seqs):
        for g in range(heads // 2):
            pair = []
            for c in range(2):
                chip, u = head_units(seqs, heads, members, shift_ref[0], s, 2 * g + c)
                pair.append(o_ref[chip, u].astype(F4))
            early, late = pair_swap(*pair)
            part = slice(g * LANES, (g + 1) * LANES)
            mixed_ref[s, :chunk, part] = early.astype(BF)
            mixed_ref[s, chunk:, part] = late.astype(BF)
    inner = heads * HEAD_DIM // count
    made = 0.0
    for k in range(count):
        mixed = mixed_ref[:, :, k * inner : (k + 1) * inner].reshape(seqs * rows, inner)
        made = made + dot(mixed, w_refs[k][...])
    for s in range(seqs):
        state = x_ref[s].astype(F4) + made[s * rows : (s + 1) * rows]
        state_ref[s] = state
        scale = lax.rsqrt(jnp.mean(state * state, axis=-1, keepdims=True) + EPS)
        a2_ref[s] = (state * scale * gain_ref[...]).astype(BF)


def mix(shift, o_msg, x, gain, parts):
    seqs, rows, width = x.shape
    inner = sum(part.shape[0] for part in parts)
    return pl.pallas_call(
        functools.partial(mix_kernel, inner // HEAD_DIM, len(parts)),
        in_specs=[SMEM] + [VMEM] * (3 + len(parts)),
        out_specs=[VMEM] * 3,
        out_shape=[
            jax.ShapeDtypeStruct((seqs, rows, inner), BF),
            jax.ShapeDtypeStruct((seqs, rows, width), F4),
            jax.ShapeDtypeStruct((seqs, rows, width), BF),
        ],
        compiler_params=params(0),
        name="mix",
    )(shift, o_msg, x, gain, *parts)


def norm_back(values, gain, upstream):
    scale = lax.rsqrt(jnp.mean(values * values, axis=-1, keepdims=True) + EPS)
    unit = values * scale
    pulled = upstream * gain
    result = scale * (pulled - unit * jnp.mean(pulled * unit, axis=-1, keepdims=True))
    return result, jnp.sum(upstream * unit, axis=0, keepdims=True)


def unrotate_kernel(heads, count, shift_ref, msg_ref, cos_ref, sin_ref, dqkv_ref):
    members, triple, chunk, _ = msg_ref.shape
    units = triple // 3
    seqs = dqkv_ref.shape[0]
    cosine, sine = cos_ref[...], sin_ref[...]
    per = heads // count
    inner = per * HEAD_DIM

    def rope_back(grad):
        return grad * cosine - turn_halves(grad) * sine

    for k in range(count):
        for s in range(seqs):
            for g in range(per // 2):
                pair, asked = [], []
                for c in range(2):
                    chip, u = head_units(
                        seqs, heads, members, shift_ref[0], s, k * per + 2 * g + c
                    )
                    both = [msg_ref[chip, 2 * u], msg_ref[chip, 2 * u + 1]]
                    pair.append(jnp.concatenate(both, axis=0).astype(F4))
                    asked.append(msg_ref[chip, 2 * units + u].astype(F4))
                key, value = pair_swap(*pair)
                query = jnp.concatenate(pair_swap(*asked), axis=0)
                at = 3 * k * inner + g * LANES
                dqkv_ref[s, :, at : at + LANES] = rope_back(query).astype(BF)
                at = at + inner
                dqkv_ref[s, :, at : at + LANES] = rope_back(key).astype(BF)
                at = at + inner
                dqkv_ref[s, :, at : at + LANES] = value.astype(BF)


def unrotate(shift, msg, cosine, sine, seqs, heads, count):
    rows = 2 * msg.shape[2]
    return pl.pallas_call(
        functools.partial(unrotate_kernel, heads, count),
        in_specs=[SMEM] + [VMEM] * 3,
        out_specs=VMEM,
        out_shape=jax.ShapeDtypeStruct((seqs, rows, 3 * heads * HEAD_DIM), BF),
        compiler_params=params(0),
        name="unrotate",
    )(shift, msg, cosine, sine)


def unproject_kernel(count, dqkv_ref, x_ref, dstate_ref, gain_ref, *refs):
    w_refs = refs[:count]
    dx_ref, dgain_ref = refs[count:]
    seqs, rows, width = x_ref.shape
    inner = dqkv_ref.shape[2] // count
    made = 0.0
    for k in range(count):
        cols = dqkv_ref[:, :, k * inner : (k + 1) * inner].reshape(seqs * rows, inner)
        made = made + dot(cols, w_refs[k][...])
    total = jnp.zeros((1, width), F4)
    for s in range(seqs):
        pulled, dgain = norm_back(
            x_ref[s].astype(F4), gain_ref[...], made[s * rows : (s + 1) * rows]
        )
        total = total + dgain
        dx_ref[s] = (dstate_ref[s] + pulled).astype(BF)
    dgain_ref[...] = total


def unproject(dqkv, x, dstate, gain, parts):
    seqs, rows, width = x.shape
    return pl.pallas_call(
        functools.partial(unproject_kernel, len(parts)),
        in_specs=[VMEM] * (4 + len(parts)),
        out_specs=[VMEM] * 2,
        out_shape=[
            jax.ShapeDtypeStruct((seqs, rows, width), BF),
            jax.ShapeDtypeStruct((1, width), F4),
        ],
        compiler_params=params(0),
        name="unproject",
    )(dqkv, x, dstate, gain, *parts)


def dispatch_kernel(info_ref, second_ref, cot_ref, out_ref):
    step = pl.program_id(0)
    count, held, double = out_ref.shape
    width = double // 2
    shape = (count * held, info_ref.shape[1])
    ids = lax.broadcasted_iota(jnp.int32, shape, 0) + step * (count * held)
    target = info_ref[0:2, :].astype(jnp.int32)
    one, two = ids == target[0:1], ids == target[1:2]
    hits = (one | two).astype(BF)
    gate = jnp.where(one, info_ref[2:3, :], 0.0) + jnp.where(two, info_ref[3:4, :], 0.0)
    gate = jnp.sum(gate, axis=1, keepdims=True)
    out_ref[:, :, :width] = dot(hits, second_ref[...]).astype(BF).reshape(count, held, width)
    out_ref[:, :, width:] = (
        (dot(hits, cot_ref[...]) * gate).astype(BF).reshape(count, held, width)
    )


def dispatch(info, second, cot, experts, held):
    total, width = second.shape
    count = 4 if experts % 4 == 0 else 1
    return pl.pallas_call(
        dispatch_kernel,
        grid=(experts // count,),
        in_specs=[whole(info.shape), whole(second.shape), whole(cot.shape)],
        out_specs=pl.BlockSpec((count, held, 2 * width), lambda e: (e, 0, 0)),
        out_shape=jax.ShapeDtypeStruct((experts, held, 2 * width), BF),
        compiler_params=params(1),
        name="dispatch",
    )(info, second, cot)


def finish_kernel(heads, size, count, shift_ref, info_ref, state_ref, cot_ref, gain_ref, router_ref, *refs):
    home_refs, refs = refs[:size], refs[size:]
    dense_refs, refs = refs[:size], refs[size:]
    w_refs = refs[:count]
    out_ref, dstate_ref, low_ref, logit_ref, msg_ref, dgain_ref = refs[count:]
    step = pl.program_id(0)
    take, rows, width = state_ref.shape
    lines = take * rows
    members, units, chunk, _ = msg_ref.shape
    slots = home_refs[0].shape[0]
    experts = router_ref.shape[0]
    info = info_ref[...].reshape(lines, info_ref.shape[2])
    target = info[:, : 2 * size].astype(jnp.int32)
    gates = [info[:, 2 * size + c : 2 * size + c + 1] for c in range(2)]
    chosen = info[:, 2 * size + 2 : 2 * size + 4].astype(jnp.int32)
    ids = lax.broadcasted_iota(jnp.int32, (lines, slots), 1)
    made, back = [0.0, 0.0], 0.0
    for k in range(size):
        hits = [ids == target[:, 2 * k + c : 2 * k + c + 1] for c in range(2)]
        for c in range(2):
            made[c] = made[c] + dot(hits[c].astype(BF), home_refs[k][:, :width])
        back = back + dot((hits[0] | hits[1]).astype(BF), home_refs[k][:, width:])
    cot = cot_ref[...].reshape(lines, width).astype(F4)
    pulled = [jnp.sum(y * cot, axis=-1, keepdims=True) for y in made]
    middle = gates[0] * pulled[0] + gates[1] * pulled[1]
    names = lax.broadcasted_iota(jnp.int32, (lines, experts), 1)
    logit = 0.0
    for c in range(2):
        logit = logit + jnp.where(
            names == chosen[:, c : c + 1], gates[c] * (pulled[c] - middle), 0.0
        )
    logit = logit.astype(BF)
    logit_ref[...] = logit.reshape(take, rows, experts)
    back = back + dot(logit, router_ref[...])
    branch = gates[0] * made[0] + gates[1] * made[1]
    for ref in dense_refs:
        dense = ref[...].reshape(lines, 2 * width)
        branch = branch + dense[:, :width]
        back = back + dense[:, width:]
    state = state_ref[...].reshape(lines, width)
    out_ref[...] = (state + branch).astype(BF).reshape(take, rows, width)
    pulled, dgain = norm_back(state, gain_ref[...], back)
    dstate = cot + pulled
    dstate_ref[...] = dstate.reshape(take, rows, width)
    low = dstate.astype(BF)
    low_ref[...] = low.reshape(take, rows, width)
    seqs = take * pl.num_programs(0)

    @pl.when(step == 0)
    def _():
        dgain_ref[...] = jnp.zeros_like(dgain_ref)
        if members * units > heads * seqs:
            msg_ref[...] = jnp.zeros_like(msg_ref)

    dgain_ref[...] += dgain
    per = heads // count
    for k in range(count):
        mixed_back = dot(low, w_refs[k][...])
        for s in range(take):
            for g in range(per // 2):
                part = mixed_back[s * rows : (s + 1) * rows, g * LANES : (g + 1) * LANES]
                pair = pair_swap(part[:chunk], part[chunk:])
                for c in range(2):
                    chip, u = head_units(
                        seqs, heads, members, shift_ref[0], step * take + s, k * per + 2 * g + c
                    )
                    msg_ref[chip, u] = pair[c].astype(BF)


def finish(shift, info, state, cot, gain, router, homes, denses, parts, members, units):
    seqs, rows, width = state.shape
    inner = sum(part.shape[1] for part in parts)
    experts = router.shape[0]
    take = max(1, min(seqs, 256 // rows))
    msg = (members, units, rows // 2, LANES)
    some = lambda cols: pl.BlockSpec((take, rows, cols), lambda s: (s, 0, 0))
    return pl.pallas_call(
        functools.partial(finish_kernel, inner // HEAD_DIM, len(homes), len(parts)),
        grid=(seqs // take,),
        in_specs=[SMEM, some(info.shape[2]), some(width), some(width), whole((1, width))]
        + [whole(router.shape)]
        + [whole(home.shape) for home in homes]
        + [some(2 * width)] * len(denses)
        + [whole(part.shape) for part in parts],
        out_specs=[some(width)] * 3 + [some(experts), whole(msg), whole((1, width))],
        out_shape=[
            jax.ShapeDtypeStruct((seqs, rows, width), BF),
            jax.ShapeDtypeStruct((seqs, rows, width), F4),
            jax.ShapeDtypeStruct((seqs, rows, width), BF),
            jax.ShapeDtypeStruct((seqs, rows, experts), BF),
            jax.ShapeDtypeStruct(msg, BF),
            jax.ShapeDtypeStruct((1, width), F4),
        ],
        compiler_params=params(1),
        name="finish",
    )(shift, info, state, cot, gain, router, *homes, *denses, *parts)


def place_kernel(copies, *refs):
    total = refs[0][...].astype(F4)
    for ref in refs[1:copies]:
        total = total + ref[...].astype(F4)
    for n, out in enumerate(refs[copies:]):
        out[...] = untile(total, n)


def place(blocks, experts):
    members, rows, triple = blocks.shape
    hidden = triple // 3
    copies = members // experts
    take = 2 if experts % 2 == 0 else 1
    return pl.pallas_call(
        functools.partial(place_kernel, copies),
        grid=(experts // take,),
        in_specs=[
            pl.BlockSpec((take, rows, triple), lambda e, n=n: (n * experts // take + e, 0, 0))
            for n in range(copies)
        ],
        out_specs=[pl.BlockSpec((take, rows, hidden), lambda e: (e, 0, 0))] * 3,
        out_shape=[jax.ShapeDtypeStruct((experts, rows, hidden), F4)] * 3,
        compiler_params=params(1),
        name="place",
    )(*[blocks] * copies)


def gated_kernel(count, tiles, x_ref, d_ref, *refs):
    w_refs = refs[: 3 * count]
    out_ref, hid_ref, acc_ref = refs[3 * count :]
    step = pl.program_id(0)
    rows, width = x_ref.shape
    tile = hid_ref.shape[1] // 3
    take = min(256, rows)

    @pl.when(step == 0)
    def _():
        acc_ref[...] = jnp.zeros_like(acc_ref)

    for k in range(count):

        @pl.when(step // tiles == k)
        def _(k=k):
            gate_w, up_w, down_w = w_refs[3 * k : 3 * k + 3]
            gate_t, up_t, down_t = gate_w[...].T, up_w[...].T, down_w[...].T
            for r in range(0, rows, take):
                mine = slice(r, r + take)
                x, d = x_ref[mine, :], d_ref[mine, :]
                gate, up, back = dot(x, gate_w[...]), dot(x, up_w[...]), dot(d, down_t)
                share = 1.0 / (1.0 + jnp.exp(-gate))
                silu = gate * share
                hidden = (silu * up).astype(BF)
                dup = (back * silu).astype(BF)
                dgate = (back * up * (share * (1.0 + gate * (1.0 - share)))).astype(BF)
                hid_ref[mine, :tile] = dgate
                hid_ref[mine, tile : 2 * tile] = dup
                hid_ref[mine, 2 * tile :] = hidden
                acc_ref[mine, :width] += dot(hidden, down_w[...])
                acc_ref[mine, width:] += dot(dgate, gate_t) + dot(dup, up_t)

    @pl.when(step == pl.num_programs(0) - 1)
    def _():
        out_ref[...] = acc_ref[...].astype(out_ref.dtype)


def tile_of(hidden):
    return min(512, hidden)


def gated(x, d, parts, kind, name, both=False):
    rows = x.shape[0]
    width, hidden = parts[0][0].shape
    tile = tile_of(hidden)
    tiles = hidden // tile
    count = len(parts)
    flat, specs = [], []
    for k, part in enumerate(parts):
        at = lambda f, k=k: jnp.clip(f - k * tiles, 0, tiles - 1)
        cols = pl.BlockSpec((width, tile), lambda f, at=at: (0, at(f)))
        lines = pl.BlockSpec((tile, width), lambda f, at=at: (at(f), 0))
        flat += list(part)
        specs += [cols, cols, lines]
    return pl.pallas_call(
        functools.partial(gated_kernel, count, tiles),
        grid=(count * tiles,),
        in_specs=[
            pl.BlockSpec((rows, width), lambda f: (0, 0)),
            pl.BlockSpec((rows, width), lambda f: (0, 1 if both else 0)),
        ]
        + specs,
        out_specs=[whole((rows, 2 * width)), pl.BlockSpec((rows, 3 * tile), lambda f: (0, f))],
        out_shape=[
            jax.ShapeDtypeStruct((rows, 2 * width), kind),
            jax.ShapeDtypeStruct((rows, 3 * count * hidden), BF),
        ],
        scratch_shapes=[pltpu.VMEM((rows, 2 * width), F4)],
        compiler_params=params(1),
        name=name,
    )(x, d, *flat)


def gated_grads_kernel(x_ref, d_ref, hid_ref, out_ref, xt_ref, dt_ref):
    tile = hid_ref.shape[1] // 3

    @pl.when(pl.program_id(0) == 0)
    def _():
        xt_ref[...] = x_ref[...].T
        dt_ref[...] = d_ref[...].T

    out_ref[:, : 2 * tile] = dot(xt_ref[...], hid_ref[:, : 2 * tile]).astype(BF)
    out_ref[:, 2 * tile :] = dot(dt_ref[...], hid_ref[:, 2 * tile :]).astype(BF)


def gated_grads(x, d, hid, k, count, name, both=False):
    rows = x.shape[0]
    width = x.shape[1] // 2 if both else x.shape[1]
    hidden = hid.shape[1] // 3 // count
    tile = tile_of(hidden)
    tiles = hidden // tile
    return pl.pallas_call(
        gated_grads_kernel,
        grid=(tiles,),
        in_specs=[
            pl.BlockSpec((rows, width), lambda f: (0, 0)),
            pl.BlockSpec((rows, width), lambda f: (0, 1 if both else 0)),
            pl.BlockSpec((rows, 3 * tile), lambda f: (0, k * tiles + f)),
        ],
        out_specs=pl.BlockSpec((width, 3 * tile), lambda f: (0, f)),
        out_shape=jax.ShapeDtypeStruct((width, 3 * hidden), BF),
        scratch_shapes=[pltpu.VMEM((width, rows), BF)] * 2,
        compiler_params=params(1),
        cost_estimate=pl.CostEstimate(
            flops=6 * rows * width * hidden,
            bytes_accessed=2 * (2 * rows * width + 3 * hidden * (rows + width)),
            transcendentals=0,
        ),
        name=name,
    )(x, d, hid)


def untile(array, n):
    hidden = array.shape[-1] // 3
    tile = tile_of(hidden)
    parts = [
        array[..., (3 * j + n) * tile : (3 * j + n + 1) * tile] for j in range(hidden // tile)
    ]
    return jnp.concatenate(parts, axis=-1)


def per_device(
    inputs,
    cotangent,
    lengths,
    block_pairs,
    routes,
    attn_gain,
    query_weight,
    key_weight,
    value_weight,
    out_weight,
    ffn_gain,
    router_weight,
    expert_gate,
    expert_up,
    expert_down,
    dense_gate,
    dense_up,
    dense_down,
):
    pair_rows, seqs, width = inputs.shape[1:]
    members, size = lax.axis_size("ctx"), lax.axis_size("wt")
    ctx, w = lax.axis_index("ctx"), lax.axis_index("wt")
    experts = expert_gate.shape[0]
    block = pair_rows // 2
    chunk = block // size
    rows = 2 * chunk * seqs
    inner = query_weight.shape[1] * size
    heads = inner // HEAD_DIM
    units = -(-(seqs * heads) // members)

    def rows_of(array, k):
        parted = array.reshape(2, size, chunk, seqs, -1)
        mine = lax.dynamic_index_in_dim(parted, (w + k) % size, 1, False)
        return mine.transpose(2, 0, 1, 3).reshape(seqs, 2 * chunk, -1)

    def places_of(k):
        pair = lax.dynamic_index_in_dim(block_pairs, ctx, 0, False)
        blocks = jnp.stack([pair, 2 * members - 1 - pair])
        core = (w + k) % size
        return (blocks[:, None] * block + core * chunk + jnp.arange(chunk)[None, :]).reshape(-1)

    x = rows_of(inputs[0], 0)
    half = HEAD_DIM // 2
    freqs = THETA ** (-jnp.arange(half, dtype=F4) / half)
    angles = places_of(0).astype(F4)[:, None] * freqs[None, :]
    cosine = jnp.tile(jnp.cos(angles), (1, LANES // half))
    sine = jnp.tile(
        jnp.concatenate([-jnp.sin(angles), jnp.sin(angles)], axis=1), (1, LANES // HEAD_DIM)
    )

    local = inner // size
    split = size == 2 and local % LANES == 0
    shift = (w * (heads // size) if split else jnp.zeros_like(w)).astype(jnp.int32)[None]
    own_qkv = [query_weight, key_weight, value_weight]
    if split:
        parts = list(zip(*[wt_gather(weight) for weight in own_qkv]))
        out_parts = wt_gather(out_weight)
    else:
        parts = [[lax.all_gather(weight, "wt", axis=1, tiled=True) for weight in own_qkv]]
        out_parts = [lax.all_gather(out_weight, "wt", axis=0, tiled=True)]
    msg, a1 = project(shift, x, attn_gain[None], cosine, sine, parts, members, units)
    got = lax.all_to_all(msg, "ctx", 0, 0, tiled=True)

    back_parts = [jnp.concatenate([weight.T for weight in part]) for part in parts]
    out_back = [part.T for part in out_parts]
    expert = ctx % experts
    expert_parts = list(
        zip(
            *[
                wt_gather(lax.dynamic_index_in_dim(weights, expert, 0, False))
                for weights in (expert_gate, expert_up, expert_down)
            ]
        )
    )
    total_rows = rows * size
    cots = []
    for k in range(size):
        valid = places_of(k)[None, :] < lengths[:, None]
        cots.append(
            jnp.where(valid[:, :, None], rows_of(cotangent[0], k), jnp.zeros((), BF)).reshape(
                rows, width
            )
        )
    cot = jnp.concatenate(cots)

    parted = routes[0].reshape(2, size, chunk, seqs, 2).transpose(1, 3, 0, 2, 4)
    chosen_all = parted.reshape(total_rows, 2)
    names = jnp.arange(experts, dtype=jnp.int32)
    picks_all = chosen_all[:, :, None] == names
    marks = jnp.any(picks_all, axis=1).astype(BF)
    index = jnp.arange(total_rows)
    before = dot((index[None, :] < index[:, None]).astype(BF), marks)
    order_all = jnp.sum(jnp.where(picks_all, before[:, None, :], 0.0), axis=-1).astype(jnp.int32)
    share = -(-CAPACITY // size)
    held = -(-share // 16) * 16

    def targets(chosen, order, core):
        inside = (order >= core * held) & (order < (core + 1) * held)
        return jnp.where(inside, chosen * held + order - core * held, -1)

    def own_first(array):
        pieces = array.reshape(size, rows, 2)
        pieces = jnp.concatenate([pieces, pieces[:-1]])
        return lax.dynamic_slice_in_dim(pieces, w, size, 0).reshape(total_rows, 2)

    chosen, order_here = own_first(chosen_all), own_first(order_all)
    target = targets(chosen, order_here, w)
    own_targets = [
        targets(chosen[:rows], order_here[:rows], (w + k) % size).astype(F4) for k in range(size)
    ]
    inv = jnp.argsort(block_pairs).astype(jnp.int32)
    unit_slots = jnp.minimum((ctx + members * jnp.arange(units)) // heads, seqs - 1)
    unit_lengths = lengths[unit_slots]
    w_arg = w.astype(jnp.int32)[None]
    got, back_parts, out_back, expert_parts, cots, cot, chosen, target, own_targets, inv, unit_lengths = (
        lax.optimization_barrier(
            (
                got,
                back_parts,
                out_back,
                expert_parts,
                cots,
                cot,
                chosen,
                target,
                own_targets,
                inv,
                unit_lengths,
            )
        )
    )

    blocks = wt_gather(got)
    o_msg, kept, lse = attend(inv, unit_lengths, w_arg, blocks, units)
    o_got = lax.all_to_all(o_msg, "ctx", 0, 0, tiled=True)
    mixed, state, second_own = mix(shift, o_got, x, ffn_gain[None], out_parts)

    second = jnp.concatenate(wt_gather(second_own.reshape(rows, width)))
    picks = chosen[:, :, None] == names
    logits = dot(second, router_weight)
    selected = jnp.sum(jnp.where(picks, logits[:, None, :], 0.0), axis=-1)
    raised = jnp.exp(selected - jnp.max(selected, axis=-1, keepdims=True))
    gates = raised / jnp.sum(raised, axis=-1, keepdims=True)
    info = jnp.concatenate([target.astype(F4), gates, jnp.zeros((total_rows, 4), F4)], axis=1)
    sent = dispatch(info.T, second, cot, experts, held)
    info = jnp.concatenate(own_targets + [gates[:rows], chosen[:rows].astype(F4)], axis=1)
    info = info.reshape(seqs, 2 * chunk, -1)
    groups = None
    if members != experts:
        groups = [[g * experts + e for e in range(experts)] for g in range(members // experts)]
    swap = functools.partial(
        lax.all_to_all,
        axis_name="ctx",
        split_axis=0,
        concat_axis=0,
        axis_index_groups=groups,
        tiled=True,
    )

    sent, second = lax.optimization_barrier((sent, second))
    arrived = swap(sent)
    dense, dense_hid = gated(second, cot, [[dense_gate, dense_up, dense_down]], F4, "dense_branch")
    dense_grads = gated_grads(second, cot, dense_hid, 0, 1, "dense_grads")
    near = 4 if members % 4 == 0 else 1
    outer = members // near
    near_groups = [[o * near + i for i in range(near)] for o in range(outer)]
    far_groups = [[o * near + i for o in range(outer)] for i in range(near)]
    dense_grads = dense_grads.reshape(outer, near, width // members, -1).swapaxes(0, 1)
    dense_grads = dense_grads.reshape(width, -1)
    denses = [dense[:rows]]
    for k in range(1, size):
        perm = [(i, (i + k) % size) for i in range(size)]
        denses.append(lax.ppermute(dense[k * rows : (k + 1) * rows], "wt", perm))
    arrived, denses, dense_grads = lax.optimization_barrier((arrived, denses, dense_grads))
    dense_near = lax.psum_scatter(
        dense_grads,
        "ctx",
        scatter_dimension=0,
        tiled=True,
        axis_index_groups=near_groups,
    )

    arrived = arrived.reshape(experts * held, 2 * width)
    returned, hid = gated(
        arrived, arrived, [list(part) for part in expert_parts], BF, "expert_branch", True
    )
    home = swap(returned.reshape(experts, held, 2 * width))
    hidden = expert_gate.shape[2]
    expert_sum = None
    for k in list(range(1, size)) + [0]:
        made = gated_grads(arrived, arrived, hid, k, size, "expert_grads", True)
        if k:
            made = lax.ppermute(made, "wt", [(i, (i + k) % size) for i in range(size)])
        expert_sum = made.astype(F4) if expert_sum is None else expert_sum + made.astype(F4)
    expert_sum = expert_sum.astype(BF).reshape(members, width // members, 3 * hidden)
    home, expert_sum, dense_near = lax.optimization_barrier((home, expert_sum, dense_near))
    dense_sum = lax.psum_scatter(
        dense_near, "ctx", scatter_dimension=0, tiled=True, axis_index_groups=far_groups
    )
    homes = wt_gather(home.reshape(experts * held, 2 * width))

    own_cot = cots[0].reshape(seqs, 2 * chunk, width)
    denses = [part.reshape(seqs, 2 * chunk, 2 * width) for part in denses]
    output, dstate, dstate_low, logit_back, do_msg, ffn_grad = finish(
        shift,
        info,
        state,
        own_cot,
        ffn_gain[None],
        router_weight.T,
        homes,
        denses,
        out_back,
        members,
        units,
    )
    do_got = lax.all_to_all(do_msg, "ctx", 0, 0, tiled=True)

    def share_of(array, kinds, k):
        if split:
            return array[..., k * kinds * local : (k + 1) * kinds * local].reshape(rows, -1)
        cols = array.reshape(rows, kinds, size, local)
        return lax.dynamic_index_in_dim(cols, (w + k) % size, 2, False).reshape(rows, -1)

    def split_wt(left, right, kinds):
        pieces = []
        for k in range(size):
            made = dot_tn(left.reshape(rows, -1), share_of(right, kinds, k))
            pieces.append(made if k == 0 else made.astype(BF))
        return wt_scatter(pieces).astype(BF)

    def by_owner(blocks):
        return jnp.concatenate(blocks, axis=1).reshape(members, width // members, -1)

    router_grad = dot_tn(second_own.reshape(rows, width), logit_back.reshape(rows, experts))
    small = wt_sum(jnp.concatenate([ffn_grad.T, router_grad], axis=1))
    out_grad = split_wt(dstate_low, mixed, 1)
    do_got, out_grad, small, output, expert_sum, dense_sum = lax.optimization_barrier(
        (do_got, out_grad, small, output, expert_sum, dense_sum)
    )
    expert_got = lax.all_to_all(expert_sum, "ctx", 0, 0, tiled=True)
    dq, *dkv = attend_back(inv, unit_lengths, w_arg, blocks, do_got, kept, lse, units)
    dq, dkv, expert_got = lax.optimization_barrier((dq, dkv, expert_got))
    dkv = wt_scatter(dkv).astype(BF)
    grad_msg = jnp.concatenate([dkv, dq], axis=1)
    grad_got = lax.all_to_all(grad_msg, "ctx", 0, 0, tiled=True)
    expert_grads = place(expert_got, experts)
    dqkv = unrotate(shift, grad_got, cosine, sine, seqs, heads, len(parts))
    dx, attn_grad = unproject(dqkv, x, dstate, attn_gain[None], back_parts)
    small = jnp.concatenate([wt_sum(attn_grad).T, small], axis=1)
    small_high = small.astype(BF)
    small_low = (small - small_high.astype(F4)).astype(BF)
    few = experts + 2
    blank = jnp.zeros((width, -(2 * few) % LANES), BF)
    last_msg = by_owner([split_wt(a1, dqkv, 3), out_grad, small_high, small_low, blank])
    last_got = lax.all_to_all(last_msg, "ctx", 0, 0, tiled=True)
    last_sum = jnp.sum(last_got.astype(F4), axis=0)
    tail = last_sum[:, 4 * local :]
    tail = tail[:, :few] + tail[:, few : 2 * few]

    def to_tokens(own):
        array = in_order(wt_gather(own)).reshape(size, seqs, 2, chunk, width)
        return array.transpose(2, 0, 3, 1, 4).reshape(inputs.shape)

    return (
        to_tokens(output),
        to_tokens(dx),
        tail[:, 0],
        *[last_sum[:, n * local : (n + 1) * local] for n in range(3)],
        last_sum[:, 3 * local : 4 * local].T,
        tail[:, 1],
        tail[:, 2:],
        *expert_grads[:2],
        expert_grads[2].transpose(0, 2, 1),
        *[untile(dense_sum, n).astype(F4) for n in range(2)],
        untile(dense_sum, 2).astype(F4).T,
    )


def solution(mesh):
    placed = (
        P("ctx", None, None, None),
        P("ctx", None, None, None),
        P(),
        P(),
        P("ctx", None, None, None),
        P(),
        P(None, "wt"),
        P(None, "wt"),
        P(None, "wt"),
        P("wt", None),
        P(),
        P(),
        P(None, None, "wt"),
        P(None, None, "wt"),
        P(None, "wt", None),
        P(None, "wt"),
        P(None, "wt"),
        P("wt", None),
    )
    return jax.shard_map(
        per_device,
        mesh=mesh,
        in_specs=placed,
        out_specs=(
            P("ctx", None, None, None),
            P("ctx", None, None, None),
            P("ctx"),
            P("ctx", "wt"),
            P("ctx", "wt"),
            P("ctx", "wt"),
            P("wt", "ctx"),
            P("ctx"),
            P("ctx", None),
            P(None, "ctx", "wt"),
            P(None, "ctx", "wt"),
            P(None, "wt", "ctx"),
            P("ctx", "wt"),
            P("ctx", "wt"),
            P("wt", "ctx"),
        ),
        check_vma=False,
    )
```

```python
import functools

import jax
import jax.numpy as jnp
from jax import lax
from jax.experimental import pallas as pl
from jax.experimental.pallas import tpu as pltpu
from jax.sharding import PartitionSpec as P

HEAD_DIM = 64
CAPACITY = 160
EPS = 1e-06
THETA = 10000.0
LANES = 128
BF = jnp.bfloat16
F4 = jnp.float32
TQ = 512
TK = 1024
VMEM_LIMIT = 56 * 1024 * 1024


def dot(a, b):
    return jnp.dot(a, b, preferred_element_type=F4)


def dot_nt(a, b):
    return lax.dot_general(a, b, (((1,), (1,)), ((), ())), preferred_element_type=F4)


def dot_tn(a, b):
    return lax.dot_general(a, b, (((0,), (0,)), ((), ())), preferred_element_type=F4)


def wt_gather(x):
    size = lax.axis_size("wt")
    return [x] + [
        lax.ppermute(x, "wt", [(i, (i - k) % size) for i in range(size)]) for k in range(1, size)
    ]


def wt_scatter(pieces):
    size = lax.axis_size("wt")
    total = pieces[0]
    for k in range(1, size):
        moved = lax.ppermute(pieces[k], "wt", [(i, (i + k) % size) for i in range(size)])
        total = total + moved.astype(total.dtype)
    return total


def wt_sum(x):
    if lax.axis_size("wt") == 2:
        return x + lax.ppermute(x, "wt", [(0, 1), (1, 0)])
    return lax.psum(x, "wt")


def ctx_sum(x):
    size = lax.axis_size("ctx")
    if size & (size - 1):
        return lax.psum(x, "ctx")
    by = 1
    while by < size:
        x = x + lax.ppermute(x, "ctx", [(i, i ^ by) for i in range(size)])
        by *= 2
    return x


def in_order(parts):
    size = len(parts)
    start = (size - lax.axis_index("wt")) % size
    return lax.dynamic_slice_in_dim(jnp.stack(parts + parts[:-1]), start, size, 0)


def lane_of(shape):
    return lax.broadcasted_iota(jnp.int32, shape, len(shape) - 1)


def pair_swap(a, b):
    low = lane_of(a.shape) < HEAD_DIM
    return (
        jnp.where(low, a, pltpu.roll(b, HEAD_DIM, 1)),
        jnp.where(low, pltpu.roll(a, HEAD_DIM, 1), b),
    )


def turn_halves(t):
    first = lane_of(t.shape) % HEAD_DIM < HEAD_DIM // 2
    return jnp.where(
        first,
        pltpu.roll(t, LANES - HEAD_DIM // 2, 1),
        pltpu.roll(t, HEAD_DIM // 2, 1),
    )


def params(count):
    return pltpu.CompilerParams(
        vmem_limit_bytes=VMEM_LIMIT, dimension_semantics=("arbitrary",) * count
    )


def whole(shape):
    return pl.BlockSpec(shape, lambda *i: (0,) * len(shape))


def head_units(seqs, heads, members, shift, s, rel):
    unit = s * heads + lax.rem(rel + shift, heads)
    return lax.rem(unit, members), lax.div(unit, members)


def project_kernel(heads, units, members, count, shift_ref, x_ref, gain_ref, cos_ref, sin_ref, *refs):
    w_refs = refs[: 3 * count]
    msg_ref, a1_ref = refs[3 * count :]
    seqs, rows, width = x_ref.shape
    chunk = rows // 2
    for s in range(seqs):
        x = x_ref[s].astype(F4)
        scale = lax.rsqrt(jnp.mean(x * x, axis=-1, keepdims=True) + EPS)
        a1_ref[s] = (x * scale * gain_ref[...]).astype(BF)
    if units * members > heads * seqs:
        msg_ref[...] = jnp.zeros_like(msg_ref)
    a1 = a1_ref[...].reshape(seqs * rows, width)
    cosine, sine = cos_ref[...], sin_ref[...]

    def rope(t):
        return t * cosine + turn_halves(t) * sine

    per = heads // count
    for k in range(count):
        query, key, value = (dot(a1, ref[...]) for ref in w_refs[3 * k : 3 * k + 3])
        for s in range(seqs):
            mine = slice(s * rows, (s + 1) * rows)
            for g in range(per // 2):
                part = slice(g * LANES, (g + 1) * LANES)
                pairs = pair_swap(rope(key[mine, part]), value[mine, part])
                turned = rope(query[mine, part])
                asked = pair_swap(turned[:chunk], turned[chunk:])
                for c in range(2):
                    chip, u = head_units(
                        seqs, heads, members, shift_ref[0], s, k * per + 2 * g + c
                    )
                    msg_ref[chip, 3 * u] = pairs[c][:chunk].astype(BF)
                    msg_ref[chip, 3 * u + 1] = pairs[c][chunk:].astype(BF)
                    msg_ref[chip, 3 * u + 2] = asked[c].astype(BF)


SMEM = pl.BlockSpec(memory_space=pltpu.SMEM)


def one_step(kernel, name, shift, arrays, shapes):
    return pl.pallas_call(
        kernel,
        grid=(1,),
        in_specs=[SMEM] + [whole(array.shape) for array in arrays],
        out_specs=[whole(shape.shape) for shape in shapes],
        out_shape=shapes,
        compiler_params=params(1),
        name=name,
    )(shift, *arrays)


def project(shift, x, gain, cosine, sine, parts, members, units):
    seqs, rows, width = x.shape
    count = len(parts)
    heads = sum(part[0].shape[1] for part in parts) // HEAD_DIM
    flat = [w for part in parts for w in part]
    return one_step(
        functools.partial(project_kernel, heads, units, members, count),
        "project",
        shift,
        [x, gain, cosine, sine, *flat],
        [
            jax.ShapeDtypeStruct((members, 3 * units, rows // 2, LANES), BF),
            jax.ShapeDtypeStruct((seqs, rows, width), BF),
        ],
    )


def gather_keys(inv_ref, w, kv_refs, kv_s, members, chunk):
    size = len(kv_refs)
    for block in range(2 * members):
        half = 0 if block < members else 1
        chip = inv_ref[block if half == 0 else 2 * members - 1 - block]
        for k, ref in enumerate(kv_refs):
            core = lax.rem(w + k, size)
            start = pl.multiple_of(block * size * chunk + core * chunk, chunk)
            kv_s[pl.ds(start, chunk), :] = ref[chip, half]


def gather_rows(inv_ref, read, put, members, to_high):
    for block in range(2 * members):
        half = 0 if block < members else 1
        chip = inv_ref[block if half == 0 else 2 * members - 1 - block]
        rows = read(chip).astype(F4)
        if (half == 1) != to_high:
            rows = pltpu.roll(rows, HEAD_DIM, 1)
        low = lane_of(rows.shape) < HEAD_DIM
        rows = jnp.where(low, 0.0, rows) if to_high else jnp.where(low, rows, 0.0)
        put(block, rows)


def attend_kernel(members, size, inv_ref, len_ref, w_ref, *refs):
    kv_refs = refs[:size]
    o_ref, of_ref, lse_ref = refs[size : size + 3]
    kv_s, vt_s, q_s, o_s, s_s = refs[size + 3 :]
    u = pl.program_id(0)
    chunk = kv_refs[0].shape[2]
    own_rows = q_s.shape[0]
    slot = kv_s.shape[0]
    w = w_ref[0]
    length = len_ref[u]
    gather_keys(inv_ref, w, kv_refs, kv_s, members, chunk)

    def put(block, rows):
        q_s[block * chunk : (block + 1) * chunk, :] = rows * HEAD_DIM ** (-0.5)

    gather_rows(inv_ref, lambda chip: kv_refs[0][chip, 2], put, members, False)

    def flip(i, carry):
        tile = kv_s[pl.ds(pl.multiple_of(i * TK, TK), TK), :].astype(F4)
        vt_s[i] = tile.T[HEAD_DIM:].astype(BF)
        return carry

    lax.fori_loop(0, slot // TK, flip, 0)
    span = TQ * size

    def row_tile(t, carry):
        row = pl.multiple_of(t * TQ, TQ)
        qt = q_s[pl.ds(row, TQ), :].T.astype(BF)
        index = lax.broadcasted_iota(jnp.int32, (1, TQ), 1)
        place = t * span + (index // chunk) * (size * chunk) + w * chunk + index % chunk
        limit = jnp.minimum(place, length - 1)

        def first_step(masked, kt, top):
            start = pl.multiple_of(kt * TK, TK)
            scores = dot(kv_s[pl.ds(start, TK), :], qt)
            if masked:
                keys = kt * TK + lax.broadcasted_iota(jnp.int32, (TK, 1), 0)
                scores = jnp.where(keys <= limit, scores, -1e30)
            s_s[kt] = scores
            return jnp.maximum(top, jnp.max(scores.reshape(TK // 8, 8, TQ), axis=0))

        def second_step(kt, state):
            total, acc = state
            weights = jnp.exp(s_s[kt] - top)
            total = total + jnp.sum(weights.reshape(TK // 8, 8, TQ), axis=0)
            return total, acc + dot(vt_s[kt], weights.astype(BF))

        clear = jnp.minimum(t * span, length) // TK
        last = jnp.minimum(pl.cdiv((t + 1) * span, TK), pl.cdiv(length, TK))
        top = jnp.full((8, TQ), -1e30, F4)
        top = lax.fori_loop(0, clear, functools.partial(first_step, False), top)
        top = lax.fori_loop(clear, last, functools.partial(first_step, True), top)
        top = jnp.max(top, axis=0, keepdims=True)
        state = (jnp.zeros((8, TQ), F4), jnp.zeros((HEAD_DIM, TQ), F4))
        total, acc = lax.fori_loop(0, last, second_step, state)
        total = jnp.sum(total, axis=0, keepdims=True)
        result = acc / total
        of_ref[0, t] = result
        lse_ref[0, t] = top + jnp.log(total)
        blank = jnp.zeros_like(result)
        first = 2 * t * TQ < own_rows
        both = jnp.concatenate(
            [jnp.where(first, result, blank), jnp.where(first, blank, result)], axis=0
        )
        o_s[pl.ds(row, TQ), :] = both.T
        return carry

    lax.fori_loop(0, own_rows // TQ, row_tile, 0)
    for b in range(members):
        other = 2 * members - 1 - b
        rows = (
            o_s[b * chunk : (b + 1) * chunk, :] + o_s[other * chunk : (other + 1) * chunk, :]
        )
        o_ref[inv_ref[b], 0] = rows.astype(BF)


def attend(inv, lengths, w, blocks, units):
    members, _, chunk, _ = blocks[0].shape
    size = len(blocks)
    slot = 2 * members * chunk * size
    rows = 2 * members * chunk
    spec = pl.BlockSpec((members, 3, chunk, LANES), lambda u, *_: (0, u, 0, 0))
    return pl.pallas_call(
        functools.partial(attend_kernel, members, size),
        grid_spec=pltpu.PrefetchScalarGridSpec(
            num_scalar_prefetch=3,
            grid=(units,),
            in_specs=[spec] * size,
            out_specs=[
                pl.BlockSpec((members, 1, chunk, LANES), lambda u, *_: (0, u, 0, 0)),
                pl.BlockSpec((1, rows // TQ, HEAD_DIM, TQ), lambda u, *_: (u, 0, 0, 0)),
                pl.BlockSpec((1, rows // TQ, 1, TQ), lambda u, *_: (u, 0, 0, 0)),
            ],
            scratch_shapes=[
                pltpu.VMEM((slot, LANES), BF),
                pltpu.VMEM((slot // TK, HEAD_DIM, TK), BF),
                pltpu.VMEM((rows, LANES), F4),
                pltpu.VMEM((rows, LANES), F4),
                pltpu.VMEM((slot // TK, TK, TQ), F4),
            ],
        ),
        out_shape=[
            jax.ShapeDtypeStruct((members, units, chunk, LANES), BF),
            jax.ShapeDtypeStruct((units, rows // TQ, HEAD_DIM, TQ), F4),
            jax.ShapeDtypeStruct((units, rows // TQ, 1, TQ), F4),
        ],
        compiler_params=params(1),
        name="attend",
    )(inv, lengths, w, *blocks)


def attend_back_kernel(members, size, inv_ref, len_ref, w_ref, *refs):
    kv_refs = refs[:size]
    do_ref, of_ref, lse_ref = refs[size : size + 3]
    dq_ref = refs[size + 3]
    dkv_refs = refs[size + 4 : 2 * size + 4]
    kv_s, kt_s, q_s, do_s, dq_s, dkv_s = refs[2 * size + 4 :]
    u = pl.program_id(0)
    chunk = kv_refs[0].shape[2]
    own_rows = q_s.shape[0]
    slot = kv_s.shape[0]
    w = w_ref[0]
    length = len_ref[u]
    gather_keys(inv_ref, w, kv_refs, kv_s, members, chunk)

    def put_q(block, rows):
        q_s[block * chunk : (block + 1) * chunk, :] = rows * HEAD_DIM ** (-0.5)

    def put_do(block, rows):
        do_s[block * chunk : (block + 1) * chunk, :] = rows

    gather_rows(inv_ref, lambda chip: kv_refs[0][chip, 2], put_q, members, False)
    gather_rows(inv_ref, lambda chip: do_ref[chip, 0], put_do, members, True)

    def flip(i, carry):
        tile = kv_s[pl.ds(pl.multiple_of(i * TK, TK), TK), :].astype(F4)
        kt_s[i] = tile.T[:HEAD_DIM].astype(BF)
        return carry

    lax.fori_loop(0, slot // TK, flip, 0)
    dkv_s[...] = jnp.zeros_like(dkv_s)
    dq_s[...] = jnp.zeros_like(dq_s)
    span = TQ * size

    def row_tile(t, carry):
        row = pl.multiple_of(t * TQ, TQ)
        q_rows = q_s[pl.ds(row, TQ), :]
        do_rows = do_s[pl.ds(row, TQ), :]
        qt, dot_ = q_rows.T, do_rows.T
        delta = jnp.sum(dot_[HEAD_DIM:] * of_ref[0, t], axis=0, keepdims=True)
        qt, dot_ = qt.astype(BF), dot_.astype(BF)
        stacked = jnp.concatenate([do_rows.astype(BF), q_rows.astype(BF)], axis=0)
        lse = lse_ref[0, t]
        index = lax.broadcasted_iota(jnp.int32, (1, TQ), 1)
        place = t * span + (index // chunk) * (size * chunk) + w * chunk + index % chunk
        limit = jnp.minimum(place, length - 1)

        def step(masked, kt, dqt):
            start = pl.multiple_of(kt * TK, TK)
            kv = kv_s[pl.ds(start, TK), :]
            weights = jnp.exp(dot(kv, qt) - lse)
            if masked:
                keys = kt * TK + lax.broadcasted_iota(jnp.int32, (TK, 1), 0)
                weights = jnp.where(keys <= limit, weights, 0.0)
            pulled = dot(kv, dot_)
            back = (weights * (pulled - delta)).astype(BF)
            dkv_s[pl.ds(start, TK), :] += dot(
                jnp.concatenate([weights.astype(BF), back], axis=1), stacked
            )
            return dqt + dot(kt_s[kt], back)

        clear = jnp.minimum(t * span, length) // TK
        last = jnp.minimum(pl.cdiv((t + 1) * span, TK), pl.cdiv(length, TK))
        dqt = jnp.zeros((HEAD_DIM, TQ), F4)
        dqt = lax.fori_loop(0, clear, functools.partial(step, False), dqt)
        dqt = lax.fori_loop(clear, last, functools.partial(step, True), dqt)
        dqt = dqt * HEAD_DIM ** (-0.5)
        blank = jnp.zeros_like(dqt)
        first = 2 * t * TQ < own_rows
        both = jnp.concatenate(
            [jnp.where(first, dqt, blank), jnp.where(first, blank, dqt)], axis=0
        )
        dq_s[pl.ds(row, TQ), :] = both.T
        return carry

    lax.fori_loop(0, jnp.minimum(pl.cdiv(length, span), own_rows // TQ), row_tile, 0)
    for b in range(members):
        other = 2 * members - 1 - b
        chip = inv_ref[b]
        rows = (
            dq_s[b * chunk : (b + 1) * chunk, :] + dq_s[other * chunk : (other + 1) * chunk, :]
        )
        dq_ref[chip, 0] = rows.astype(BF)
        for half, block in ((0, b), (1, other)):
            for k, ref in enumerate(dkv_refs):
                core = lax.rem(w + k, size)
                start = pl.multiple_of(block * size * chunk + core * chunk, chunk)
                ref[chip, half] = dkv_s[pl.ds(start, chunk), :].astype(ref.dtype)


def attend_back(inv, lengths, w, blocks, do_msg, kept, lse, units):
    members, _, chunk, _ = blocks[0].shape
    size = len(blocks)
    slot = 2 * members * chunk * size
    rows = 2 * members * chunk
    spec = pl.BlockSpec((members, 3, chunk, LANES), lambda u, *_: (0, u, 0, 0))
    one = pl.BlockSpec((members, 1, chunk, LANES), lambda u, *_: (0, u, 0, 0))
    two = pl.BlockSpec((members, 2, chunk, LANES), lambda u, *_: (0, u, 0, 0))
    return pl.pallas_call(
        functools.partial(attend_back_kernel, members, size),
        grid_spec=pltpu.PrefetchScalarGridSpec(
            num_scalar_prefetch=3,
            grid=(units,),
            in_specs=[spec] * size
            + [
                one,
                pl.BlockSpec((1, rows // TQ, HEAD_DIM, TQ), lambda u, *_: (u, 0, 0, 0)),
                pl.BlockSpec((1, rows // TQ, 1, TQ), lambda u, *_: (u, 0, 0, 0)),
            ],
            out_specs=[one] + [two] * size,
            scratch_shapes=[
                pltpu.VMEM((slot, LANES), BF),
                pltpu.VMEM((slot // TK, HEAD_DIM, TK), BF),
                pltpu.VMEM((rows, LANES), F4),
                pltpu.VMEM((rows, LANES), F4),
                pltpu.VMEM((rows, LANES), F4),
                pltpu.VMEM((slot, LANES), F4),
            ],
        ),
        out_shape=[jax.ShapeDtypeStruct((members, units, chunk, LANES), BF)]
        + [
            jax.ShapeDtypeStruct((members, 2 * units, chunk, LANES), BF if k else F4)
            for k in range(size)
        ],
        compiler_params=params(1),
        name="attend_back",
    )(inv, lengths, w, *blocks, do_msg, kept, lse)


def mix_kernel(heads, count, shift_ref, o_ref, x_ref, gain_ref, *refs):
    w_refs = refs[:count]
    mixed_ref, state_ref, a2_ref = refs[count:]
    members, _, chunk, _ = o_ref.shape
    seqs, rows, width = x_ref.shape
    for s in range(seqs):
        for g in range(heads // 2):
            pair = []
            for c in range(2):
                chip, u = head_units(seqs, heads, members, shift_ref[0], s, 2 * g + c)
                pair.append(o_ref[chip, u].astype(F4))
            early, late = pair_swap(*pair)
            part = slice(g * LANES, (g + 1) * LANES)
            mixed_ref[s, :chunk, part] = early.astype(BF)
            mixed_ref[s, chunk:, part] = late.astype(BF)
    inner = heads * HEAD_DIM // count
    made = 0.0
    for k in range(count):
        mixed = mixed_ref[:, :, k * inner : (k + 1) * inner].reshape(seqs * rows, inner)
        made = made + dot(mixed, w_refs[k][...])
    for s in range(seqs):
        state = x_ref[s].astype(F4) + made[s * rows : (s + 1) * rows]
        state_ref[s] = state
        scale = lax.rsqrt(jnp.mean(state * state, axis=-1, keepdims=True) + EPS)
        a2_ref[s] = (state * scale * gain_ref[...]).astype(BF)


def mix(shift, o_msg, x, gain, parts):
    seqs, rows, width = x.shape
    inner = sum(part.shape[0] for part in parts)
    return one_step(
        functools.partial(mix_kernel, inner // HEAD_DIM, len(parts)),
        "mix",
        shift,
        [o_msg, x, gain, *parts],
        [
            jax.ShapeDtypeStruct((seqs, rows, inner), BF),
            jax.ShapeDtypeStruct((seqs, rows, width), F4),
            jax.ShapeDtypeStruct((seqs, rows, width), BF),
        ],
    )


def norm_back(values, gain, upstream):
    scale = lax.rsqrt(jnp.mean(values * values, axis=-1, keepdims=True) + EPS)
    unit = values * scale
    pulled = upstream * gain
    result = scale * (pulled - unit * jnp.mean(pulled * unit, axis=-1, keepdims=True))
    return result, jnp.sum(upstream * unit, axis=0, keepdims=True)


def unrotate_kernel(heads, count, shift_ref, msg_ref, cos_ref, sin_ref, at_ref, *outs):
    dqkv_ref, *grad_refs = outs
    members, triple, chunk, _ = msg_ref.shape
    units = triple // 3
    seqs, rows, _ = dqkv_ref.shape
    cosine, sine = cos_ref[...], sin_ref[...]
    per = heads // count
    inner = per * HEAD_DIM

    def rope_back(grad):
        return grad * cosine - turn_halves(grad) * sine

    for k in list(range(1, count)) + [0]:
        for s in range(seqs):
            for g in range(per // 2):
                pair, asked = [], []
                for c in range(2):
                    chip, u = head_units(
                        seqs, heads, members, shift_ref[0], s, k * per + 2 * g + c
                    )
                    both = [msg_ref[chip, 2 * u], msg_ref[chip, 2 * u + 1]]
                    pair.append(jnp.concatenate(both, axis=0).astype(F4))
                    asked.append(msg_ref[chip, 2 * units + u].astype(F4))
                key, value = pair_swap(*pair)
                query = jnp.concatenate(pair_swap(*asked), axis=0)
                at = 3 * k * inner + g * LANES
                dqkv_ref[s, :, at : at + LANES] = rope_back(query).astype(BF)
                at = at + inner
                dqkv_ref[s, :, at : at + LANES] = rope_back(key).astype(BF)
                at = at + inner
                dqkv_ref[s, :, at : at + LANES] = value.astype(BF)
        cols = dqkv_ref[:, :, 3 * k * inner : 3 * (k + 1) * inner]
        made = dot(at_ref[...], cols.reshape(seqs * rows, 3 * inner))
        grad_refs[k][...] = made.astype(grad_refs[k].dtype)


def unrotate(shift, msg, cosine, sine, a1_turned, seqs, heads, count):
    rows = 2 * msg.shape[2]
    width = a1_turned.shape[0]
    inner = heads * HEAD_DIM
    return one_step(
        functools.partial(unrotate_kernel, heads, count),
        "unrotate",
        shift,
        [msg, cosine, sine, a1_turned],
        [jax.ShapeDtypeStruct((seqs, rows, 3 * inner), BF)]
        + [jax.ShapeDtypeStruct((width, 3 * inner // count), BF if k else F4) for k in range(count)],
    )


def unproject_kernel(count, shift_ref, dqkv_ref, x_ref, dstate_ref, gain_ref, *refs):
    w_refs = refs[:count]
    dx_ref, dgain_ref = refs[count:]
    seqs, rows, width = x_ref.shape
    inner = dqkv_ref.shape[2] // count
    made = 0.0
    for k in range(count):
        cols = dqkv_ref[:, :, k * inner : (k + 1) * inner].reshape(seqs * rows, inner)
        made = made + dot(cols, w_refs[k][...])
    total = jnp.zeros((1, width), F4)
    for s in range(seqs):
        pulled, dgain = norm_back(
            x_ref[s].astype(F4), gain_ref[...], made[s * rows : (s + 1) * rows]
        )
        total = total + dgain
        dx_ref[s] = (dstate_ref[s] + pulled).astype(BF)
    dgain_ref[...] = total


def unproject(shift, dqkv, x, dstate, gain, parts):
    seqs, rows, width = x.shape
    return one_step(
        functools.partial(unproject_kernel, len(parts)),
        "unproject",
        shift,
        [dqkv, x, dstate, gain, *parts],
        [
            jax.ShapeDtypeStruct((seqs, rows, width), BF),
            jax.ShapeDtypeStruct((1, width), F4),
        ],
    )


def two_gates(picked):
    top = jnp.maximum(*picked)
    raised = [jnp.exp(value - top) for value in picked]
    total = raised[0] + raised[1]
    return [value / total for value in raised]


def slot_hits(info_ref, count):
    shape = (count, info_ref.shape[1])
    ids = lax.broadcasted_iota(jnp.int32, shape, 0) + pl.program_id(0) * count
    return ids == info_ref[0:1, :], ids == info_ref[1:2, :]


def dispatch_kernel(info_ref, *refs):
    *second_refs, out_ref = refs
    count, held, width = out_ref.shape
    part = second_refs[0].shape[0]
    one, two = slot_hits(info_ref, count * held)
    hits = (one | two).astype(BF)
    routed = 0.0
    for k, ref in enumerate(second_refs):
        routed = routed + dot(hits[:, k * part : (k + 1) * part], ref[...])
    out_ref[...] = routed.astype(BF).reshape(count, held, width)


def dispatch_early_kernel(info_ref, cot_ref, out_ref):
    count, held, wide = out_ref.shape
    width = cot_ref.shape[1]
    one, two = slot_hits(info_ref, count * held)
    hits = (one | two).astype(BF)
    out_ref[:, :, :width] = dot(hits, cot_ref[...]).astype(BF).reshape(count, held, width)
    other = jnp.where(one, info_ref[3:4, :], 0) + jnp.where(two, info_ref[2:3, :], 0)
    other = jnp.sum(other.astype(F4), axis=1, keepdims=True)
    other = jnp.broadcast_to(other, (count * held, wide - width)).astype(BF)
    out_ref[:, :, width:] = other.reshape(count, held, wide - width)


def dispatch(kernel, info, arrays, wide, experts, held, name):
    count = 4 if experts % 4 == 0 else 1
    return pl.pallas_call(
        kernel,
        grid=(experts // count,),
        in_specs=[whole(array.shape) for array in (info, *arrays)],
        out_specs=pl.BlockSpec((count, held, wide), lambda e: (e, 0, 0)),
        out_shape=jax.ShapeDtypeStruct((experts, held, wide), BF),
        compiler_params=params(1),
        name=name,
    )(info, *arrays)


def two_gates(picked):
    top = jnp.maximum(*picked)
    raised = [jnp.exp(value - top) for value in picked]
    total = raised[0] + raised[1]
    return [value / total for value in raised]


def finish_kernel(
    heads, size, count, shift_ref, info_ref, second_ref, state_ref, cot_ref, gain_ref, *refs
):
    router_ref, turned_ref, *refs = refs
    home_refs, refs = refs[:size], refs[size:]
    dense_refs, refs = refs[:size], refs[size:]
    w_refs = refs[:count]
    out_ref, dstate_ref, low_ref, logit_ref, msg_ref, dgain_ref = refs[count:]
    step = pl.program_id(0)
    take, rows, width = state_ref.shape
    lines = take * rows
    members, units, chunk, _ = msg_ref.shape
    slots = home_refs[0].shape[0]
    experts = turned_ref.shape[0]
    info = info_ref[...].reshape(lines, info_ref.shape[2])
    target = info[:, : 2 * size]
    chosen = [info[:, 2 * size + c : 2 * size + c + 1] for c in range(2)]
    logits = dot(second_ref[...].reshape(lines, width), router_ref[...])[:, :experts]
    names = lax.broadcasted_iota(jnp.int32, (lines, experts), 1)
    gates = two_gates(
        [jnp.sum(jnp.where(names == pick, logits, 0.0), axis=1, keepdims=True) for pick in chosen]
    )
    ids = lax.broadcasted_iota(jnp.int32, (lines, slots), 1)
    made, back = [0.0, 0.0], 0.0
    for k in range(size):
        hits = [ids == target[:, 2 * k + c : 2 * k + c + 1] for c in range(2)]
        for c in range(2):
            made[c] = made[c] + dot(hits[c].astype(BF), home_refs[k][:, :width])
        back = back + dot((hits[0] | hits[1]).astype(BF), home_refs[k][:, width:])
    cot = cot_ref[...].reshape(lines, width).astype(F4)
    pulled = [jnp.sum(y * cot, axis=-1, keepdims=True) for y in made]
    middle = gates[0] * pulled[0] + gates[1] * pulled[1]
    logit = 0.0
    for c in range(2):
        logit = logit + jnp.where(names == chosen[c], gates[c] * (pulled[c] - middle), 0.0)
    logit = logit.astype(BF)
    logit_ref[...] = logit.reshape(take, rows, experts)
    back = back + dot(logit, turned_ref[...])
    branch = gates[0] * made[0] + gates[1] * made[1]
    for ref in dense_refs:
        dense = ref[...].reshape(lines, 2 * width)
        branch = branch + dense[:, :width]
        back = back + dense[:, width:]
    state = state_ref[...].reshape(lines, width)
    out_ref[...] = (state + branch).astype(BF).reshape(take, rows, width)
    pulled, dgain = norm_back(state, gain_ref[...], back)
    dstate = cot + pulled
    dstate_ref[...] = dstate.reshape(take, rows, width)
    low = dstate.astype(BF)
    low_ref[...] = low.reshape(take, rows, width)
    seqs = take * pl.num_programs(0)

    @pl.when(step == 0)
    def _():
        dgain_ref[...] = jnp.zeros_like(dgain_ref)
        if members * units > heads * seqs:
            msg_ref[...] = jnp.zeros_like(msg_ref)

    dgain_ref[...] += dgain
    per = heads // count
    for k in range(count):
        mixed_back = dot(low, w_refs[k][...])
        for s in range(take):
            for g in range(per // 2):
                part = mixed_back[s * rows : (s + 1) * rows, g * LANES : (g + 1) * LANES]
                pair = pair_swap(part[:chunk], part[chunk:])
                for c in range(2):
                    chip, u = head_units(
                        seqs, heads, members, shift_ref[0], step * take + s, k * per + 2 * g + c
                    )
                    msg_ref[chip, u] = pair[c].astype(BF)


def finish(shift, info, second, state, cot, gain, router, turned, homes, denses, parts, members, units):
    seqs, rows, width = state.shape
    inner = sum(part.shape[1] for part in parts)
    experts = turned.shape[0]
    take = max(1, min(seqs, 256 // rows))
    msg = (members, units, rows // 2, LANES)
    some = lambda cols: pl.BlockSpec((take, rows, cols), lambda s: (s, 0, 0))
    return pl.pallas_call(
        functools.partial(finish_kernel, inner // HEAD_DIM, len(homes), len(parts)),
        grid=(seqs // take,),
        in_specs=[SMEM, some(info.shape[2]), some(width), some(width), some(width)]
        + [whole((1, width)), whole(router.shape), whole(turned.shape)]
        + [whole(home.shape) for home in homes]
        + [some(2 * width)] * len(denses)
        + [whole(part.shape) for part in parts],
        out_specs=[some(width)] * 3 + [some(experts), whole(msg), whole((1, width))],
        out_shape=[
            jax.ShapeDtypeStruct((seqs, rows, width), BF),
            jax.ShapeDtypeStruct((seqs, rows, width), F4),
            jax.ShapeDtypeStruct((seqs, rows, width), BF),
            jax.ShapeDtypeStruct((seqs, rows, experts), BF),
            jax.ShapeDtypeStruct(msg, BF),
            jax.ShapeDtypeStruct((1, width), F4),
        ],
        compiler_params=params(1),
        name="finish",
    )(shift, info, second, state, cot, gain, router, turned, *homes, *denses, *parts)


def place_kernel(copies, cuts, *refs):
    whole_refs = refs[cuts * copies :]
    blocks = []
    for n in range(cuts):
        total = refs[n * copies][...].astype(F4)
        for ref in refs[n * copies + 1 : (n + 1) * copies]:
            total = total + ref[...].astype(F4)
        blocks.append(total)
    total = jnp.concatenate(blocks, axis=-1)
    for n, out in enumerate(whole_refs):
        out[...] = untile(total, n)


def place(blocks, experts):
    members, rows, _ = blocks[0].shape
    hidden = sum(block.shape[2] for block in blocks) // 3
    copies = members // experts
    take = 2 if experts % 2 == 0 else 1
    return pl.pallas_call(
        functools.partial(place_kernel, copies, len(blocks)),
        grid=(experts // take,),
        in_specs=[
            pl.BlockSpec(
                (take, rows, block.shape[2]), lambda e, n=n: (n * experts // take + e, 0, 0)
            )
            for block in blocks
            for n in range(copies)
        ],
        out_specs=[pl.BlockSpec((take, rows, hidden), lambda e: (e, 0, 0))] * 3,
        out_shape=[jax.ShapeDtypeStruct((experts, rows, hidden), F4)] * 3,
        compiler_params=params(1),
        name="place",
    )(*[block for block in blocks for n in range(copies)])


def gated_kernel(count, tiles, routed, *refs):
    if routed:
        expert_ref, router_ref, early_ref, x_ref, *refs = refs
        d_ref = refs[3 * count]
    else:
        d_ref, x_ref, *refs = refs
    w_refs, (out_ref, hid_ref, acc_ref) = refs[: 3 * count], refs[-3:]
    step = pl.program_id(0)
    rows, width = x_ref.shape
    tile = hid_ref.shape[1] // 3
    take = min(256, rows)

    @pl.when(step == 0)
    def _():
        acc_ref[...] = jnp.zeros_like(acc_ref)
        if routed:
            logits = dot(x_ref[...], router_ref[...])
            names = lane_of(logits.shape)
            other = early_ref[:, width : width + 1].astype(F4).astype(jnp.int32)
            picked = [
                jnp.sum(jnp.where(names == name, logits, 0.0), axis=1, keepdims=True)
                for name in (expert_ref[0], other)
            ]
            gate = two_gates(picked)[0]
            d_ref[...] = (early_ref[:, :width].astype(F4) * gate).astype(BF)

    for k in range(count):

        @pl.when(step // tiles == k)
        def _(k=k):
            gate_w, up_w, down_w = w_refs[3 * k : 3 * k + 3]
            gate_t, up_t, down_t = gate_w[...].T, up_w[...].T, down_w[...].T
            for r in range(0, rows, take):
                mine = slice(r, r + take)
                x, d = x_ref[mine, :], d_ref[mine, :]
                gate, up, back = dot(x, gate_w[...]), dot(x, up_w[...]), dot(d, down_t)
                share = 1.0 / (1.0 + jnp.exp(-gate))
                silu = gate * share
                hidden = (silu * up).astype(BF)
                dup = (back * silu).astype(BF)
                dgate = (back * up * (share * (1.0 + gate * (1.0 - share)))).astype(BF)
                hid_ref[mine, :tile] = dgate
                hid_ref[mine, tile : 2 * tile] = dup
                hid_ref[mine, 2 * tile :] = hidden
                acc_ref[mine, :width] += dot(hidden, down_w[...])
                acc_ref[mine, width:] += dot(dgate, gate_t) + dot(dup, up_t)

    @pl.when(step == pl.num_programs(0) - 1)
    def _():
        out_ref[...] = acc_ref[...].astype(out_ref.dtype)


def tile_of(hidden):
    return min(512, hidden)


def gated(x, d, parts, kind, name, routed=()):
    rows = x.shape[0]
    width, hidden = parts[0][0].shape
    tile = tile_of(hidden)
    tiles = hidden // tile
    count = len(parts)
    flat, specs = [], []
    for k, part in enumerate(parts):
        at = lambda f, k=k: jnp.clip(f - k * tiles, 0, tiles - 1)
        cols = pl.BlockSpec((width, tile), lambda f, at=at: (0, at(f)))
        lines = pl.BlockSpec((tile, width), lambda f, at=at: (at(f), 0))
        flat += list(part)
        specs += [cols, cols, lines]
    ahead = [SMEM, whole(routed[1].shape)] if routed else []
    gated_out = [(whole((rows, width)), jax.ShapeDtypeStruct((rows, width), BF))] if routed else []
    return pl.pallas_call(
        functools.partial(gated_kernel, count, tiles, bool(routed)),
        grid=(count * tiles,),
        in_specs=ahead + [whole(d.shape), whole(x.shape)] + specs,
        out_specs=[spec for spec, _ in gated_out]
        + [whole((rows, 2 * width)), pl.BlockSpec((rows, 3 * tile), lambda f: (0, f))],
        out_shape=[shape for _, shape in gated_out]
        + [
            jax.ShapeDtypeStruct((rows, 2 * width), kind),
            jax.ShapeDtypeStruct((rows, 3 * count * hidden), BF),
        ],
        scratch_shapes=[pltpu.VMEM((rows, 2 * width), F4)],
        compiler_params=params(1),
        name=name,
    )(*routed, d, x, *flat)


def gated_grads_kernel(x_ref, d_ref, hid_ref, out_ref, xt_ref, dt_ref):
    tile = hid_ref.shape[1] // 3

    @pl.when(pl.program_id(0) == 0)
    def _():
        xt_ref[...] = x_ref[...].T
        dt_ref[...] = d_ref[...].T

    out_ref[:, : 2 * tile] = dot(xt_ref[...], hid_ref[:, : 2 * tile]).astype(BF)
    out_ref[:, 2 * tile :] = dot(dt_ref[...], hid_ref[:, 2 * tile :]).astype(BF)


def gated_grads(x, d, hid, k, count, name):
    rows, width = x.shape
    hidden = hid.shape[1] // 3 // count
    tile = tile_of(hidden)
    tiles = hidden // tile
    return pl.pallas_call(
        gated_grads_kernel,
        grid=(tiles,),
        in_specs=[
            whole(x.shape),
            whole(d.shape),
            pl.BlockSpec((rows, 3 * tile), lambda f: (0, k * tiles + f)),
        ],
        out_specs=pl.BlockSpec((width, 3 * tile), lambda f: (0, f)),
        out_shape=jax.ShapeDtypeStruct((width, 3 * hidden), BF),
        scratch_shapes=[pltpu.VMEM((width, rows), BF)] * 2,
        compiler_params=params(1),
        cost_estimate=pl.CostEstimate(
            flops=6 * rows * width * hidden,
            bytes_accessed=2 * (2 * rows * width + 3 * hidden * (rows + width)),
            transcendentals=0,
        ),
        name=name,
    )(x, d, hid)


def untile(array, n):
    hidden = array.shape[-1] // 3
    tile = tile_of(hidden)
    parts = [
        array[..., (3 * j + n) * tile : (3 * j + n + 1) * tile] for j in range(hidden // tile)
    ]
    return jnp.concatenate(parts, axis=-1)


def per_device(
    inputs,
    cotangent,
    lengths,
    block_pairs,
    routes,
    attn_gain,
    query_weight,
    key_weight,
    value_weight,
    out_weight,
    ffn_gain,
    router_weight,
    expert_gate,
    expert_up,
    expert_down,
    dense_gate,
    dense_up,
    dense_down,
):
    pair_rows, seqs, width = inputs.shape[1:]
    members, size = lax.axis_size("ctx"), lax.axis_size("wt")
    ctx, w = lax.axis_index("ctx"), lax.axis_index("wt")
    experts = expert_gate.shape[0]
    block = pair_rows // 2
    chunk = block // size
    rows = 2 * chunk * seqs
    inner = query_weight.shape[1] * size
    heads = inner // HEAD_DIM
    units = -(-(seqs * heads) // members)

    def rows_of(array, k):
        parted = array.reshape(2, size, chunk, seqs, -1)
        mine = lax.dynamic_index_in_dim(parted, (w + k) % size, 1, False)
        return mine.transpose(2, 0, 1, 3).reshape(seqs, 2 * chunk, -1)

    def places_of(k):
        pair = lax.dynamic_index_in_dim(block_pairs, ctx, 0, False)
        blocks = jnp.stack([pair, 2 * members - 1 - pair])
        core = (w + k) % size
        return (blocks[:, None] * block + core * chunk + jnp.arange(chunk)[None, :]).reshape(-1)

    x = rows_of(inputs[0], 0)
    half = HEAD_DIM // 2
    freqs = THETA ** (-jnp.arange(half, dtype=F4) / half)
    angles = places_of(0).astype(F4)[:, None] * freqs[None, :]
    cosine = jnp.tile(jnp.cos(angles), (1, LANES // half))
    sine = jnp.tile(
        jnp.concatenate([-jnp.sin(angles), jnp.sin(angles)], axis=1), (1, LANES // HEAD_DIM)
    )

    local = inner // size
    split = size == 2 and local % LANES == 0
    shift = (w * (heads // size) if split else jnp.zeros_like(w)).astype(jnp.int32)[None]
    own_qkv = [query_weight, key_weight, value_weight]
    if split:
        parts = list(zip(*[wt_gather(weight) for weight in own_qkv]))
        out_parts = wt_gather(out_weight)
    else:
        parts = [[lax.all_gather(weight, "wt", axis=1, tiled=True) for weight in own_qkv]]
        out_parts = [lax.all_gather(out_weight, "wt", axis=0, tiled=True)]
    msg, a1 = project(shift, x, attn_gain[None], cosine, sine, parts, members, units)
    got = lax.all_to_all(msg, "ctx", 0, 0, tiled=True)

    near = 4 if members % 4 == 0 else 1
    outer = members // near
    near_groups = [[o * near + i for i in range(near)] for o in range(outer)]
    far_groups = [[o * near + i for o in range(outer)] for i in range(near)]

    def by_steps(array):
        array = array.reshape(outer, near, width // members, -1).swapaxes(0, 1)
        return array.reshape(width, -1)

    def near_scatter(array):
        return lax.psum_scatter(
            array, "ctx", scatter_dimension=0, tiled=True, axis_index_groups=near_groups
        )

    def far_scatter(array):
        return lax.psum_scatter(
            array, "ctx", scatter_dimension=0, tiled=True, axis_index_groups=far_groups
        )

    a1_turned = by_steps(a1.reshape(rows, width).T)
    back_parts = [jnp.concatenate([weight.T for weight in part]) for part in parts]
    out_back = [part.T for part in out_parts]
    expert = ctx % experts
    expert_parts = list(
        zip(
            *[
                wt_gather(lax.dynamic_index_in_dim(weights, expert, 0, False))
                for weights in (expert_gate, expert_up, expert_down)
            ]
        )
    )
    total_rows = rows * size
    cots = []
    for k in range(size):
        valid = places_of(k)[None, :] < lengths[:, None]
        cots.append(
            jnp.where(valid[:, :, None], rows_of(cotangent[0], k), jnp.zeros((), BF)).reshape(
                rows, width
            )
        )
    cot = jnp.concatenate(cots)

    parted = routes[0].reshape(2, size, chunk, seqs, 2).transpose(1, 3, 0, 2, 4)
    chosen_all = parted.reshape(total_rows, 2)
    names = jnp.arange(experts, dtype=jnp.int32)
    picks_all = chosen_all[:, :, None] == names
    marks = jnp.any(picks_all, axis=1).astype(BF)
    index = jnp.arange(total_rows)
    before = dot((index[None, :] < index[:, None]).astype(BF), marks)
    order_all = jnp.sum(jnp.where(picks_all, before[:, None, :], 0.0), axis=-1).astype(jnp.int32)
    share = -(-CAPACITY // size)
    held = -(-share // 16) * 16

    def targets(chosen, order, core):
        inside = (order >= core * held) & (order < (core + 1) * held)
        return jnp.where(inside, chosen * held + order - core * held, -1)

    def own_first(array):
        pieces = array.reshape(size, rows, 2)
        pieces = jnp.concatenate([pieces, pieces[:-1]])
        return lax.dynamic_slice_in_dim(pieces, w, size, 0).reshape(total_rows, 2)

    chosen, order_here = own_first(chosen_all), own_first(order_all)
    target = targets(chosen, order_here, w)
    own_targets = [
        targets(chosen[:rows], order_here[:rows], (w + k) % size) for k in range(size)
    ]
    own_info = jnp.concatenate(own_targets + [chosen[:rows]], axis=1)
    own_info = own_info.reshape(seqs, 2 * chunk, -1)
    info = jnp.concatenate([target, chosen, jnp.zeros((total_rows, 4), jnp.int32)], axis=1).T
    router_wide = jnp.pad(router_weight, ((0, 0), (0, LANES - experts)))
    router_turned = router_weight.T
    inv = jnp.argsort(block_pairs).astype(jnp.int32)
    unit_slots = jnp.minimum((ctx + members * jnp.arange(units)) // heads, seqs - 1)
    unit_lengths = lengths[unit_slots]
    w_arg = w.astype(jnp.int32)[None]
    groups = None
    if members != experts:
        groups = [[g * experts + e for e in range(experts)] for g in range(members // experts)]
    swap = functools.partial(
        lax.all_to_all,
        axis_name="ctx",
        split_axis=0,
        concat_axis=0,
        axis_index_groups=groups,
        tiled=True,
    )

    early = dispatch(
        dispatch_early_kernel, info, [cot], width + LANES, experts, held, "dispatch_early"
    )
    (
        got,
        early,
        a1_turned,
        back_parts,
        out_back,
        expert_parts,
        cots,
        cot,
        own_info,
        info,
        router_wide,
        router_turned,
        inv,
        unit_lengths,
    ) = (
        lax.optimization_barrier(
            (
                got,
                early,
                a1_turned,
                back_parts,
                out_back,
                expert_parts,
                cots,
                cot,
                own_info,
                info,
                router_wide,
                router_turned,
                inv,
                unit_lengths,
            )
        )
    )

    blocks = wt_gather(got)
    early = swap(early)
    o_msg, kept, lse = attend(inv, unit_lengths, w_arg, blocks, units)
    o_msg, early = lax.optimization_barrier((o_msg, early))
    o_got = lax.all_to_all(o_msg, "ctx", 0, 0, tiled=True)
    mixed, state, second_own = mix(shift, o_got, x, ffn_gain[None], out_parts)

    seconds = wt_gather(second_own.reshape(rows, width))
    sent = dispatch(dispatch_kernel, info, seconds, width, experts, held, "dispatch")

    sent, seconds = lax.optimization_barrier((sent, seconds))
    second = jnp.concatenate(seconds)
    arrived = swap(sent)
    dense, dense_hid = gated(second, cot, [[dense_gate, dense_up, dense_down]], F4, "dense_branch")
    dense_grads = gated_grads(second, cot, dense_hid, 0, 1, "dense_grads")
    dense_grads = by_steps(dense_grads)
    denses = [dense[:rows]]
    for k in range(1, size):
        perm = [(i, (i + k) % size) for i in range(size)]
        denses.append(lax.ppermute(dense[k * rows : (k + 1) * rows], "wt", perm))
    arrived, denses, dense_grads = lax.optimization_barrier((arrived, denses, dense_grads))
    dense_near = near_scatter(dense_grads)

    arrived = arrived.reshape(experts * held, width)
    dye, returned, hid = gated(
        arrived,
        early.reshape(experts * held, -1),
        expert_parts,
        BF,
        "expert_branch",
        (expert.astype(jnp.int32)[None], router_wide),
    )
    home = swap(returned.reshape(experts, held, 2 * width))
    hidden = expert_gate.shape[2]
    expert_sum = None
    for k in list(range(1, size)) + [0]:
        made = gated_grads(arrived, dye, hid, k, size, "expert_grads")
        if k:
            made = lax.ppermute(made, "wt", [(i, (i + k) % size) for i in range(size)])
        expert_sum = made.astype(F4) if expert_sum is None else expert_sum + made.astype(F4)
    expert_sum = expert_sum.astype(BF).reshape(members, width // members, 3 * hidden)
    cut = 3 * hidden // 2
    expert_sum = [expert_sum[:, :, :cut], expert_sum[:, :, cut:]]
    home, expert_sum, dense_near = lax.optimization_barrier((home, expert_sum, dense_near))
    dense_sum = far_scatter(dense_near)
    homes = wt_gather(home.reshape(experts * held, 2 * width))

    own_cot = cots[0].reshape(seqs, 2 * chunk, width)
    denses = [part.reshape(seqs, 2 * chunk, 2 * width) for part in denses]
    output, dstate, dstate_low, logit_back, do_msg, ffn_grad = finish(
        shift,
        own_info,
        second_own,
        state,
        own_cot,
        ffn_gain[None],
        router_wide,
        router_turned,
        homes,
        denses,
        out_back,
        members,
        units,
    )
    do_got = lax.all_to_all(do_msg, "ctx", 0, 0, tiled=True)

    def share_of(array, kinds, k):
        if split:
            return array[..., k * kinds * local : (k + 1) * kinds * local].reshape(rows, -1)
        cols = array.reshape(rows, kinds, size, local)
        return lax.dynamic_index_in_dim(cols, (w + k) % size, 2, False).reshape(rows, -1)

    def split_wt(left, right, kinds):
        pieces = []
        for k in range(size):
            made = dot_tn(left.reshape(rows, -1), share_of(right, kinds, k))
            pieces.append(made if k == 0 else made.astype(BF))
        return wt_scatter(pieces).astype(BF)

    router_grad = dot_tn(second_own.reshape(rows, width), logit_back.reshape(rows, experts))
    small = wt_sum(jnp.concatenate([ffn_grad.T, router_grad], axis=1))
    small_high = small.astype(BF)
    small_low = (small - small_high.astype(F4)).astype(BF)
    few = experts + 1
    blank = jnp.zeros((width, -(2 * few) % LANES), BF)
    out_msg = [split_wt(dstate_low, mixed, 1), small_high, small_low, blank]
    out_msg = by_steps(jnp.concatenate(out_msg, axis=1))
    do_got, out_msg, output, dense_sum, expert_sum = lax.optimization_barrier(
        (do_got, out_msg, output, dense_sum, expert_sum)
    )
    expert_got = [lax.all_to_all(expert_sum[0], "ctx", 0, 0, tiled=True)]
    out_near = near_scatter(out_msg)
    dq, *dkv = attend_back(inv, unit_lengths, w_arg, blocks, do_got, kept, lse, units)
    dq, dkv, expert_got, out_near = lax.optimization_barrier((dq, dkv, expert_got, out_near))
    out_sum = far_scatter(out_near)
    dkv = wt_scatter(dkv).astype(BF)
    grad_msg = jnp.concatenate([dkv, dq], axis=1)
    grad_got = lax.all_to_all(grad_msg, "ctx", 0, 0, tiled=True)
    grad_got, out_sum, expert_sum = lax.optimization_barrier((grad_got, out_sum, expert_sum))
    expert_got.append(lax.all_to_all(expert_sum[1], "ctx", 0, 0, tiled=True))
    dqkv, *pieces = unrotate(shift, grad_got, cosine, sine, a1_turned, seqs, heads, len(parts))
    if split:
        last_msg = wt_scatter(pieces).astype(BF)
    else:
        last_msg = by_steps(split_wt(a1, dqkv, 3))
    last_sum = far_scatter(near_scatter(last_msg))
    dqkv, last_msg = lax.optimization_barrier((dqkv, last_msg))
    dx, attn_grad = unproject(shift, dqkv, x, dstate, attn_gain[None], back_parts)
    attn_grad = ctx_sum(wt_sum(attn_grad)).reshape(members, -1)
    attn_grad = lax.dynamic_index_in_dim(attn_grad, ctx, 0, False)
    expert_grads = place(expert_got, experts)
    last_sum = last_sum.astype(F4)
    out_sum = out_sum.astype(F4)
    tail = out_sum[:, local:]
    tail = tail[:, :few] + tail[:, few : 2 * few]

    def to_tokens(own):
        array = in_order(wt_gather(own)).reshape(size, seqs, 2, chunk, width)
        return array.transpose(2, 0, 3, 1, 4).reshape(inputs.shape)

    return (
        to_tokens(output),
        to_tokens(dx),
        attn_grad,
        *[last_sum[:, n * local : (n + 1) * local] for n in range(3)],
        out_sum[:, :local].T,
        tail[:, 0],
        tail[:, 1:],
        *expert_grads[:2],
        expert_grads[2].transpose(0, 2, 1),
        *[untile(dense_sum, n).astype(F4) for n in range(2)],
        untile(dense_sum, 2).astype(F4).T,
    )


def solution(mesh):
    placed = (
        P("ctx", None, None, None),
        P("ctx", None, None, None),
        P(),
        P(),
        P("ctx", None, None, None),
        P(),
        P(None, "wt"),
        P(None, "wt"),
        P(None, "wt"),
        P("wt", None),
        P(),
        P(),
        P(None, None, "wt"),
        P(None, None, "wt"),
        P(None, "wt", None),
        P(None, "wt"),
        P(None, "wt"),
        P("wt", None),
    )
    return jax.shard_map(
        per_device,
        mesh=mesh,
        in_specs=placed,
        out_specs=(
            P("ctx", None, None, None),
            P("ctx", None, None, None),
            P("ctx"),
            P("ctx", "wt"),
            P("ctx", "wt"),
            P("ctx", "wt"),
            P("wt", "ctx"),
            P("ctx"),
            P("ctx", None),
            P(None, "ctx", "wt"),
            P(None, "ctx", "wt"),
            P(None, "wt", "ctx"),
            P("ctx", "wt"),
            P("ctx", "wt"),
            P("wt", "ctx"),
        ),
        check_vma=False,
    )
```

```python
import functools

import jax
import jax.numpy as jnp
from jax import lax
from jax.experimental import pallas as pl
from jax.experimental.pallas import tpu as pltpu
from jax.sharding import PartitionSpec as P

HEAD_DIM = 64
CAPACITY = 160
EPS = 1e-06
THETA = 10000.0
LANES = 128
BF = jnp.bfloat16
F4 = jnp.float32
TQ = 512
TK = 1024
VMEM_LIMIT = 56 * 1024 * 1024


def dot(a, b):
    return jnp.dot(a, b, preferred_element_type=F4)


def dot_nt(a, b):
    return lax.dot_general(a, b, (((1,), (1,)), ((), ())), preferred_element_type=F4)


def dot_tn(a, b):
    return lax.dot_general(a, b, (((0,), (0,)), ((), ())), preferred_element_type=F4)


def wt_gather(x):
    size = lax.axis_size("wt")
    return [x] + [
        lax.ppermute(x, "wt", [(i, (i - k) % size) for i in range(size)]) for k in range(1, size)
    ]


def wt_scatter(pieces):
    size = lax.axis_size("wt")
    total = pieces[0]
    for k in range(1, size):
        moved = lax.ppermute(pieces[k], "wt", [(i, (i + k) % size) for i in range(size)])
        total = total + moved.astype(total.dtype)
    return total


def wt_sum(x):
    if lax.axis_size("wt") == 2:
        return x + lax.ppermute(x, "wt", [(0, 1), (1, 0)])
    return lax.psum(x, "wt")


def ctx_sum(x):
    size = lax.axis_size("ctx")
    if size & (size - 1):
        return lax.psum(x, "ctx")
    by = 1
    while by < size:
        x = x + lax.ppermute(x, "ctx", [(i, i ^ by) for i in range(size)])
        by *= 2
    return x


def in_order(parts):
    size = len(parts)
    start = (size - lax.axis_index("wt")) % size
    return lax.dynamic_slice_in_dim(jnp.stack(parts + parts[:-1]), start, size, 0)


def lane_of(shape):
    return lax.broadcasted_iota(jnp.int32, shape, len(shape) - 1)


def pair_swap(a, b):
    low = lane_of(a.shape) < HEAD_DIM
    return (
        jnp.where(low, a, pltpu.roll(b, HEAD_DIM, 1)),
        jnp.where(low, pltpu.roll(a, HEAD_DIM, 1), b),
    )


def turn_halves(t):
    first = lane_of(t.shape) % HEAD_DIM < HEAD_DIM // 2
    return jnp.where(
        first,
        pltpu.roll(t, LANES - HEAD_DIM // 2, 1),
        pltpu.roll(t, HEAD_DIM // 2, 1),
    )


def params(count):
    return pltpu.CompilerParams(
        vmem_limit_bytes=VMEM_LIMIT, dimension_semantics=("arbitrary",) * count
    )


def whole(shape):
    return pl.BlockSpec(shape, lambda *i: (0,) * len(shape))


def head_units(seqs, heads, members, shift, s, rel):
    unit = s * heads + lax.rem(rel + shift, heads)
    return lax.rem(unit, members), lax.div(unit, members)


def project_kernel(heads, units, members, count, shift_ref, x_ref, gain_ref, cos_ref, sin_ref, *refs):
    w_refs = refs[: 3 * count]
    msg_ref, a1_ref = refs[3 * count :]
    seqs, rows, width = x_ref.shape
    chunk = rows // 2
    for s in range(seqs):
        x = x_ref[s].astype(F4)
        scale = lax.rsqrt(jnp.mean(x * x, axis=-1, keepdims=True) + EPS)
        a1_ref[s] = (x * scale * gain_ref[...]).astype(BF)
    if units * members > heads * seqs:
        msg_ref[...] = jnp.zeros_like(msg_ref)
    a1 = a1_ref[...].reshape(seqs * rows, width)
    cosine, sine = cos_ref[...], sin_ref[...]

    def rope(t):
        return t * cosine + turn_halves(t) * sine

    per = heads // count
    for k in range(count):
        query, key, value = (dot(a1, ref[...]) for ref in w_refs[3 * k : 3 * k + 3])
        for s in range(seqs):
            mine = slice(s * rows, (s + 1) * rows)
            for g in range(per // 2):
                part = slice(g * LANES, (g + 1) * LANES)
                pairs = pair_swap(rope(key[mine, part]), value[mine, part])
                turned = rope(query[mine, part])
                asked = pair_swap(turned[:chunk], turned[chunk:])
                for c in range(2):
                    chip, u = head_units(
                        seqs, heads, members, shift_ref[0], s, k * per + 2 * g + c
                    )
                    msg_ref[chip, 3 * u] = pairs[c][:chunk].astype(BF)
                    msg_ref[chip, 3 * u + 1] = pairs[c][chunk:].astype(BF)
                    msg_ref[chip, 3 * u + 2] = asked[c].astype(BF)


SMEM = pl.BlockSpec(memory_space=pltpu.SMEM)


def one_step(kernel, name, shift, arrays, shapes):
    return pl.pallas_call(
        kernel,
        grid=(1,),
        in_specs=[SMEM] + [whole(array.shape) for array in arrays],
        out_specs=[whole(shape.shape) for shape in shapes],
        out_shape=shapes,
        compiler_params=params(1),
        name=name,
    )(shift, *arrays)


def project(shift, x, gain, cosine, sine, parts, members, units):
    seqs, rows, width = x.shape
    count = len(parts)
    heads = sum(part[0].shape[1] for part in parts) // HEAD_DIM
    flat = [w for part in parts for w in part]
    return one_step(
        functools.partial(project_kernel, heads, units, members, count),
        "project",
        shift,
        [x, gain, cosine, sine, *flat],
        [
            jax.ShapeDtypeStruct((members, 3 * units, rows // 2, LANES), BF),
            jax.ShapeDtypeStruct((seqs, rows, width), BF),
        ],
    )


def turn_kernel(count, shift_ref, *refs):
    (a1_ref, *ins), (a1t_ref, *outs) = refs[: 1 + 4 * count], refs[1 + 4 * count :]
    a1t_ref[...] = a1_ref[...].T
    for k in range(count):
        inner = ins[4 * k].shape[1]
        for n in range(3):
            outs[2 * k][n * inner : (n + 1) * inner, :] = ins[4 * k + n][...].T
        outs[2 * k + 1][...] = ins[4 * k + 3][...].T


def turn(a1, parts, out_parts):
    rows, width = a1.shape
    ins = [a1]
    shapes = [jax.ShapeDtypeStruct((width, rows), BF)]
    for part, out_part in zip(parts, out_parts):
        ins += [*part, out_part]
        inner = out_part.shape[0]
        shapes += [
            jax.ShapeDtypeStruct((3 * inner, width), BF),
            jax.ShapeDtypeStruct((width, inner), BF),
        ]
    made = one_step(
        functools.partial(turn_kernel, len(parts)), "turn", jnp.zeros((1,), jnp.int32), ins, shapes
    )
    return made[0], list(made[1::2]), list(made[2::2])


def gather_keys(inv_ref, w, kv_refs, kv_s, members, chunk):
    size = len(kv_refs)
    for block in range(2 * members):
        half = 0 if block < members else 1
        chip = inv_ref[block if half == 0 else 2 * members - 1 - block]
        for k, ref in enumerate(kv_refs):
            core = lax.rem(w + k, size)
            start = pl.multiple_of(block * size * chunk + core * chunk, chunk)
            kv_s[pl.ds(start, chunk), :] = ref[chip, half]


def gather_rows(inv_ref, read, put, members, to_high):
    for block in range(2 * members):
        half = 0 if block < members else 1
        chip = inv_ref[block if half == 0 else 2 * members - 1 - block]
        rows = read(chip).astype(F4)
        if (half == 1) != to_high:
            rows = pltpu.roll(rows, HEAD_DIM, 1)
        low = lane_of(rows.shape) < HEAD_DIM
        rows = jnp.where(low, 0.0, rows) if to_high else jnp.where(low, rows, 0.0)
        put(block, rows)


def attend_kernel(members, size, inv_ref, len_ref, w_ref, *refs):
    kv_refs = refs[:size]
    o_ref, of_ref, lse_ref = refs[size : size + 3]
    kv_s, vt_s, q_s, o_s, s_s = refs[size + 3 :]
    u = pl.program_id(0)
    chunk = kv_refs[0].shape[2]
    own_rows = q_s.shape[0]
    slot = kv_s.shape[0]
    w = w_ref[0]
    length = len_ref[u]
    gather_keys(inv_ref, w, kv_refs, kv_s, members, chunk)

    def put(block, rows):
        q_s[block * chunk : (block + 1) * chunk, :] = rows * HEAD_DIM ** (-0.5)

    gather_rows(inv_ref, lambda chip: kv_refs[0][chip, 2], put, members, False)

    def flip(i, carry):
        tile = kv_s[pl.ds(pl.multiple_of(i * TK, TK), TK), :].astype(F4)
        vt_s[i] = tile.T[HEAD_DIM:].astype(BF)
        return carry

    lax.fori_loop(0, slot // TK, flip, 0)
    span = TQ * size

    def row_tile(t, carry):
        row = pl.multiple_of(t * TQ, TQ)
        qt = q_s[pl.ds(row, TQ), :].T.astype(BF)
        index = lax.broadcasted_iota(jnp.int32, (1, TQ), 1)
        place = t * span + (index // chunk) * (size * chunk) + w * chunk + index % chunk
        limit = jnp.minimum(place, length - 1)

        def first_step(masked, kt, top):
            start = pl.multiple_of(kt * TK, TK)
            scores = dot(kv_s[pl.ds(start, TK), :], qt)
            if masked:
                keys = kt * TK + lax.broadcasted_iota(jnp.int32, (TK, 1), 0)
                scores = jnp.where(keys <= limit, scores, -1e30)
            s_s[kt] = scores
            return jnp.maximum(top, jnp.max(scores.reshape(TK // 8, 8, TQ), axis=0))

        def second_step(kt, state):
            total, acc = state
            weights = jnp.exp(s_s[kt] - top)
            total = total + jnp.sum(weights.reshape(TK // 8, 8, TQ), axis=0)
            return total, acc + dot(vt_s[kt], weights.astype(BF))

        clear = jnp.minimum(t * span, length) // TK
        last = jnp.minimum(pl.cdiv((t + 1) * span, TK), pl.cdiv(length, TK))
        top = jnp.full((8, TQ), -1e30, F4)
        top = lax.fori_loop(0, clear, functools.partial(first_step, False), top)
        top = lax.fori_loop(clear, last, functools.partial(first_step, True), top)
        top = jnp.max(top, axis=0, keepdims=True)
        state = (jnp.zeros((8, TQ), F4), jnp.zeros((HEAD_DIM, TQ), F4))
        total, acc = lax.fori_loop(0, last, second_step, state)
        total = jnp.sum(total, axis=0, keepdims=True)
        result = acc / total
        of_ref[0, t] = result
        lse_ref[0, t] = top + jnp.log(total)
        blank = jnp.zeros_like(result)
        first = 2 * t * TQ < own_rows
        both = jnp.concatenate(
            [jnp.where(first, result, blank), jnp.where(first, blank, result)], axis=0
        )
        o_s[pl.ds(row, TQ), :] = both.T
        return carry

    lax.fori_loop(0, own_rows // TQ, row_tile, 0)
    for b in range(members):
        other = 2 * members - 1 - b
        rows = (
            o_s[b * chunk : (b + 1) * chunk, :] + o_s[other * chunk : (other + 1) * chunk, :]
        )
        o_ref[inv_ref[b], 0] = rows.astype(BF)


def attend(inv, lengths, w, blocks, units):
    members, _, chunk, _ = blocks[0].shape
    size = len(blocks)
    slot = 2 * members * chunk * size
    rows = 2 * members * chunk
    spec = pl.BlockSpec((members, 3, chunk, LANES), lambda u, *_: (0, u, 0, 0))
    return pl.pallas_call(
        functools.partial(attend_kernel, members, size),
        grid_spec=pltpu.PrefetchScalarGridSpec(
            num_scalar_prefetch=3,
            grid=(units,),
            in_specs=[spec] * size,
            out_specs=[
                pl.BlockSpec((members, 1, chunk, LANES), lambda u, *_: (0, u, 0, 0)),
                pl.BlockSpec((1, rows // TQ, HEAD_DIM, TQ), lambda u, *_: (u, 0, 0, 0)),
                pl.BlockSpec((1, rows // TQ, 1, TQ), lambda u, *_: (u, 0, 0, 0)),
            ],
            scratch_shapes=[
                pltpu.VMEM((slot, LANES), BF),
                pltpu.VMEM((slot // TK, HEAD_DIM, TK), BF),
                pltpu.VMEM((rows, LANES), F4),
                pltpu.VMEM((rows, LANES), F4),
                pltpu.VMEM((slot // TK, TK, TQ), F4),
            ],
        ),
        out_shape=[
            jax.ShapeDtypeStruct((members, units, chunk, LANES), BF),
            jax.ShapeDtypeStruct((units, rows // TQ, HEAD_DIM, TQ), F4),
            jax.ShapeDtypeStruct((units, rows // TQ, 1, TQ), F4),
        ],
        compiler_params=params(1),
        name="attend",
    )(inv, lengths, w, *blocks)


def attend_back_kernel(members, size, inv_ref, len_ref, w_ref, *refs):
    kv_refs = refs[:size]
    do_ref, of_ref, lse_ref = refs[size : size + 3]
    dq_ref = refs[size + 3]
    dkv_refs = refs[size + 4 : 2 * size + 4]
    kv_s, kt_s, q_s, do_s, dq_s, dkv_s = refs[2 * size + 4 :]
    u = pl.program_id(0)
    chunk = kv_refs[0].shape[2]
    own_rows = q_s.shape[0]
    slot = kv_s.shape[0]
    w = w_ref[0]
    length = len_ref[u]
    gather_keys(inv_ref, w, kv_refs, kv_s, members, chunk)

    def put_q(block, rows):
        q_s[block * chunk : (block + 1) * chunk, :] = rows * HEAD_DIM ** (-0.5)

    def put_do(block, rows):
        do_s[block * chunk : (block + 1) * chunk, :] = rows

    gather_rows(inv_ref, lambda chip: kv_refs[0][chip, 2], put_q, members, False)
    gather_rows(inv_ref, lambda chip: do_ref[chip, 0], put_do, members, True)

    def flip(i, carry):
        tile = kv_s[pl.ds(pl.multiple_of(i * TK, TK), TK), :].astype(F4)
        kt_s[i] = tile.T[:HEAD_DIM].astype(BF)
        return carry

    lax.fori_loop(0, slot // TK, flip, 0)
    dkv_s[...] = jnp.zeros_like(dkv_s)
    dq_s[...] = jnp.zeros_like(dq_s)
    span = TQ * size

    def row_tile(t, carry):
        row = pl.multiple_of(t * TQ, TQ)
        q_rows = q_s[pl.ds(row, TQ), :]
        do_rows = do_s[pl.ds(row, TQ), :]
        qt, dot_ = q_rows.T, do_rows.T
        delta = jnp.sum(dot_[HEAD_DIM:] * of_ref[0, t], axis=0, keepdims=True)
        qt, dot_ = qt.astype(BF), dot_.astype(BF)
        stacked = jnp.concatenate([do_rows.astype(BF), q_rows.astype(BF)], axis=0)
        lse = lse_ref[0, t]
        index = lax.broadcasted_iota(jnp.int32, (1, TQ), 1)
        place = t * span + (index // chunk) * (size * chunk) + w * chunk + index % chunk
        limit = jnp.minimum(place, length - 1)

        def step(masked, kt, dqt):
            start = pl.multiple_of(kt * TK, TK)
            kv = kv_s[pl.ds(start, TK), :]
            weights = jnp.exp(dot(kv, qt) - lse)
            if masked:
                keys = kt * TK + lax.broadcasted_iota(jnp.int32, (TK, 1), 0)
                weights = jnp.where(keys <= limit, weights, 0.0)
            pulled = dot(kv, dot_)
            back = (weights * (pulled - delta)).astype(BF)
            dkv_s[pl.ds(start, TK), :] += dot(
                jnp.concatenate([weights.astype(BF), back], axis=1), stacked
            )
            return dqt + dot(kt_s[kt], back)

        clear = jnp.minimum(t * span, length) // TK
        last = jnp.minimum(pl.cdiv((t + 1) * span, TK), pl.cdiv(length, TK))
        dqt = jnp.zeros((HEAD_DIM, TQ), F4)
        dqt = lax.fori_loop(0, clear, functools.partial(step, False), dqt)
        dqt = lax.fori_loop(clear, last, functools.partial(step, True), dqt)
        dqt = dqt * HEAD_DIM ** (-0.5)
        blank = jnp.zeros_like(dqt)
        first = 2 * t * TQ < own_rows
        both = jnp.concatenate(
            [jnp.where(first, dqt, blank), jnp.where(first, blank, dqt)], axis=0
        )
        dq_s[pl.ds(row, TQ), :] = both.T
        return carry

    lax.fori_loop(0, jnp.minimum(pl.cdiv(length, span), own_rows // TQ), row_tile, 0)
    for b in range(members):
        other = 2 * members - 1 - b
        chip = inv_ref[b]
        rows = (
            dq_s[b * chunk : (b + 1) * chunk, :] + dq_s[other * chunk : (other + 1) * chunk, :]
        )
        dq_ref[chip, 0] = rows.astype(BF)
        for half, block in ((0, b), (1, other)):
            for k, ref in enumerate(dkv_refs):
                core = lax.rem(w + k, size)
                start = pl.multiple_of(block * size * chunk + core * chunk, chunk)
                ref[chip, half] = dkv_s[pl.ds(start, chunk), :].astype(ref.dtype)


def attend_back(inv, lengths, w, blocks, do_msg, kept, lse, units):
    members, _, chunk, _ = blocks[0].shape
    size = len(blocks)
    slot = 2 * members * chunk * size
    rows = 2 * members * chunk
    spec = pl.BlockSpec((members, 3, chunk, LANES), lambda u, *_: (0, u, 0, 0))
    one = pl.BlockSpec((members, 1, chunk, LANES), lambda u, *_: (0, u, 0, 0))
    two = pl.BlockSpec((members, 2, chunk, LANES), lambda u, *_: (0, u, 0, 0))
    return pl.pallas_call(
        functools.partial(attend_back_kernel, members, size),
        grid_spec=pltpu.PrefetchScalarGridSpec(
            num_scalar_prefetch=3,
            grid=(units,),
            in_specs=[spec] * size
            + [
                one,
                pl.BlockSpec((1, rows // TQ, HEAD_DIM, TQ), lambda u, *_: (u, 0, 0, 0)),
                pl.BlockSpec((1, rows // TQ, 1, TQ), lambda u, *_: (u, 0, 0, 0)),
            ],
            out_specs=[one] + [two] * size,
            scratch_shapes=[
                pltpu.VMEM((slot, LANES), BF),
                pltpu.VMEM((slot // TK, HEAD_DIM, TK), BF),
                pltpu.VMEM((rows, LANES), F4),
                pltpu.VMEM((rows, LANES), F4),
                pltpu.VMEM((rows, LANES), F4),
                pltpu.VMEM((slot, LANES), F4),
            ],
        ),
        out_shape=[jax.ShapeDtypeStruct((members, units, chunk, LANES), BF)]
        + [
            jax.ShapeDtypeStruct((members, 2 * units, chunk, LANES), BF if k else F4)
            for k in range(size)
        ],
        compiler_params=params(1),
        name="attend_back",
    )(inv, lengths, w, *blocks, do_msg, kept, lse)


def mix_kernel(heads, count, shift_ref, o_ref, x_ref, gain_ref, *refs):
    w_refs = refs[:count]
    mixed_ref, state_ref, a2_ref = refs[count:]
    members, _, chunk, _ = o_ref.shape
    seqs, rows, width = x_ref.shape
    for s in range(seqs):
        for g in range(heads // 2):
            pair = []
            for c in range(2):
                chip, u = head_units(seqs, heads, members, shift_ref[0], s, 2 * g + c)
                pair.append(o_ref[chip, u].astype(F4))
            early, late = pair_swap(*pair)
            part = slice(g * LANES, (g + 1) * LANES)
            mixed_ref[s, :chunk, part] = early.astype(BF)
            mixed_ref[s, chunk:, part] = late.astype(BF)
    inner = heads * HEAD_DIM // count
    made = 0.0
    for k in range(count):
        mixed = mixed_ref[:, :, k * inner : (k + 1) * inner].reshape(seqs * rows, inner)
        made = made + dot(mixed, w_refs[k][...])
    for s in range(seqs):
        state = x_ref[s].astype(F4) + made[s * rows : (s + 1) * rows]
        state_ref[s] = state
        scale = lax.rsqrt(jnp.mean(state * state, axis=-1, keepdims=True) + EPS)
        a2_ref[s] = (state * scale * gain_ref[...]).astype(BF)


def mix(shift, o_msg, x, gain, parts):
    seqs, rows, width = x.shape
    inner = sum(part.shape[0] for part in parts)
    return one_step(
        functools.partial(mix_kernel, inner // HEAD_DIM, len(parts)),
        "mix",
        shift,
        [o_msg, x, gain, *parts],
        [
            jax.ShapeDtypeStruct((seqs, rows, inner), BF),
            jax.ShapeDtypeStruct((seqs, rows, width), F4),
            jax.ShapeDtypeStruct((seqs, rows, width), BF),
        ],
    )


def norm_back(values, gain, upstream):
    scale = lax.rsqrt(jnp.mean(values * values, axis=-1, keepdims=True) + EPS)
    unit = values * scale
    pulled = upstream * gain
    result = scale * (pulled - unit * jnp.mean(pulled * unit, axis=-1, keepdims=True))
    return result, jnp.sum(upstream * unit, axis=0, keepdims=True)


def unrotate_kernel(heads, count, shift_ref, msg_ref, cos_ref, sin_ref, at_ref, *outs):
    dqkv_ref, *grad_refs = outs
    members, triple, chunk, _ = msg_ref.shape
    units = triple // 3
    seqs, rows, _ = dqkv_ref.shape
    cosine, sine = cos_ref[...], sin_ref[...]
    per = heads // count
    inner = per * HEAD_DIM

    def rope_back(grad):
        return grad * cosine - turn_halves(grad) * sine

    for k in list(range(1, count)) + [0]:
        for s in range(seqs):
            for g in range(per // 2):
                pair, asked = [], []
                for c in range(2):
                    chip, u = head_units(
                        seqs, heads, members, shift_ref[0], s, k * per + 2 * g + c
                    )
                    both = [msg_ref[chip, 2 * u], msg_ref[chip, 2 * u + 1]]
                    pair.append(jnp.concatenate(both, axis=0).astype(F4))
                    asked.append(msg_ref[chip, 2 * units + u].astype(F4))
                key, value = pair_swap(*pair)
                query = jnp.concatenate(pair_swap(*asked), axis=0)
                at = 3 * k * inner + g * LANES
                dqkv_ref[s, :, at : at + LANES] = rope_back(query).astype(BF)
                at = at + inner
                dqkv_ref[s, :, at : at + LANES] = rope_back(key).astype(BF)
                at = at + inner
                dqkv_ref[s, :, at : at + LANES] = value.astype(BF)
        cols = dqkv_ref[:, :, 3 * k * inner : 3 * (k + 1) * inner]
        made = dot(at_ref[...], cols.reshape(seqs * rows, 3 * inner))
        grad_refs[k][...] = made.astype(grad_refs[k].dtype)


def unrotate(shift, msg, cosine, sine, a1_turned, seqs, heads, count):
    rows = 2 * msg.shape[2]
    width = a1_turned.shape[0]
    inner = heads * HEAD_DIM
    return one_step(
        functools.partial(unrotate_kernel, heads, count),
        "unrotate",
        shift,
        [msg, cosine, sine, a1_turned],
        [jax.ShapeDtypeStruct((seqs, rows, 3 * inner), BF)]
        + [jax.ShapeDtypeStruct((width, 3 * inner // count), BF if k else F4) for k in range(count)],
    )


def unproject_kernel(count, shift_ref, dqkv_ref, x_ref, dstate_ref, gain_ref, *refs):
    w_refs = refs[:count]
    dx_ref, dgain_ref = refs[count:]
    seqs, rows, width = x_ref.shape
    inner = dqkv_ref.shape[2] // count
    made = 0.0
    for k in range(count):
        cols = dqkv_ref[:, :, k * inner : (k + 1) * inner].reshape(seqs * rows, inner)
        made = made + dot(cols, w_refs[k][...])
    total = jnp.zeros((1, width), F4)
    for s in range(seqs):
        pulled, dgain = norm_back(
            x_ref[s].astype(F4), gain_ref[...], made[s * rows : (s + 1) * rows]
        )
        total = total + dgain
        dx_ref[s] = (dstate_ref[s] + pulled).astype(BF)
    dgain_ref[...] = total


def unproject(shift, dqkv, x, dstate, gain, parts):
    seqs, rows, width = x.shape
    return one_step(
        functools.partial(unproject_kernel, len(parts)),
        "unproject",
        shift,
        [dqkv, x, dstate, gain, *parts],
        [
            jax.ShapeDtypeStruct((seqs, rows, width), BF),
            jax.ShapeDtypeStruct((1, width), F4),
        ],
    )


def two_gates(picked):
    top = jnp.maximum(*picked)
    raised = [jnp.exp(value - top) for value in picked]
    total = raised[0] + raised[1]
    return [value / total for value in raised]


def slot_hits(info_ref, count):
    shape = (count, info_ref.shape[1])
    ids = lax.broadcasted_iota(jnp.int32, shape, 0) + pl.program_id(0) * count
    return ids == info_ref[0:1, :], ids == info_ref[1:2, :]


def dispatch_kernel(info_ref, *refs):
    *second_refs, out_ref = refs
    count, held, width = out_ref.shape
    part = second_refs[0].shape[0]
    one, two = slot_hits(info_ref, count * held)
    hits = (one | two).astype(BF)
    routed = 0.0
    for k, ref in enumerate(second_refs):
        routed = routed + dot(hits[:, k * part : (k + 1) * part], ref[...])
    out_ref[...] = routed.astype(BF).reshape(count, held, width)


def dispatch_early_kernel(info_ref, cot_ref, out_ref):
    count, held, wide = out_ref.shape
    width = cot_ref.shape[1]
    one, two = slot_hits(info_ref, count * held)
    hits = (one | two).astype(BF)
    out_ref[:, :, :width] = dot(hits, cot_ref[...]).astype(BF).reshape(count, held, width)
    other = jnp.where(one, info_ref[3:4, :], 0) + jnp.where(two, info_ref[2:3, :], 0)
    other = jnp.sum(other.astype(F4), axis=1, keepdims=True)
    other = jnp.broadcast_to(other, (count * held, wide - width)).astype(BF)
    out_ref[:, :, width:] = other.reshape(count, held, wide - width)


def dispatch(kernel, info, arrays, wide, experts, held, name):
    count = 4 if experts % 4 == 0 else 1
    return pl.pallas_call(
        kernel,
        grid=(experts // count,),
        in_specs=[whole(array.shape) for array in (info, *arrays)],
        out_specs=pl.BlockSpec((count, held, wide), lambda e: (e, 0, 0)),
        out_shape=jax.ShapeDtypeStruct((experts, held, wide), BF),
        compiler_params=params(1),
        name=name,
    )(info, *arrays)


def two_gates(picked):
    top = jnp.maximum(*picked)
    raised = [jnp.exp(value - top) for value in picked]
    total = raised[0] + raised[1]
    return [value / total for value in raised]


def finish_kernel(
    heads, size, count, shift_ref, info_ref, second_ref, state_ref, cot_ref, gain_ref, *refs
):
    router_ref, turned_ref, *refs = refs
    home_refs, refs = refs[:size], refs[size:]
    dense_ref, *refs = refs
    w_refs = refs[:count]
    out_ref, dstate_ref, low_ref, logit_ref, msg_ref, dgain_ref = refs[count:]
    step = pl.program_id(0)
    take, rows, width = state_ref.shape
    lines = take * rows
    members, units, chunk, _ = msg_ref.shape
    slots = home_refs[0].shape[0]
    experts = turned_ref.shape[0]
    info = info_ref[...].reshape(lines, info_ref.shape[2])
    target = info[:, : 2 * size]
    chosen = [info[:, 2 * size + c : 2 * size + c + 1] for c in range(2)]
    logits = dot(second_ref[...].reshape(lines, width), router_ref[...])[:, :experts]
    names = lax.broadcasted_iota(jnp.int32, (lines, experts), 1)
    gates = two_gates(
        [jnp.sum(jnp.where(names == pick, logits, 0.0), axis=1, keepdims=True) for pick in chosen]
    )
    ids = lax.broadcasted_iota(jnp.int32, (lines, slots), 1)
    made, back = [0.0, 0.0], 0.0
    for k in range(size):
        hits = [ids == target[:, 2 * k + c : 2 * k + c + 1] for c in range(2)]
        for c in range(2):
            made[c] = made[c] + dot(hits[c].astype(BF), home_refs[k][:, :width])
        back = back + dot((hits[0] | hits[1]).astype(BF), home_refs[k][:, width:])
    cot = cot_ref[...].reshape(lines, width).astype(F4)
    pulled = [jnp.sum(y * cot, axis=-1, keepdims=True) for y in made]
    middle = gates[0] * pulled[0] + gates[1] * pulled[1]
    logit = 0.0
    for c in range(2):
        logit = logit + jnp.where(names == chosen[c], gates[c] * (pulled[c] - middle), 0.0)
    logit = logit.astype(BF)
    logit_ref[...] = logit.reshape(take, rows, experts)
    back = back + dot(logit, turned_ref[...])
    branch = gates[0] * made[0] + gates[1] * made[1]
    dense = dense_ref[...].reshape(lines, 2 * width)
    branch = branch + dense[:, :width]
    back = back + dense[:, width:]
    state = state_ref[...].reshape(lines, width)
    out_ref[...] = (state + branch).astype(BF).reshape(take, rows, width)
    pulled, dgain = norm_back(state, gain_ref[...], back)
    dstate = cot + pulled
    dstate_ref[...] = dstate.reshape(take, rows, width)
    low = dstate.astype(BF)
    low_ref[...] = low.reshape(take, rows, width)
    seqs = take * pl.num_programs(0)

    @pl.when(step == 0)
    def _():
        dgain_ref[...] = jnp.zeros_like(dgain_ref)
        if members * units > heads * seqs:
            msg_ref[...] = jnp.zeros_like(msg_ref)

    dgain_ref[...] += dgain
    per = heads // count
    for k in range(count):
        mixed_back = dot(low, w_refs[k][...])
        for s in range(take):
            for g in range(per // 2):
                part = mixed_back[s * rows : (s + 1) * rows, g * LANES : (g + 1) * LANES]
                pair = pair_swap(part[:chunk], part[chunk:])
                for c in range(2):
                    chip, u = head_units(
                        seqs, heads, members, shift_ref[0], step * take + s, k * per + 2 * g + c
                    )
                    msg_ref[chip, u] = pair[c].astype(BF)


def finish(shift, info, second, state, cot, gain, router, turned, homes, dense, parts, members, units):
    seqs, rows, width = state.shape
    inner = sum(part.shape[1] for part in parts)
    experts = turned.shape[0]
    take = max(1, min(seqs, 256 // rows))
    msg = (members, units, rows // 2, LANES)
    some = lambda cols: pl.BlockSpec((take, rows, cols), lambda s: (s, 0, 0))
    return pl.pallas_call(
        functools.partial(finish_kernel, inner // HEAD_DIM, len(homes), len(parts)),
        grid=(seqs // take,),
        in_specs=[SMEM, some(info.shape[2]), some(width), some(width), some(width)]
        + [whole((1, width)), whole(router.shape), whole(turned.shape)]
        + [whole(home.shape) for home in homes]
        + [some(2 * width)]
        + [whole(part.shape) for part in parts],
        out_specs=[some(width)] * 3 + [some(experts), whole(msg), whole((1, width))],
        out_shape=[
            jax.ShapeDtypeStruct((seqs, rows, width), BF),
            jax.ShapeDtypeStruct((seqs, rows, width), F4),
            jax.ShapeDtypeStruct((seqs, rows, width), BF),
            jax.ShapeDtypeStruct((seqs, rows, experts), BF),
            jax.ShapeDtypeStruct(msg, BF),
            jax.ShapeDtypeStruct((1, width), F4),
        ],
        compiler_params=params(1),
        name="finish",
    )(shift, info, second, state, cot, gain, router, turned, *homes, dense, *parts)


def place_kernel(copies, cuts, *refs):
    whole_refs = refs[cuts * copies :]
    blocks = []
    for n in range(cuts):
        total = refs[n * copies][...].astype(F4)
        for ref in refs[n * copies + 1 : (n + 1) * copies]:
            total = total + ref[...].astype(F4)
        blocks.append(total)
    total = jnp.concatenate(blocks, axis=-1)
    for n, out in enumerate(whole_refs):
        out[...] = untile(total, n)


def place(blocks, experts):
    members, rows, _ = blocks[0].shape
    hidden = sum(block.shape[2] for block in blocks) // 3
    copies = members // experts
    take = 2 if experts % 2 == 0 else 1
    return pl.pallas_call(
        functools.partial(place_kernel, copies, len(blocks)),
        grid=(experts // take,),
        in_specs=[
            pl.BlockSpec(
                (take, rows, block.shape[2]), lambda e, n=n: (n * experts // take + e, 0, 0)
            )
            for block in blocks
            for n in range(copies)
        ],
        out_specs=[pl.BlockSpec((take, rows, hidden), lambda e: (e, 0, 0))] * 3,
        out_shape=[jax.ShapeDtypeStruct((experts, rows, hidden), F4)] * 3,
        compiler_params=params(1),
        name="place",
    )(*[block for block in blocks for n in range(copies)])


def gated_kernel(count, tiles, routed, *refs):
    if routed:
        expert_ref, router_ref, early_ref, x_ref, *refs = refs
        d_ref = refs[3 * count]
    else:
        d_ref, x_ref, *refs = refs
    w_refs, (out_ref, hid_ref, acc_ref) = refs[: 3 * count], refs[-3:]
    step = pl.program_id(0)
    rows, width = x_ref.shape
    tile = hid_ref.shape[1] // 3
    take = min(256, rows)

    @pl.when(step == 0)
    def _():
        acc_ref[...] = jnp.zeros_like(acc_ref)
        if routed:
            logits = dot(x_ref[...], router_ref[...])
            names = lane_of(logits.shape)
            other = early_ref[:, width : width + 1].astype(F4).astype(jnp.int32)
            picked = [
                jnp.sum(jnp.where(names == name, logits, 0.0), axis=1, keepdims=True)
                for name in (expert_ref[0], other)
            ]
            gate = two_gates(picked)[0]
            d_ref[...] = (early_ref[:, :width].astype(F4) * gate).astype(BF)

    for k in range(count):

        @pl.when(step // tiles == k)
        def _(k=k):
            gate_w, up_w, down_w = w_refs[3 * k : 3 * k + 3]
            gate_t, up_t, down_t = gate_w[...].T, up_w[...].T, down_w[...].T
            for r in range(0, rows, take):
                mine = slice(r, r + take)
                x, d = x_ref[mine, :], d_ref[mine, :]
                gate, up, back = dot(x, gate_w[...]), dot(x, up_w[...]), dot(d, down_t)
                share = 1.0 / (1.0 + jnp.exp(-gate))
                silu = gate * share
                hidden = (silu * up).astype(BF)
                dup = (back * silu).astype(BF)
                dgate = (back * up * (share * (1.0 + gate * (1.0 - share)))).astype(BF)
                hid_ref[mine, :tile] = dgate
                hid_ref[mine, tile : 2 * tile] = dup
                hid_ref[mine, 2 * tile :] = hidden
                acc_ref[mine, :width] += dot(hidden, down_w[...])
                acc_ref[mine, width:] += dot(dgate, gate_t) + dot(dup, up_t)

    @pl.when(step == pl.num_programs(0) - 1)
    def _():
        out_ref[...] = acc_ref[...].astype(out_ref.dtype)


def tile_of(hidden):
    return min(512, hidden)


def gated(x, d, parts, kind, name, routed=()):
    rows = x.shape[0]
    width, hidden = parts[0][0].shape
    tile = tile_of(hidden)
    tiles = hidden // tile
    count = len(parts)
    flat, specs = [], []
    for k, part in enumerate(parts):
        at = lambda f, k=k: jnp.clip(f - k * tiles, 0, tiles - 1)
        cols = pl.BlockSpec((width, tile), lambda f, at=at: (0, at(f)))
        lines = pl.BlockSpec((tile, width), lambda f, at=at: (at(f), 0))
        flat += list(part)
        specs += [cols, cols, lines]
    ahead = [SMEM, whole(routed[1].shape)] if routed else []
    gated_out = [(whole((rows, width)), jax.ShapeDtypeStruct((rows, width), BF))] if routed else []
    return pl.pallas_call(
        functools.partial(gated_kernel, count, tiles, bool(routed)),
        grid=(count * tiles,),
        in_specs=ahead + [whole(d.shape), whole(x.shape)] + specs,
        out_specs=[spec for spec, _ in gated_out]
        + [whole((rows, 2 * width)), pl.BlockSpec((rows, 3 * tile), lambda f: (0, f))],
        out_shape=[shape for _, shape in gated_out]
        + [
            jax.ShapeDtypeStruct((rows, 2 * width), kind),
            jax.ShapeDtypeStruct((rows, 3 * count * hidden), BF),
        ],
        scratch_shapes=[pltpu.VMEM((rows, 2 * width), F4)],
        compiler_params=params(1),
        name=name,
    )(*routed, d, x, *flat)


def gated_grads_kernel(x_ref, d_ref, hid_ref, out_ref, xt_ref, dt_ref):
    tile = hid_ref.shape[1] // 3

    @pl.when(pl.program_id(0) == 0)
    def _():
        xt_ref[...] = x_ref[...].T
        dt_ref[...] = d_ref[...].T

    out_ref[:, : 2 * tile] = dot(xt_ref[...], hid_ref[:, : 2 * tile]).astype(BF)
    out_ref[:, 2 * tile :] = dot(dt_ref[...], hid_ref[:, 2 * tile :]).astype(BF)


def gated_grads(x, d, hid, k, count, name):
    rows, width = x.shape
    hidden = hid.shape[1] // 3 // count
    tile = tile_of(hidden)
    tiles = hidden // tile
    return pl.pallas_call(
        gated_grads_kernel,
        grid=(tiles,),
        in_specs=[
            whole(x.shape),
            whole(d.shape),
            pl.BlockSpec((rows, 3 * tile), lambda f: (0, k * tiles + f)),
        ],
        out_specs=pl.BlockSpec((width, 3 * tile), lambda f: (0, f)),
        out_shape=jax.ShapeDtypeStruct((width, 3 * hidden), BF),
        scratch_shapes=[pltpu.VMEM((width, rows), BF)] * 2,
        compiler_params=params(1),
        cost_estimate=pl.CostEstimate(
            flops=6 * rows * width * hidden,
            bytes_accessed=2 * (2 * rows * width + 3 * hidden * (rows + width)),
            transcendentals=0,
        ),
        name=name,
    )(x, d, hid)


def untile(array, n):
    hidden = array.shape[-1] // 3
    tile = tile_of(hidden)
    parts = [
        array[..., (3 * j + n) * tile : (3 * j + n + 1) * tile] for j in range(hidden // tile)
    ]
    return jnp.concatenate(parts, axis=-1)


def per_device(
    inputs,
    cotangent,
    lengths,
    block_pairs,
    routes,
    attn_gain,
    query_weight,
    key_weight,
    value_weight,
    out_weight,
    ffn_gain,
    router_weight,
    expert_gate,
    expert_up,
    expert_down,
    dense_gate,
    dense_up,
    dense_down,
):
    pair_rows, seqs, width = inputs.shape[1:]
    members, size = lax.axis_size("ctx"), lax.axis_size("wt")
    ctx, w = lax.axis_index("ctx"), lax.axis_index("wt")
    experts = expert_gate.shape[0]
    block = pair_rows // 2
    chunk = block // size
    rows = 2 * chunk * seqs
    inner = query_weight.shape[1] * size
    heads = inner // HEAD_DIM
    units = -(-(seqs * heads) // members)

    def rows_of(array, k):
        parted = array.reshape(2, size, chunk, seqs, -1)
        mine = lax.dynamic_index_in_dim(parted, (w + k) % size, 1, False)
        return mine.transpose(2, 0, 1, 3).reshape(seqs, 2 * chunk, -1)

    def places_of(k):
        pair = lax.dynamic_index_in_dim(block_pairs, ctx, 0, False)
        blocks = jnp.stack([pair, 2 * members - 1 - pair])
        core = (w + k) % size
        return (blocks[:, None] * block + core * chunk + jnp.arange(chunk)[None, :]).reshape(-1)

    x = rows_of(inputs[0], 0)
    half = HEAD_DIM // 2
    lane = jnp.arange(LANES)
    freqs = THETA ** (-(lane % half).astype(F4) / half)
    angles = places_of(0).astype(F4)[:, None] * freqs[None, :]
    cosine = jnp.cos(angles)
    sine = jnp.sin(angles) * jnp.where(lane % HEAD_DIM < half, -1.0, 1.0)[None, :]

    local = inner // size
    split = size == 2 and local % LANES == 0
    shift = (w * (heads // size) if split else jnp.zeros_like(w)).astype(jnp.int32)[None]
    own_qkv = [query_weight, key_weight, value_weight]
    if split:
        parts = list(zip(*[wt_gather(weight) for weight in own_qkv]))
        out_parts = wt_gather(out_weight)
    else:
        parts = [[lax.all_gather(weight, "wt", axis=1, tiled=True) for weight in own_qkv]]
        out_parts = [lax.all_gather(out_weight, "wt", axis=0, tiled=True)]
    x, cosine, sine = lax.optimization_barrier((x, cosine, sine))
    msg, a1 = project(shift, x, attn_gain[None], cosine, sine, parts, members, units)
    msg, cotangent, routes = lax.optimization_barrier((msg, cotangent, routes))
    got = lax.all_to_all(msg, "ctx", 0, 0, tiled=True)

    near = 4 if members % 4 == 0 else 1
    outer = members // near
    near_groups = [[o * near + i for i in range(near)] for o in range(outer)]
    far_groups = [[o * near + i for o in range(outer)] for i in range(near)]

    def by_steps(array):
        array = array.reshape(outer, near, width // members, -1).swapaxes(0, 1)
        return array.reshape(width, -1)

    def near_scatter(array):
        return lax.psum_scatter(
            array, "ctx", scatter_dimension=0, tiled=True, axis_index_groups=near_groups
        )

    def far_scatter(array):
        return lax.psum_scatter(
            array, "ctx", scatter_dimension=0, tiled=True, axis_index_groups=far_groups
        )

    a1_turned, back_parts, out_back = turn(a1.reshape(rows, width), parts, out_parts)
    a1_turned = by_steps(a1_turned)
    expert = ctx % experts
    expert_parts = list(
        zip(
            *[
                wt_gather(lax.dynamic_index_in_dim(weights, expert, 0, False))
                for weights in (expert_gate, expert_up, expert_down)
            ]
        )
    )
    total_rows = rows * size
    cots = []
    for k in range(size):
        valid = places_of(k)[None, :] < lengths[:, None]
        cots.append(
            jnp.where(valid[:, :, None], rows_of(cotangent[0], k), jnp.zeros((), BF)).reshape(
                rows, width
            )
        )
    cot = jnp.concatenate(cots)

    parted = routes[0].reshape(2, size, chunk, seqs, 2).transpose(1, 3, 0, 2, 4)
    chosen_all = parted.reshape(total_rows, 2)
    names = jnp.arange(experts, dtype=jnp.int32)
    picks_all = chosen_all[:, :, None] == names
    marks = jnp.any(picks_all, axis=1).astype(BF)
    index = jnp.arange(total_rows)
    before = dot((index[None, :] < index[:, None]).astype(BF), marks)
    order_all = jnp.sum(jnp.where(picks_all, before[:, None, :], 0.0), axis=-1).astype(jnp.int32)
    share = -(-CAPACITY // size)
    held = -(-share // 16) * 16

    def targets(chosen, order, core):
        inside = (order >= core * held) & (order < (core + 1) * held)
        return jnp.where(inside, chosen * held + order - core * held, -1)

    def own_first(array):
        pieces = array.reshape(size, rows, 2)
        pieces = jnp.concatenate([pieces, pieces[:-1]])
        return lax.dynamic_slice_in_dim(pieces, w, size, 0).reshape(total_rows, 2)

    chosen, order_here = own_first(chosen_all), own_first(order_all)
    target = targets(chosen, order_here, w)
    own_targets = [
        targets(chosen[:rows], order_here[:rows], (w + k) % size) for k in range(size)
    ]
    own_info = jnp.concatenate(own_targets + [chosen[:rows]], axis=1)
    own_info = own_info.reshape(seqs, 2 * chunk, -1)
    info = jnp.concatenate([target, chosen, jnp.zeros((total_rows, 4), jnp.int32)], axis=1).T
    router_wide = jnp.pad(router_weight, ((0, 0), (0, LANES - experts)))
    router_turned = router_weight.T
    inv = jnp.argsort(block_pairs).astype(jnp.int32)
    unit_slots = jnp.minimum((ctx + members * jnp.arange(units)) // heads, seqs - 1)
    unit_lengths = lengths[unit_slots]
    w_arg = w.astype(jnp.int32)[None]
    groups = None
    if members != experts:
        groups = [[g * experts + e for e in range(experts)] for g in range(members // experts)]
    swap = functools.partial(
        lax.all_to_all,
        axis_name="ctx",
        split_axis=0,
        concat_axis=0,
        axis_index_groups=groups,
        tiled=True,
    )

    early = dispatch(
        dispatch_early_kernel, info, [cot], width + LANES, experts, held, "dispatch_early"
    )
    (
        got,
        early,
        a1_turned,
        back_parts,
        out_back,
        expert_parts,
        cots,
        cot,
        own_info,
        info,
        router_wide,
        router_turned,
        inv,
        unit_lengths,
    ) = (
        lax.optimization_barrier(
            (
                got,
                early,
                a1_turned,
                back_parts,
                out_back,
                expert_parts,
                cots,
                cot,
                own_info,
                info,
                router_wide,
                router_turned,
                inv,
                unit_lengths,
            )
        )
    )

    blocks = wt_gather(got)
    early = swap(early)
    o_msg, kept, lse = attend(inv, unit_lengths, w_arg, blocks, units)
    o_msg, early = lax.optimization_barrier((o_msg, early))
    o_got = lax.all_to_all(o_msg, "ctx", 0, 0, tiled=True)
    mixed, state, second_own = mix(shift, o_got, x, ffn_gain[None], out_parts)

    seconds = wt_gather(second_own.reshape(rows, width))
    sent = dispatch(dispatch_kernel, info, seconds, width, experts, held, "dispatch")

    sent, seconds = lax.optimization_barrier((sent, seconds))
    second = jnp.concatenate(seconds)
    arrived = swap(sent)
    dense, dense_hid = gated(second, cot, [[dense_gate, dense_up, dense_down]], F4, "dense_branch")
    dense_grads = gated_grads(second, cot, dense_hid, 0, 1, "dense_grads")
    dense_grads = by_steps(dense_grads)
    denses = [dense[:rows]]
    for k in range(1, size):
        perm = [(i, (i + k) % size) for i in range(size)]
        denses.append(lax.ppermute(dense[k * rows : (k + 1) * rows], "wt", perm))
    arrived, denses, dense_grads = lax.optimization_barrier((arrived, denses, dense_grads))
    dense = denses[0]
    for part in denses[1:]:
        dense = dense + part
    dense_near = near_scatter(dense_grads)

    arrived = arrived.reshape(experts * held, width)
    dye, returned, hid = gated(
        arrived,
        early.reshape(experts * held, -1),
        expert_parts,
        BF,
        "expert_branch",
        (expert.astype(jnp.int32)[None], router_wide),
    )
    home = swap(returned.reshape(experts, held, 2 * width))
    hidden = expert_gate.shape[2]
    expert_sum = None
    for k in list(range(1, size)) + [0]:
        made = gated_grads(arrived, dye, hid, k, size, "expert_grads")
        if k:
            made = lax.ppermute(made, "wt", [(i, (i + k) % size) for i in range(size)])
        expert_sum = made.astype(F4) if expert_sum is None else expert_sum + made.astype(F4)
    expert_sum = expert_sum.astype(BF).reshape(members, width // members, 3 * hidden)
    cut = 3 * hidden // 2
    expert_sum = [expert_sum[:, :, :cut], expert_sum[:, :, cut:]]
    home, expert_sum, dense_near, dense = lax.optimization_barrier(
        (home, expert_sum, dense_near, dense)
    )
    dense_sum = far_scatter(dense_near)
    homes = wt_gather(home.reshape(experts * held, 2 * width))

    own_cot = cots[0].reshape(seqs, 2 * chunk, width)
    dense = dense.reshape(seqs, 2 * chunk, 2 * width)
    output, dstate, dstate_low, logit_back, do_msg, ffn_grad = finish(
        shift,
        own_info,
        second_own,
        state,
        own_cot,
        ffn_gain[None],
        router_wide,
        router_turned,
        homes,
        dense,
        out_back,
        members,
        units,
    )
    do_got = lax.all_to_all(do_msg, "ctx", 0, 0, tiled=True)

    def share_of(array, kinds, k):
        if split:
            return array[..., k * kinds * local : (k + 1) * kinds * local].reshape(rows, -1)
        cols = array.reshape(rows, kinds, size, local)
        return lax.dynamic_index_in_dim(cols, (w + k) % size, 2, False).reshape(rows, -1)

    def split_wt(left, right, kinds):
        pieces = []
        for k in range(size):
            made = dot_tn(left.reshape(rows, -1), share_of(right, kinds, k))
            pieces.append(made if k == 0 else made.astype(BF))
        return wt_scatter(pieces).astype(BF)

    router_grad = dot_tn(second_own.reshape(rows, width), logit_back.reshape(rows, experts))
    small = wt_sum(jnp.concatenate([ffn_grad.T, router_grad], axis=1))
    small_high = small.astype(BF)
    small_low = (small - small_high.astype(F4)).astype(BF)
    few = experts + 1
    blank = jnp.zeros((width, -(2 * few) % LANES), BF)
    out_msg = [split_wt(dstate_low, mixed, 1), small_high, small_low, blank]
    out_msg = by_steps(jnp.concatenate(out_msg, axis=1))
    do_got, out_msg, output, dense_sum, expert_sum = lax.optimization_barrier(
        (do_got, out_msg, output, dense_sum, expert_sum)
    )
    expert_got = [lax.all_to_all(expert_sum[0], "ctx", 0, 0, tiled=True)]
    out_near = near_scatter(out_msg)
    dq, *dkv = attend_back(inv, unit_lengths, w_arg, blocks, do_got, kept, lse, units)
    dq, dkv, expert_got, out_near = lax.optimization_barrier((dq, dkv, expert_got, out_near))
    out_sum = far_scatter(out_near)
    dkv = wt_scatter(dkv).astype(BF)
    grad_msg = jnp.concatenate([dkv, dq], axis=1)
    grad_got = lax.all_to_all(grad_msg, "ctx", 0, 0, tiled=True)
    grad_got, out_sum, expert_sum = lax.optimization_barrier((grad_got, out_sum, expert_sum))
    expert_got.append(lax.all_to_all(expert_sum[1], "ctx", 0, 0, tiled=True))
    dqkv, *pieces = unrotate(shift, grad_got, cosine, sine, a1_turned, seqs, heads, len(parts))
    if split:
        last_msg = wt_scatter(pieces).astype(BF)
    else:
        last_msg = by_steps(split_wt(a1, dqkv, 3))
    last_sum = far_scatter(near_scatter(last_msg))
    dx, attn_grad = unproject(shift, dqkv, x, dstate, attn_gain[None], back_parts)
    attn_grad = ctx_sum(wt_sum(attn_grad)).reshape(members, -1)
    attn_grad = lax.dynamic_index_in_dim(attn_grad, ctx, 0, False)
    expert_grads = place(expert_got, experts)
    last_sum = last_sum.astype(F4)
    out_sum = out_sum.astype(F4)
    tail = out_sum[:, local:]
    tail = tail[:, :few] + tail[:, few : 2 * few]

    def to_tokens(own):
        array = in_order(wt_gather(own)).reshape(size, seqs, 2, chunk, width)
        return array.transpose(2, 0, 3, 1, 4).reshape(inputs.shape)

    return (
        to_tokens(output),
        to_tokens(dx),
        attn_grad,
        *[last_sum[:, n * local : (n + 1) * local] for n in range(3)],
        out_sum[:, :local].T,
        tail[:, 0],
        tail[:, 1:],
        *expert_grads[:2],
        expert_grads[2].transpose(0, 2, 1),
        *[untile(dense_sum, n).astype(F4) for n in range(2)],
        untile(dense_sum, 2).astype(F4).T,
    )


def solution(mesh):
    placed = (
        P("ctx", None, None, None),
        P("ctx", None, None, None),
        P(),
        P(),
        P("ctx", None, None, None),
        P(),
        P(None, "wt"),
        P(None, "wt"),
        P(None, "wt"),
        P("wt", None),
        P(),
        P(),
        P(None, None, "wt"),
        P(None, None, "wt"),
        P(None, "wt", None),
        P(None, "wt"),
        P(None, "wt"),
        P("wt", None),
    )
    return jax.shard_map(
        per_device,
        mesh=mesh,
        in_specs=placed,
        out_specs=(
            P("ctx", None, None, None),
            P("ctx", None, None, None),
            P("ctx"),
            P("ctx", "wt"),
            P("ctx", "wt"),
            P("ctx", "wt"),
            P("wt", "ctx"),
            P("ctx"),
            P("ctx", None),
            P(None, "ctx", "wt"),
            P(None, "ctx", "wt"),
            P(None, "wt", "ctx"),
            P("ctx", "wt"),
            P("ctx", "wt"),
            P("wt", "ctx"),
        ),
        check_vma=False,
    )
```

```python
import functools

import jax
import jax.numpy as jnp
from jax import lax
from jax.experimental import pallas as pl
from jax.experimental.pallas import tpu as pltpu
from jax.sharding import PartitionSpec as P

HEAD_DIM = 64
CAPACITY = 160
EPS = 1e-06
THETA = 10000.0
LANES = 128
BF = jnp.bfloat16
F4 = jnp.float32
TQ = 512
TK = 1024
VMEM_LIMIT = 56 * 1024 * 1024


def dot(a, b):
    return jnp.dot(a, b, preferred_element_type=F4)


def dot_nt(a, b):
    return lax.dot_general(a, b, (((1,), (1,)), ((), ())), preferred_element_type=F4)


def dot_tn(a, b):
    return lax.dot_general(a, b, (((0,), (0,)), ((), ())), preferred_element_type=F4)


def wt_gather(x):
    size = lax.axis_size("wt")
    return [x] + [
        lax.ppermute(x, "wt", [(i, (i - k) % size) for i in range(size)]) for k in range(1, size)
    ]


def wt_scatter(pieces):
    size = lax.axis_size("wt")
    total = pieces[0]
    for k in range(1, size):
        moved = lax.ppermute(pieces[k], "wt", [(i, (i + k) % size) for i in range(size)])
        total = total + moved.astype(total.dtype)
    return total


def wt_sum(x):
    if lax.axis_size("wt") == 2:
        return x + lax.ppermute(x, "wt", [(0, 1), (1, 0)])
    return lax.psum(x, "wt")


def ctx_sum(x):
    size = lax.axis_size("ctx")
    if size & (size - 1):
        return lax.psum(x, "ctx")
    by = 1
    while by < size:
        x = x + lax.ppermute(x, "ctx", [(i, i ^ by) for i in range(size)])
        by *= 2
    return x


def in_order(parts):
    size = len(parts)
    start = (size - lax.axis_index("wt")) % size
    return lax.dynamic_slice_in_dim(jnp.stack(parts + parts[:-1]), start, size, 0)


def lane_of(shape):
    return lax.broadcasted_iota(jnp.int32, shape, len(shape) - 1)


def pair_swap(a, b):
    low = lane_of(a.shape) < HEAD_DIM
    return (
        jnp.where(low, a, pltpu.roll(b, HEAD_DIM, 1)),
        jnp.where(low, pltpu.roll(a, HEAD_DIM, 1), b),
    )


def turn_halves(t):
    first = lane_of(t.shape) % HEAD_DIM < HEAD_DIM // 2
    return jnp.where(
        first,
        pltpu.roll(t, LANES - HEAD_DIM // 2, 1),
        pltpu.roll(t, HEAD_DIM // 2, 1),
    )


def params(count):
    return pltpu.CompilerParams(
        vmem_limit_bytes=VMEM_LIMIT, dimension_semantics=("arbitrary",) * count
    )


def whole(shape):
    return pl.BlockSpec(shape, lambda *i: (0,) * len(shape))


def head_units(seqs, heads, members, shift, s, rel):
    unit = s * heads + lax.rem(rel + shift, heads)
    return lax.rem(unit, members), lax.div(unit, members)


def project_kernel(heads, units, members, count, shift_ref, x_ref, gain_ref, cos_ref, sin_ref, *refs):
    w_refs = refs[: 3 * count]
    msg_ref, a1_ref = refs[3 * count :]
    seqs, rows, width = x_ref.shape
    chunk = rows // 2
    for s in range(seqs):
        x = x_ref[s].astype(F4)
        scale = lax.rsqrt(jnp.mean(x * x, axis=-1, keepdims=True) + EPS)
        a1_ref[s] = (x * scale * gain_ref[...]).astype(BF)
    if units * members > heads * seqs:
        msg_ref[...] = jnp.zeros_like(msg_ref)
    a1 = a1_ref[...].reshape(seqs * rows, width)
    cosine, sine = cos_ref[...], sin_ref[...]

    def rope(t):
        return t * cosine + turn_halves(t) * sine

    per = heads // count
    for k in range(count):
        query, key, value = (dot(a1, ref[...]) for ref in w_refs[3 * k : 3 * k + 3])
        for s in range(seqs):
            mine = slice(s * rows, (s + 1) * rows)
            for g in range(per // 2):
                part = slice(g * LANES, (g + 1) * LANES)
                pairs = pair_swap(rope(key[mine, part]), value[mine, part])
                turned = rope(query[mine, part])
                asked = pair_swap(turned[:chunk], turned[chunk:])
                for c in range(2):
                    chip, u = head_units(
                        seqs, heads, members, shift_ref[0], s, k * per + 2 * g + c
                    )
                    msg_ref[chip, 3 * u] = pairs[c][:chunk].astype(BF)
                    msg_ref[chip, 3 * u + 1] = pairs[c][chunk:].astype(BF)
                    msg_ref[chip, 3 * u + 2] = asked[c].astype(BF)


SMEM = pl.BlockSpec(memory_space=pltpu.SMEM)


def one_step(kernel, name, shift, arrays, shapes):
    return pl.pallas_call(
        kernel,
        grid=(1,),
        in_specs=[SMEM] + [whole(array.shape) for array in arrays],
        out_specs=[whole(shape.shape) for shape in shapes],
        out_shape=shapes,
        compiler_params=params(1),
        name=name,
    )(shift, *arrays)


def project(shift, x, gain, cosine, sine, parts, members, units):
    seqs, rows, width = x.shape
    count = len(parts)
    heads = sum(part[0].shape[1] for part in parts) // HEAD_DIM
    flat = [w for part in parts for w in part]
    return one_step(
        functools.partial(project_kernel, heads, units, members, count),
        "project",
        shift,
        [x, gain, cosine, sine, *flat],
        [
            jax.ShapeDtypeStruct((members, 3 * units, rows // 2, LANES), BF),
            jax.ShapeDtypeStruct((seqs, rows, width), BF),
        ],
    )


def turn_kernel(count, shift_ref, *refs):
    (a1_ref, *ins), (a1t_ref, *outs) = refs[: 1 + 4 * count], refs[1 + 4 * count :]
    a1t_ref[...] = a1_ref[...].T
    for k in range(count):
        inner = ins[4 * k].shape[1]
        for n in range(3):
            outs[2 * k][n * inner : (n + 1) * inner, :] = ins[4 * k + n][...].T
        outs[2 * k + 1][...] = ins[4 * k + 3][...].T


def turn(a1, parts, out_parts):
    rows, width = a1.shape
    ins = [a1]
    shapes = [jax.ShapeDtypeStruct((width, rows), BF)]
    for part, out_part in zip(parts, out_parts):
        ins += [*part, out_part]
        inner = out_part.shape[0]
        shapes += [
            jax.ShapeDtypeStruct((3 * inner, width), BF),
            jax.ShapeDtypeStruct((width, inner), BF),
        ]
    made = one_step(
        functools.partial(turn_kernel, len(parts)), "turn", jnp.zeros((1,), jnp.int32), ins, shapes
    )
    return made[0], list(made[1::2]), list(made[2::2])


def gather_keys(inv_ref, w, kv_refs, kv_s, members, chunk):
    size = len(kv_refs)
    for block in range(2 * members):
        half = 0 if block < members else 1
        chip = inv_ref[block if half == 0 else 2 * members - 1 - block]
        for k, ref in enumerate(kv_refs):
            core = lax.rem(w + k, size)
            start = pl.multiple_of(block * size * chunk + core * chunk, chunk)
            kv_s[pl.ds(start, chunk), :] = ref[chip, half]


def gather_rows(inv_ref, read, put, members, to_high):
    for block in range(2 * members):
        half = 0 if block < members else 1
        chip = inv_ref[block if half == 0 else 2 * members - 1 - block]
        rows = read(chip).astype(F4)
        if (half == 1) != to_high:
            rows = pltpu.roll(rows, HEAD_DIM, 1)
        low = lane_of(rows.shape) < HEAD_DIM
        rows = jnp.where(low, 0.0, rows) if to_high else jnp.where(low, rows, 0.0)
        put(block, rows)


def attend_kernel(members, size, inv_ref, len_ref, w_ref, *refs):
    kv_refs = refs[:size]
    o_ref, of_ref, stat_ref = refs[size : size + 3]
    kv_s, vt_s, q_s, o_s, s_s = refs[size + 3 :]
    u = pl.program_id(0)
    chunk = kv_refs[0].shape[2]
    own_rows = q_s.shape[0]
    slot = kv_s.shape[0]
    w = w_ref[0]
    length = len_ref[u]
    gather_keys(inv_ref, w, kv_refs, kv_s, members, chunk)

    def put(block, rows):
        q_s[block * chunk : (block + 1) * chunk, :] = rows * HEAD_DIM ** (-0.5)

    gather_rows(inv_ref, lambda chip: kv_refs[0][chip, 2], put, members, False)

    def flip(i, carry):
        tile = kv_s[pl.ds(pl.multiple_of(i * TK, TK), TK), :].astype(F4)
        vt_s[i] = tile.T[HEAD_DIM:].astype(BF)
        return carry

    lax.fori_loop(0, slot // TK, flip, 0)
    span = TQ * size

    def row_tile(t, carry):
        row = pl.multiple_of(t * TQ, TQ)
        qt = q_s[pl.ds(row, TQ), :].T.astype(BF)
        index = lax.broadcasted_iota(jnp.int32, (1, TQ), 1)
        place = t * span + (index // chunk) * (size * chunk) + w * chunk + index % chunk
        limit = jnp.minimum(place, length - 1)

        def first_step(masked, kt, top):
            start = pl.multiple_of(kt * TK, TK)
            scores = dot(kv_s[pl.ds(start, TK), :], qt)
            if masked:
                keys = kt * TK + lax.broadcasted_iota(jnp.int32, (TK, 1), 0)
                scores = jnp.where(keys <= limit, scores, -1e30)
            s_s[kt] = scores
            return jnp.maximum(top, jnp.max(scores.reshape(TK // 8, 8, TQ), axis=0))

        def second_step(kt, state):
            total, acc = state
            weights = jnp.exp(s_s[kt] - top)
            total = total + jnp.sum(weights.reshape(TK // 8, 8, TQ), axis=0)
            return total, acc + dot(vt_s[kt], weights.astype(BF))

        clear = jnp.minimum(t * span, length) // TK
        last = jnp.minimum(pl.cdiv((t + 1) * span, TK), pl.cdiv(length, TK))
        top = jnp.full((8, TQ), -1e30, F4)
        top = lax.fori_loop(0, clear, functools.partial(first_step, False), top)
        top = lax.fori_loop(clear, last, functools.partial(first_step, True), top)
        top = jnp.max(top, axis=0, keepdims=True)
        state = (jnp.zeros((8, TQ), F4), jnp.zeros((HEAD_DIM, TQ), F4))
        total, acc = lax.fori_loop(0, last, second_step, state)
        total = jnp.sum(total, axis=0, keepdims=True)
        result = acc / total
        of_ref[0, t] = result
        stat_ref[0, t, 0:1] = top
        stat_ref[0, t, 1:2] = 1.0 / total
        blank = jnp.zeros_like(result)
        first = 2 * t * TQ < own_rows
        both = jnp.concatenate(
            [jnp.where(first, result, blank), jnp.where(first, blank, result)], axis=0
        )
        o_s[pl.ds(row, TQ), :] = both.T
        return carry

    lax.fori_loop(0, own_rows // TQ, row_tile, 0)
    for b in range(members):
        other = 2 * members - 1 - b
        rows = (
            o_s[b * chunk : (b + 1) * chunk, :] + o_s[other * chunk : (other + 1) * chunk, :]
        )
        o_ref[inv_ref[b], 0] = rows.astype(BF)


def attend(inv, lengths, w, blocks, units):
    members, _, chunk, _ = blocks[0].shape
    size = len(blocks)
    slot = 2 * members * chunk * size
    rows = 2 * members * chunk
    spec = pl.BlockSpec((members, 3, chunk, LANES), lambda u, *_: (0, u, 0, 0))
    return pl.pallas_call(
        functools.partial(attend_kernel, members, size),
        grid_spec=pltpu.PrefetchScalarGridSpec(
            num_scalar_prefetch=3,
            grid=(units,),
            in_specs=[spec] * size,
            out_specs=[
                pl.BlockSpec((members, 1, chunk, LANES), lambda u, *_: (0, u, 0, 0)),
                pl.BlockSpec((1, rows // TQ, HEAD_DIM, TQ), lambda u, *_: (u, 0, 0, 0)),
                pl.BlockSpec((1, rows // TQ, 2, TQ), lambda u, *_: (u, 0, 0, 0)),
            ],
            scratch_shapes=[
                pltpu.VMEM((slot, LANES), BF),
                pltpu.VMEM((slot // TK, HEAD_DIM, TK), BF),
                pltpu.VMEM((rows, LANES), F4),
                pltpu.VMEM((rows, LANES), F4),
                pltpu.VMEM((slot // TK, TK, TQ), F4),
            ],
        ),
        out_shape=[
            jax.ShapeDtypeStruct((members, units, chunk, LANES), BF),
            jax.ShapeDtypeStruct((units, rows // TQ, HEAD_DIM, TQ), F4),
            jax.ShapeDtypeStruct((units, rows // TQ, 2, TQ), F4),
        ],
        compiler_params=params(1),
        name="attend",
    )(inv, lengths, w, *blocks)


def attend_back_kernel(members, size, inv_ref, len_ref, w_ref, *refs):
    kv_refs = refs[:size]
    do_ref, of_ref, stat_ref = refs[size : size + 3]
    dq_ref = refs[size + 3]
    dkv_refs = refs[size + 4 : 2 * size + 4]
    kv_s, kt_s, q_s, do_s, dq_s, dkv_s = refs[2 * size + 4 :]
    u = pl.program_id(0)
    chunk = kv_refs[0].shape[2]
    own_rows = q_s.shape[0]
    slot = kv_s.shape[0]
    w = w_ref[0]
    length = len_ref[u]
    gather_keys(inv_ref, w, kv_refs, kv_s, members, chunk)

    def put_q(block, rows):
        q_s[block * chunk : (block + 1) * chunk, :] = rows * HEAD_DIM ** (-0.5)

    def put_do(block, rows):
        do_s[block * chunk : (block + 1) * chunk, :] = rows

    gather_rows(inv_ref, lambda chip: kv_refs[0][chip, 2], put_q, members, False)
    gather_rows(inv_ref, lambda chip: do_ref[chip, 0], put_do, members, True)

    def flip(i, carry):
        tile = kv_s[pl.ds(pl.multiple_of(i * TK, TK), TK), :].astype(F4)
        kt_s[i] = tile.T[:HEAD_DIM].astype(BF)
        return carry

    lax.fori_loop(0, slot // TK, flip, 0)
    dkv_s[...] = jnp.zeros_like(dkv_s)
    dq_s[...] = jnp.zeros_like(dq_s)
    span = TQ * size

    def row_tile(t, carry):
        row = pl.multiple_of(t * TQ, TQ)
        q_rows = q_s[pl.ds(row, TQ), :]
        do_rows = do_s[pl.ds(row, TQ), :]
        qt, dot_ = q_rows.T, do_rows.T
        delta = jnp.sum(dot_[HEAD_DIM:] * of_ref[0, t], axis=0, keepdims=True)
        qt, dot_ = qt.astype(BF), dot_.astype(BF)
        stacked = jnp.concatenate([do_rows.astype(BF), q_rows.astype(BF)], axis=0)
        top, share = stat_ref[0, t, 0:1], stat_ref[0, t, 1:2]
        index = lax.broadcasted_iota(jnp.int32, (1, TQ), 1)
        place = t * span + (index // chunk) * (size * chunk) + w * chunk + index % chunk
        limit = jnp.minimum(place, length - 1)

        def step(masked, kt, dqt):
            start = pl.multiple_of(kt * TK, TK)
            kv = kv_s[pl.ds(start, TK), :]
            weights = jnp.exp(dot(kv, qt) - top) * share
            if masked:
                keys = kt * TK + lax.broadcasted_iota(jnp.int32, (TK, 1), 0)
                weights = jnp.where(keys <= limit, weights, 0.0)
            pulled = dot(kv, dot_)
            back = (weights * (pulled - delta)).astype(BF)
            dkv_s[pl.ds(start, TK), :] += dot(
                jnp.concatenate([weights.astype(BF), back], axis=1), stacked
            )
            return dqt + dot(kt_s[kt], back)

        clear = jnp.minimum(t * span, length) // TK
        last = jnp.minimum(pl.cdiv((t + 1) * span, TK), pl.cdiv(length, TK))
        dqt = jnp.zeros((HEAD_DIM, TQ), F4)
        dqt = lax.fori_loop(0, clear, functools.partial(step, False), dqt)
        dqt = lax.fori_loop(clear, last, functools.partial(step, True), dqt)
        dqt = dqt * HEAD_DIM ** (-0.5)
        blank = jnp.zeros_like(dqt)
        first = 2 * t * TQ < own_rows
        both = jnp.concatenate(
            [jnp.where(first, dqt, blank), jnp.where(first, blank, dqt)], axis=0
        )
        dq_s[pl.ds(row, TQ), :] = both.T
        return carry

    lax.fori_loop(0, jnp.minimum(pl.cdiv(length, span), own_rows // TQ), row_tile, 0)
    for b in range(members):
        other = 2 * members - 1 - b
        chip = inv_ref[b]
        rows = (
            dq_s[b * chunk : (b + 1) * chunk, :] + dq_s[other * chunk : (other + 1) * chunk, :]
        )
        dq_ref[chip, 0] = rows.astype(BF)
        for half, block in ((0, b), (1, other)):
            for k, ref in enumerate(dkv_refs):
                core = lax.rem(w + k, size)
                start = pl.multiple_of(block * size * chunk + core * chunk, chunk)
                ref[chip, half] = dkv_s[pl.ds(start, chunk), :].astype(ref.dtype)


def attend_back(inv, lengths, w, blocks, do_msg, kept, stats, units):
    members, _, chunk, _ = blocks[0].shape
    size = len(blocks)
    slot = 2 * members * chunk * size
    rows = 2 * members * chunk
    spec = pl.BlockSpec((members, 3, chunk, LANES), lambda u, *_: (0, u, 0, 0))
    one = pl.BlockSpec((members, 1, chunk, LANES), lambda u, *_: (0, u, 0, 0))
    two = pl.BlockSpec((members, 2, chunk, LANES), lambda u, *_: (0, u, 0, 0))
    return pl.pallas_call(
        functools.partial(attend_back_kernel, members, size),
        grid_spec=pltpu.PrefetchScalarGridSpec(
            num_scalar_prefetch=3,
            grid=(units,),
            in_specs=[spec] * size
            + [
                one,
                pl.BlockSpec((1, rows // TQ, HEAD_DIM, TQ), lambda u, *_: (u, 0, 0, 0)),
                pl.BlockSpec((1, rows // TQ, 2, TQ), lambda u, *_: (u, 0, 0, 0)),
            ],
            out_specs=[one] + [two] * size,
            scratch_shapes=[
                pltpu.VMEM((slot, LANES), BF),
                pltpu.VMEM((slot // TK, HEAD_DIM, TK), BF),
                pltpu.VMEM((rows, LANES), F4),
                pltpu.VMEM((rows, LANES), F4),
                pltpu.VMEM((rows, LANES), F4),
                pltpu.VMEM((slot, LANES), F4),
            ],
        ),
        out_shape=[jax.ShapeDtypeStruct((members, units, chunk, LANES), BF)]
        + [
            jax.ShapeDtypeStruct((members, 2 * units, chunk, LANES), BF if k else F4)
            for k in range(size)
        ],
        compiler_params=params(1),
        name="attend_back",
    )(inv, lengths, w, *blocks, do_msg, kept, stats)


def mix_kernel(heads, count, shift_ref, o_ref, x_ref, gain_ref, *refs):
    w_refs = refs[:count]
    mixed_ref, state_ref, a2_ref = refs[count:]
    members, _, chunk, _ = o_ref.shape
    seqs, rows, width = x_ref.shape
    for s in range(seqs):
        for g in range(heads // 2):
            pair = []
            for c in range(2):
                chip, u = head_units(seqs, heads, members, shift_ref[0], s, 2 * g + c)
                pair.append(o_ref[chip, u].astype(F4))
            early, late = pair_swap(*pair)
            part = slice(g * LANES, (g + 1) * LANES)
            mixed_ref[s, :chunk, part] = early.astype(BF)
            mixed_ref[s, chunk:, part] = late.astype(BF)
    inner = heads * HEAD_DIM // count
    made = 0.0
    for k in range(count):
        mixed = mixed_ref[:, :, k * inner : (k + 1) * inner].reshape(seqs * rows, inner)
        made = made + dot(mixed, w_refs[k][...])
    for s in range(seqs):
        state = x_ref[s].astype(F4) + made[s * rows : (s + 1) * rows]
        state_ref[s] = state
        scale = lax.rsqrt(jnp.mean(state * state, axis=-1, keepdims=True) + EPS)
        a2_ref[s] = (state * scale * gain_ref[...]).astype(BF)


def mix(shift, o_msg, x, gain, parts):
    seqs, rows, width = x.shape
    inner = sum(part.shape[0] for part in parts)
    return one_step(
        functools.partial(mix_kernel, inner // HEAD_DIM, len(parts)),
        "mix",
        shift,
        [o_msg, x, gain, *parts],
        [
            jax.ShapeDtypeStruct((seqs, rows, inner), BF),
            jax.ShapeDtypeStruct((seqs, rows, width), F4),
            jax.ShapeDtypeStruct((seqs, rows, width), BF),
        ],
    )


def norm_back(values, gain, upstream):
    scale = lax.rsqrt(jnp.mean(values * values, axis=-1, keepdims=True) + EPS)
    unit = values * scale
    pulled = upstream * gain
    result = scale * (pulled - unit * jnp.mean(pulled * unit, axis=-1, keepdims=True))
    return result, jnp.sum(upstream * unit, axis=0, keepdims=True)


def unrotate_kernel(heads, per, k, shift_ref, msg_ref, cos_ref, sin_ref, at_ref, dqkv_ref, grad_ref):
    members, triple, chunk, _ = msg_ref.shape
    units = triple // 3
    seqs, rows, _ = dqkv_ref.shape
    cosine, sine = cos_ref[...], sin_ref[...]
    inner = per * HEAD_DIM

    def rope_back(grad):
        return grad * cosine - turn_halves(grad) * sine

    for s in range(seqs):
        for g in range(per // 2):
            pair, asked = [], []
            for c in range(2):
                chip, u = head_units(seqs, heads, members, shift_ref[0], s, k * per + 2 * g + c)
                both = [msg_ref[chip, 2 * u], msg_ref[chip, 2 * u + 1]]
                pair.append(jnp.concatenate(both, axis=0).astype(F4))
                asked.append(msg_ref[chip, 2 * units + u].astype(F4))
            key, value = pair_swap(*pair)
            query = jnp.concatenate(pair_swap(*asked), axis=0)
            at = g * LANES
            dqkv_ref[s, :, at : at + LANES] = rope_back(query).astype(BF)
            at = at + inner
            dqkv_ref[s, :, at : at + LANES] = rope_back(key).astype(BF)
            at = at + inner
            dqkv_ref[s, :, at : at + LANES] = value.astype(BF)
    made = dot(at_ref[...], dqkv_ref[...].reshape(seqs * rows, 3 * inner))
    grad_ref[...] = made.astype(grad_ref.dtype)


def unrotate(shift, msg, cosine, sine, a1_turned, seqs, heads, k, count):
    rows = 2 * msg.shape[2]
    width = a1_turned.shape[0]
    per = heads // count
    inner = per * HEAD_DIM
    return one_step(
        functools.partial(unrotate_kernel, heads, per, k),
        "unrotate",
        shift,
        [msg, cosine, sine, a1_turned],
        [
            jax.ShapeDtypeStruct((seqs, rows, 3 * inner), BF),
            jax.ShapeDtypeStruct((width, 3 * inner), BF if k else F4),
        ],
    )


def unproject_kernel(count, shift_ref, x_ref, dstate_ref, gain_ref, *refs):
    dqkv_refs, w_refs = refs[:count], refs[count : 2 * count]
    dx_ref, dgain_ref = refs[2 * count :]
    seqs, rows, width = x_ref.shape
    made = 0.0
    for dqkv_ref, w_ref in zip(dqkv_refs, w_refs):
        made = made + dot(dqkv_ref[...].reshape(seqs * rows, -1), w_ref[...])
    total = jnp.zeros((1, width), F4)
    for s in range(seqs):
        pulled, dgain = norm_back(
            x_ref[s].astype(F4), gain_ref[...], made[s * rows : (s + 1) * rows]
        )
        total = total + dgain
        dx_ref[s] = (dstate_ref[s] + pulled).astype(BF)
    dgain_ref[...] = total


def unproject(shift, dqkv, x, dstate, gain, parts):
    seqs, rows, width = x.shape
    return one_step(
        functools.partial(unproject_kernel, len(parts)),
        "unproject",
        shift,
        [x, dstate, gain, *dqkv, *parts],
        [
            jax.ShapeDtypeStruct((seqs, rows, width), BF),
            jax.ShapeDtypeStruct((1, width), F4),
        ],
    )


def two_gates(picked):
    top = jnp.maximum(*picked)
    raised = [jnp.exp(value - top) for value in picked]
    total = raised[0] + raised[1]
    return [value / total for value in raised]


def slot_hits(info_ref, count):
    shape = (count, info_ref.shape[1])
    ids = lax.broadcasted_iota(jnp.int32, shape, 0) + pl.program_id(0) * count
    return ids == info_ref[0:1, :], ids == info_ref[1:2, :]


def dispatch_kernel(info_ref, *refs):
    *second_refs, out_ref = refs
    count, held, width = out_ref.shape
    part = second_refs[0].shape[0]
    one, two = slot_hits(info_ref, count * held)
    hits = (one | two).astype(BF)
    routed = 0.0
    for k, ref in enumerate(second_refs):
        routed = routed + dot(hits[:, k * part : (k + 1) * part], ref[...])
    out_ref[...] = routed.astype(BF).reshape(count, held, width)


def dispatch_early_kernel(info_ref, cot_ref, out_ref):
    count, held, wide = out_ref.shape
    width = cot_ref.shape[1]
    one, two = slot_hits(info_ref, count * held)
    hits = (one | two).astype(BF)
    out_ref[:, :, :width] = dot(hits, cot_ref[...]).astype(BF).reshape(count, held, width)
    other = jnp.where(one, info_ref[3:4, :], 0) + jnp.where(two, info_ref[2:3, :], 0)
    other = jnp.sum(other.astype(F4), axis=1, keepdims=True)
    other = jnp.broadcast_to(other, (count * held, wide - width)).astype(BF)
    out_ref[:, :, width:] = other.reshape(count, held, wide - width)


def dispatch(kernel, info, arrays, wide, experts, held, name):
    count = 4 if experts % 4 == 0 else 1
    return pl.pallas_call(
        kernel,
        grid=(experts // count,),
        in_specs=[whole(array.shape) for array in (info, *arrays)],
        out_specs=pl.BlockSpec((count, held, wide), lambda e: (e, 0, 0)),
        out_shape=jax.ShapeDtypeStruct((experts, held, wide), BF),
        compiler_params=params(1),
        name=name,
    )(info, *arrays)


def two_gates(picked):
    top = jnp.maximum(*picked)
    raised = [jnp.exp(value - top) for value in picked]
    total = raised[0] + raised[1]
    return [value / total for value in raised]


def take_back(info, home_ref, k, width):
    target = info[:, 2 * k : 2 * k + 2]
    ids = lax.broadcasted_iota(jnp.int32, (info.shape[0], home_ref.shape[0]), 1)
    hits = [ids == target[:, c : c + 1] for c in range(2)]
    made = [dot(hit.astype(BF), home_ref[:, :width]) for hit in hits]
    return [*made, dot((hits[0] | hits[1]).astype(BF), home_ref[:, width:])]


def first_part_kernel(info_ref, home_ref, out_ref):
    take, rows, triple = out_ref.shape
    width = triple // 3
    info = info_ref[...].reshape(take * rows, info_ref.shape[2])
    for n, part in enumerate(take_back(info, home_ref, 0, width)):
        out_ref[:, :, n * width : (n + 1) * width] = part.reshape(take, rows, width)


def first_part(info, home):
    seqs, rows, cols = info.shape
    width = home.shape[1] // 2
    take = max(1, min(seqs, 256 // rows))
    return pl.pallas_call(
        first_part_kernel,
        grid=(seqs // take,),
        in_specs=[pl.BlockSpec((take, rows, cols), lambda s: (s, 0, 0)), whole(home.shape)],
        out_specs=pl.BlockSpec((take, rows, 3 * width), lambda s: (s, 0, 0)),
        out_shape=jax.ShapeDtypeStruct((seqs, rows, 3 * width), F4),
        compiler_params=params(1),
        name="first_part",
    )(info, home)


def finish_kernel(
    heads, size, count, shift_ref, info_ref, second_ref, state_ref, cot_ref, gain_ref, *refs
):
    router_ref, turned_ref, *refs = refs
    home_refs, refs = refs[: size - 1], refs[size - 1 :]
    first_ref, dense_ref, *refs = refs
    w_refs = refs[:count]
    out_ref, dstate_ref, low_ref, logit_ref, msg_ref, dgain_ref = refs[count:]
    step = pl.program_id(0)
    take, rows, width = state_ref.shape
    lines = take * rows
    members, units, chunk, _ = msg_ref.shape
    experts = turned_ref.shape[0]
    info = info_ref[...].reshape(lines, info_ref.shape[2])
    chosen = [info[:, 2 * size + c : 2 * size + c + 1] for c in range(2)]
    logits = dot(second_ref[...].reshape(lines, width), router_ref[...])[:, :experts]
    names = lax.broadcasted_iota(jnp.int32, (lines, experts), 1)
    gates = two_gates(
        [jnp.sum(jnp.where(names == pick, logits, 0.0), axis=1, keepdims=True) for pick in chosen]
    )
    first = first_ref[...].reshape(lines, 3 * width)
    *made, back = [first[:, n * width : (n + 1) * width] for n in range(3)]
    for k, home_ref in enumerate(home_refs):
        more = take_back(info, home_ref, k + 1, width)
        made = [a + b for a, b in zip(made, more)]
        back = back + more[2]
    cot = cot_ref[...].reshape(lines, width).astype(F4)
    pulled = [jnp.sum(y * cot, axis=-1, keepdims=True) for y in made]
    middle = gates[0] * pulled[0] + gates[1] * pulled[1]
    logit = 0.0
    for c in range(2):
        logit = logit + jnp.where(names == chosen[c], gates[c] * (pulled[c] - middle), 0.0)
    logit = logit.astype(BF)
    logit_ref[...] = logit.reshape(take, rows, experts)
    back = back + dot(logit, turned_ref[...])
    branch = gates[0] * made[0] + gates[1] * made[1]
    dense = dense_ref[...].reshape(lines, 2 * width)
    branch = branch + dense[:, :width]
    back = back + dense[:, width:]
    state = state_ref[...].reshape(lines, width)
    out_ref[...] = (state + branch).astype(BF).reshape(take, rows, width)
    pulled, dgain = norm_back(state, gain_ref[...], back)
    dstate = cot + pulled
    dstate_ref[...] = dstate.reshape(take, rows, width)
    low = dstate.astype(BF)
    low_ref[...] = low.reshape(take, rows, width)
    seqs = take * pl.num_programs(0)

    @pl.when(step == 0)
    def _():
        dgain_ref[...] = jnp.zeros_like(dgain_ref)
        if members * units > heads * seqs:
            msg_ref[...] = jnp.zeros_like(msg_ref)

    dgain_ref[...] += dgain
    per = heads // count
    for k in range(count):
        mixed_back = dot(low, w_refs[k][...])
        for s in range(take):
            for g in range(per // 2):
                part = mixed_back[s * rows : (s + 1) * rows, g * LANES : (g + 1) * LANES]
                pair = pair_swap(part[:chunk], part[chunk:])
                for c in range(2):
                    chip, u = head_units(
                        seqs, heads, members, shift_ref[0], step * take + s, k * per + 2 * g + c
                    )
                    msg_ref[chip, u] = pair[c].astype(BF)


def finish(shift, info, second, state, cot, gain, router, turned, homes, first, dense, parts, members, units):
    seqs, rows, width = state.shape
    inner = sum(part.shape[1] for part in parts)
    experts = turned.shape[0]
    take = max(1, min(seqs, 256 // rows))
    msg = (members, units, rows // 2, LANES)
    some = lambda cols: pl.BlockSpec((take, rows, cols), lambda s: (s, 0, 0))
    return pl.pallas_call(
        functools.partial(finish_kernel, inner // HEAD_DIM, len(homes) + 1, len(parts)),
        grid=(seqs // take,),
        in_specs=[SMEM, some(info.shape[2]), some(width), some(width), some(width)]
        + [whole((1, width)), whole(router.shape), whole(turned.shape)]
        + [whole(home.shape) for home in homes]
        + [some(3 * width), some(2 * width)]
        + [whole(part.shape) for part in parts],
        out_specs=[some(width)] * 3 + [some(experts), whole(msg), whole((1, width))],
        out_shape=[
            jax.ShapeDtypeStruct((seqs, rows, width), BF),
            jax.ShapeDtypeStruct((seqs, rows, width), F4),
            jax.ShapeDtypeStruct((seqs, rows, width), BF),
            jax.ShapeDtypeStruct((seqs, rows, experts), BF),
            jax.ShapeDtypeStruct(msg, BF),
            jax.ShapeDtypeStruct((1, width), F4),
        ],
        compiler_params=params(1),
        name="finish",
    )(shift, info, second, state, cot, gain, router, turned, *homes, first, dense, *parts)


def place_kernel(copies, cuts, *refs):
    whole_refs = refs[cuts * copies :]
    blocks = []
    for n in range(cuts):
        total = refs[n * copies][...].astype(F4)
        for ref in refs[n * copies + 1 : (n + 1) * copies]:
            total = total + ref[...].astype(F4)
        blocks.append(total)
    total = jnp.concatenate(blocks, axis=-1)
    for n, out in enumerate(whole_refs):
        out[...] = untile(total, n)


def place(blocks, experts):
    members, rows, _ = blocks[0].shape
    hidden = sum(block.shape[2] for block in blocks) // 3
    copies = members // experts
    take = 2 if experts % 2 == 0 else 1
    return pl.pallas_call(
        functools.partial(place_kernel, copies, len(blocks)),
        grid=(experts // take,),
        in_specs=[
            pl.BlockSpec(
                (take, rows, block.shape[2]), lambda e, n=n: (n * experts // take + e, 0, 0)
            )
            for block in blocks
            for n in range(copies)
        ],
        out_specs=[pl.BlockSpec((take, rows, hidden), lambda e: (e, 0, 0))] * 3,
        out_shape=[jax.ShapeDtypeStruct((experts, rows, hidden), F4)] * 3,
        compiler_params=params(1),
        name="place",
    )(*[block for block in blocks for n in range(copies)])


def gated_kernel(count, tiles, routed, *refs):
    if routed:
        expert_ref, router_ref, early_ref, x_ref, *refs = refs
        d_ref = refs[3 * count]
    else:
        d_ref, x_ref, *refs = refs
    w_refs, (out_ref, hid_ref, acc_ref) = refs[: 3 * count], refs[-3:]
    step = pl.program_id(0)
    rows, width = x_ref.shape
    tile = hid_ref.shape[1] // 3
    take = min(256, rows)

    @pl.when(step == 0)
    def _():
        acc_ref[...] = jnp.zeros_like(acc_ref)
        if routed:
            logits = dot(x_ref[...], router_ref[...])
            names = lane_of(logits.shape)
            other = early_ref[:, width : width + 1].astype(F4).astype(jnp.int32)
            picked = [
                jnp.sum(jnp.where(names == name, logits, 0.0), axis=1, keepdims=True)
                for name in (expert_ref[0], other)
            ]
            gate = two_gates(picked)[0]
            d_ref[...] = (early_ref[:, :width].astype(F4) * gate).astype(BF)

    for k in range(count):

        @pl.when(step // tiles == k)
        def _(k=k):
            gate_w, up_w, down_w = w_refs[3 * k : 3 * k + 3]
            gate_t, up_t, down_t = gate_w[...].T, up_w[...].T, down_w[...].T
            for r in range(0, rows, take):
                mine = slice(r, r + take)
                x, d = x_ref[mine, :], d_ref[mine, :]
                gate, up, back = dot(x, gate_w[...]), dot(x, up_w[...]), dot(d, down_t)
                share = 1.0 / (1.0 + jnp.exp(-gate))
                silu = gate * share
                hidden = (silu * up).astype(BF)
                dup = (back * silu).astype(BF)
                dgate = (back * up * (share * (1.0 + gate * (1.0 - share)))).astype(BF)
                hid_ref[mine, :tile] = dgate
                hid_ref[mine, tile : 2 * tile] = dup
                hid_ref[mine, 2 * tile :] = hidden
                acc_ref[mine, :width] += dot(hidden, down_w[...])
                acc_ref[mine, width:] += dot(dgate, gate_t) + dot(dup, up_t)

    @pl.when(step == pl.num_programs(0) - 1)
    def _():
        out_ref[...] = acc_ref[...].astype(out_ref.dtype)


def tile_of(hidden):
    return min(512, hidden)


def gated(x, d, parts, kind, name, routed=()):
    rows = x.shape[0]
    width, hidden = parts[0][0].shape
    tile = tile_of(hidden)
    tiles = hidden // tile
    count = len(parts)
    flat, specs = [], []
    for k, part in enumerate(parts):
        at = lambda f, k=k: jnp.clip(f - k * tiles, 0, tiles - 1)
        cols = pl.BlockSpec((width, tile), lambda f, at=at: (0, at(f)))
        lines = pl.BlockSpec((tile, width), lambda f, at=at: (at(f), 0))
        flat += list(part)
        specs += [cols, cols, lines]
    ahead = [SMEM, whole(routed[1].shape)] if routed else []
    gated_out = [(whole((rows, width)), jax.ShapeDtypeStruct((rows, width), BF))] if routed else []
    return pl.pallas_call(
        functools.partial(gated_kernel, count, tiles, bool(routed)),
        grid=(count * tiles,),
        in_specs=ahead + [whole(d.shape), whole(x.shape)] + specs,
        out_specs=[spec for spec, _ in gated_out]
        + [whole((rows, 2 * width)), pl.BlockSpec((rows, 3 * tile), lambda f: (0, f))],
        out_shape=[shape for _, shape in gated_out]
        + [
            jax.ShapeDtypeStruct((rows, 2 * width), kind),
            jax.ShapeDtypeStruct((rows, 3 * count * hidden), BF),
        ],
        scratch_shapes=[pltpu.VMEM((rows, 2 * width), F4)],
        compiler_params=params(1),
        name=name,
    )(*routed, d, x, *flat)


def gated_grads_kernel(x_ref, d_ref, hid_ref, out_ref, xt_ref, dt_ref):
    tile = hid_ref.shape[1] // 3

    @pl.when(pl.program_id(0) == 0)
    def _():
        xt_ref[...] = x_ref[...].T
        dt_ref[...] = d_ref[...].T

    out_ref[:, : 2 * tile] = dot(xt_ref[...], hid_ref[:, : 2 * tile]).astype(BF)
    out_ref[:, 2 * tile :] = dot(dt_ref[...], hid_ref[:, 2 * tile :]).astype(BF)


def gated_grads(x, d, hid, k, count, name):
    rows, width = x.shape
    hidden = hid.shape[1] // 3 // count
    tile = tile_of(hidden)
    tiles = hidden // tile
    return pl.pallas_call(
        gated_grads_kernel,
        grid=(tiles,),
        in_specs=[
            whole(x.shape),
            whole(d.shape),
            pl.BlockSpec((rows, 3 * tile), lambda f: (0, k * tiles + f)),
        ],
        out_specs=pl.BlockSpec((width, 3 * tile), lambda f: (0, f)),
        out_shape=jax.ShapeDtypeStruct((width, 3 * hidden), BF),
        scratch_shapes=[pltpu.VMEM((width, rows), BF)] * 2,
        compiler_params=params(1),
        cost_estimate=pl.CostEstimate(
            flops=6 * rows * width * hidden,
            bytes_accessed=2 * (2 * rows * width + 3 * hidden * (rows + width)),
            transcendentals=0,
        ),
        name=name,
    )(x, d, hid)


def untile(array, n):
    hidden = array.shape[-1] // 3
    tile = tile_of(hidden)
    parts = [
        array[..., (3 * j + n) * tile : (3 * j + n + 1) * tile] for j in range(hidden // tile)
    ]
    return jnp.concatenate(parts, axis=-1)


def per_device(
    inputs,
    cotangent,
    lengths,
    block_pairs,
    routes,
    attn_gain,
    query_weight,
    key_weight,
    value_weight,
    out_weight,
    ffn_gain,
    router_weight,
    expert_gate,
    expert_up,
    expert_down,
    dense_gate,
    dense_up,
    dense_down,
):
    pair_rows, seqs, width = inputs.shape[1:]
    members, size = lax.axis_size("ctx"), lax.axis_size("wt")
    ctx, w = lax.axis_index("ctx"), lax.axis_index("wt")
    experts = expert_gate.shape[0]
    block = pair_rows // 2
    chunk = block // size
    rows = 2 * chunk * seqs
    inner = query_weight.shape[1] * size
    heads = inner // HEAD_DIM
    units = -(-(seqs * heads) // members)

    def rows_of(array, k):
        parted = array.reshape(2, size, chunk, seqs, -1)
        mine = lax.dynamic_index_in_dim(parted, (w + k) % size, 1, False)
        return mine.transpose(2, 0, 1, 3).reshape(seqs, 2 * chunk, -1)

    def places_of(k):
        pair = lax.dynamic_index_in_dim(block_pairs, ctx, 0, False)
        blocks = jnp.stack([pair, 2 * members - 1 - pair])
        core = (w + k) % size
        return (blocks[:, None] * block + core * chunk + jnp.arange(chunk)[None, :]).reshape(-1)

    x = rows_of(inputs[0], 0)
    half = HEAD_DIM // 2
    lane = jnp.arange(LANES)
    freqs = THETA ** (-(lane % half).astype(F4) / half)
    angles = places_of(0).astype(F4)[:, None] * freqs[None, :]
    cosine = jnp.cos(angles)
    sine = jnp.sin(angles) * jnp.where(lane % HEAD_DIM < half, -1.0, 1.0)[None, :]

    local = inner // size
    split = size == 2 and local % LANES == 0
    shift = (w * (heads // size) if split else jnp.zeros_like(w)).astype(jnp.int32)[None]
    own_qkv = [query_weight, key_weight, value_weight]
    if split:
        parts = list(zip(*[wt_gather(weight) for weight in own_qkv]))
        out_parts = wt_gather(out_weight)
    else:
        parts = [[lax.all_gather(weight, "wt", axis=1, tiled=True) for weight in own_qkv]]
        out_parts = [lax.all_gather(out_weight, "wt", axis=0, tiled=True)]
    x, cosine, sine = lax.optimization_barrier((x, cosine, sine))
    msg, a1 = project(shift, x, attn_gain[None], cosine, sine, parts, members, units)
    msg, cotangent, routes = lax.optimization_barrier((msg, cotangent, routes))
    got = lax.all_to_all(msg, "ctx", 0, 0, tiled=True)

    near = 4 if members % 4 == 0 else 1
    outer = members // near
    near_groups = [[o * near + i for i in range(near)] for o in range(outer)]
    far_groups = [[o * near + i for o in range(outer)] for i in range(near)]

    def by_steps(array):
        array = array.reshape(outer, near, width // members, -1).swapaxes(0, 1)
        return array.reshape(width, -1)

    def near_scatter(array):
        return lax.psum_scatter(
            array, "ctx", scatter_dimension=0, tiled=True, axis_index_groups=near_groups
        )

    def far_scatter(array):
        return lax.psum_scatter(
            array, "ctx", scatter_dimension=0, tiled=True, axis_index_groups=far_groups
        )

    a1_turned, back_parts, out_back = turn(a1.reshape(rows, width), parts, out_parts)
    a1_turned = by_steps(a1_turned)
    expert = ctx % experts
    expert_parts = list(
        zip(
            *[
                wt_gather(lax.dynamic_index_in_dim(weights, expert, 0, False))
                for weights in (expert_gate, expert_up, expert_down)
            ]
        )
    )
    total_rows = rows * size
    cots = []
    for k in range(size):
        valid = places_of(k)[None, :] < lengths[:, None]
        cots.append(
            jnp.where(valid[:, :, None], rows_of(cotangent[0], k), jnp.zeros((), BF)).reshape(
                rows, width
            )
        )
    cot = jnp.concatenate(cots)

    parted = routes[0].reshape(2, size, chunk, seqs, 2).transpose(1, 3, 0, 2, 4)
    chosen_all = parted.reshape(total_rows, 2)
    names = jnp.arange(experts, dtype=jnp.int32)
    picks_all = chosen_all[:, :, None] == names
    marks = jnp.any(picks_all, axis=1).astype(BF)
    index = jnp.arange(total_rows)
    before = dot((index[None, :] < index[:, None]).astype(BF), marks)
    order_all = jnp.sum(jnp.where(picks_all, before[:, None, :], 0.0), axis=-1).astype(jnp.int32)
    share = -(-CAPACITY // size)
    held = -(-share // 16) * 16

    def targets(chosen, order, core):
        inside = (order >= core * held) & (order < (core + 1) * held)
        return jnp.where(inside, chosen * held + order - core * held, -1)

    def own_first(array):
        pieces = array.reshape(size, rows, 2)
        pieces = jnp.concatenate([pieces, pieces[:-1]])
        return lax.dynamic_slice_in_dim(pieces, w, size, 0).reshape(total_rows, 2)

    chosen, order_here = own_first(chosen_all), own_first(order_all)
    target = targets(chosen, order_here, w)
    own_targets = [
        targets(chosen[:rows], order_here[:rows], (w + k) % size) for k in range(size)
    ]
    own_info = jnp.concatenate(own_targets + [chosen[:rows]], axis=1)
    own_info = own_info.reshape(seqs, 2 * chunk, -1)
    info = jnp.concatenate([target, chosen, jnp.zeros((total_rows, 4), jnp.int32)], axis=1).T
    router_wide = jnp.pad(router_weight, ((0, 0), (0, LANES - experts)))
    router_turned = router_weight.T
    inv = jnp.argsort(block_pairs).astype(jnp.int32)
    unit_slots = jnp.minimum((ctx + members * jnp.arange(units)) // heads, seqs - 1)
    unit_lengths = lengths[unit_slots]
    w_arg = w.astype(jnp.int32)[None]
    groups = None
    if members != experts:
        groups = [[g * experts + e for e in range(experts)] for g in range(members // experts)]
    swap = functools.partial(
        lax.all_to_all,
        axis_name="ctx",
        split_axis=0,
        concat_axis=0,
        axis_index_groups=groups,
        tiled=True,
    )

    early = dispatch(
        dispatch_early_kernel, info, [cot], width + LANES, experts, held, "dispatch_early"
    )
    (
        got,
        early,
        a1_turned,
        back_parts,
        out_back,
        expert_parts,
        cots,
        cot,
        own_info,
        info,
        router_wide,
        router_turned,
        inv,
        unit_lengths,
    ) = (
        lax.optimization_barrier(
            (
                got,
                early,
                a1_turned,
                back_parts,
                out_back,
                expert_parts,
                cots,
                cot,
                own_info,
                info,
                router_wide,
                router_turned,
                inv,
                unit_lengths,
            )
        )
    )

    blocks = wt_gather(got)
    early = swap(early)
    o_msg, kept, stats = attend(inv, unit_lengths, w_arg, blocks, units)
    o_msg, early = lax.optimization_barrier((o_msg, early))
    o_got = lax.all_to_all(o_msg, "ctx", 0, 0, tiled=True)
    mixed, state, second_own = mix(shift, o_got, x, ffn_gain[None], out_parts)

    seconds = wt_gather(second_own.reshape(rows, width))
    sent = dispatch(dispatch_kernel, info, seconds, width, experts, held, "dispatch")

    sent, seconds = lax.optimization_barrier((sent, seconds))
    second = jnp.concatenate(seconds)
    arrived = swap(sent)
    dense, dense_hid = gated(second, cot, [[dense_gate, dense_up, dense_down]], F4, "dense_branch")
    dense_grads = gated_grads(second, cot, dense_hid, 0, 1, "dense_grads")
    dense_grads = by_steps(dense_grads)
    denses = [dense[:rows]]
    for k in range(1, size):
        perm = [(i, (i + k) % size) for i in range(size)]
        denses.append(lax.ppermute(dense[k * rows : (k + 1) * rows], "wt", perm))
    arrived, denses, dense_grads = lax.optimization_barrier((arrived, denses, dense_grads))
    dense = denses[0]
    for part in denses[1:]:
        dense = dense + part
    dense_near = near_scatter(dense_grads)

    arrived = arrived.reshape(experts * held, width)
    dye, returned, hid = gated(
        arrived,
        early.reshape(experts * held, -1),
        expert_parts,
        BF,
        "expert_branch",
        (expert.astype(jnp.int32)[None], router_wide),
    )
    home = swap(returned.reshape(experts, held, 2 * width))
    hidden = expert_gate.shape[2]
    expert_sum = None
    for k in list(range(1, size)) + [0]:
        made = gated_grads(arrived, dye, hid, k, size, "expert_grads")
        if k:
            made = lax.ppermute(made, "wt", [(i, (i + k) % size) for i in range(size)])
        expert_sum = made.astype(F4) if expert_sum is None else expert_sum + made.astype(F4)
    expert_sum = expert_sum.astype(BF).reshape(members, width // members, 3 * hidden)
    cut = 3 * hidden // 2
    expert_sum = [expert_sum[:, :, :cut], expert_sum[:, :, cut:]]
    home, expert_sum, dense_near, dense = lax.optimization_barrier(
        (home, expert_sum, dense_near, dense)
    )
    dense_sum = far_scatter(dense_near)
    homes = wt_gather(home.reshape(experts * held, 2 * width))
    first = first_part(own_info, homes[0])

    own_cot = cots[0].reshape(seqs, 2 * chunk, width)
    dense = dense.reshape(seqs, 2 * chunk, 2 * width)
    output, dstate, dstate_low, logit_back, do_msg, ffn_grad = finish(
        shift,
        own_info,
        second_own,
        state,
        own_cot,
        ffn_gain[None],
        router_wide,
        router_turned,
        homes[1:],
        first,
        dense,
        out_back,
        members,
        units,
    )
    do_got = lax.all_to_all(do_msg, "ctx", 0, 0, tiled=True)

    def share_of(array, kinds, k):
        if split:
            return array[..., k * kinds * local : (k + 1) * kinds * local].reshape(rows, -1)
        cols = array.reshape(rows, kinds, size, local)
        return lax.dynamic_index_in_dim(cols, (w + k) % size, 2, False).reshape(rows, -1)

    def split_wt(left, right, kinds):
        pieces = []
        for k in range(size):
            made = dot_tn(left.reshape(rows, -1), share_of(right, kinds, k))
            pieces.append(made if k == 0 else made.astype(BF))
        return wt_scatter(pieces).astype(BF)

    router_grad = dot_tn(second_own.reshape(rows, width), logit_back.reshape(rows, experts))
    small = wt_sum(jnp.concatenate([ffn_grad.T, router_grad], axis=1))
    small_high = small.astype(BF)
    small_low = (small - small_high.astype(F4)).astype(BF)
    few = experts + 1
    blank = jnp.zeros((width, -(2 * few) % LANES), BF)
    out_msg = [split_wt(dstate_low, mixed, 1), small_high, small_low, blank]
    out_msg = by_steps(jnp.concatenate(out_msg, axis=1))
    do_got, out_msg, output, dense_sum, expert_sum = lax.optimization_barrier(
        (do_got, out_msg, output, dense_sum, expert_sum)
    )
    expert_got = [lax.all_to_all(expert_sum[0], "ctx", 0, 0, tiled=True)]
    out_near = near_scatter(out_msg)
    dq, *dkv = attend_back(inv, unit_lengths, w_arg, blocks, do_got, kept, stats, units)
    dq, dkv, expert_got, out_near = lax.optimization_barrier((dq, dkv, expert_got, out_near))
    out_sum = far_scatter(out_near)
    dkv = wt_scatter(dkv).astype(BF)
    grad_msg = jnp.concatenate([dkv, dq], axis=1)
    grad_got = lax.all_to_all(grad_msg, "ctx", 0, 0, tiled=True)
    grad_got, out_sum, expert_sum = lax.optimization_barrier((grad_got, out_sum, expert_sum))
    expert_got.append(lax.all_to_all(expert_sum[1], "ctx", 0, 0, tiled=True))
    count = len(parts)
    dqkv, last_msg = [None] * count, None
    for k in list(range(1, count)) + [0]:
        dqkv[k], made = unrotate(shift, grad_got, cosine, sine, a1_turned, seqs, heads, k, count)
        if k:
            made = lax.ppermute(made, "wt", [(i, (i + k) % size) for i in range(size)])
        last_msg = made.astype(F4) if last_msg is None else last_msg + made.astype(F4)
    if split:
        last_msg = last_msg.astype(BF)
    else:
        last_msg = by_steps(split_wt(a1, dqkv[0], 3))
    last_sum = far_scatter(near_scatter(last_msg))
    dx, attn_grad = unproject(shift, dqkv, x, dstate, attn_gain[None], back_parts)
    attn_grad = ctx_sum(wt_sum(attn_grad)).reshape(members, -1)
    attn_grad = lax.dynamic_index_in_dim(attn_grad, ctx, 0, False)
    expert_grads = place(expert_got, experts)
    last_sum = last_sum.astype(F4)
    out_sum = out_sum.astype(F4)
    tail = out_sum[:, local:]
    tail = tail[:, :few] + tail[:, few : 2 * few]

    def to_tokens(own):
        array = in_order(wt_gather(own)).reshape(size, seqs, 2, chunk, width)
        return array.transpose(2, 0, 3, 1, 4).reshape(inputs.shape)

    return (
        to_tokens(output),
        to_tokens(dx),
        attn_grad,
        *[last_sum[:, n * local : (n + 1) * local] for n in range(3)],
        out_sum[:, :local].T,
        tail[:, 0],
        tail[:, 1:],
        *expert_grads[:2],
        expert_grads[2].transpose(0, 2, 1),
        *[untile(dense_sum, n).astype(F4) for n in range(2)],
        untile(dense_sum, 2).astype(F4).T,
    )


def solution(mesh):
    placed = (
        P("ctx", None, None, None),
        P("ctx", None, None, None),
        P(),
        P(),
        P("ctx", None, None, None),
        P(),
        P(None, "wt"),
        P(None, "wt"),
        P(None, "wt"),
        P("wt", None),
        P(),
        P(),
        P(None, None, "wt"),
        P(None, None, "wt"),
        P(None, "wt", None),
        P(None, "wt"),
        P(None, "wt"),
        P("wt", None),
    )
    return jax.shard_map(
        per_device,
        mesh=mesh,
        in_specs=placed,
        out_specs=(
            P("ctx", None, None, None),
            P("ctx", None, None, None),
            P("ctx"),
            P("ctx", "wt"),
            P("ctx", "wt"),
            P("ctx", "wt"),
            P("wt", "ctx"),
            P("ctx"),
            P("ctx", None),
            P(None, "ctx", "wt"),
            P(None, "ctx", "wt"),
            P(None, "wt", "ctx"),
            P("ctx", "wt"),
            P("ctx", "wt"),
            P("wt", "ctx"),
        ),
        check_vma=False,
    )
```

```python
import functools

import jax
import jax.numpy as jnp
from jax import lax
from jax.experimental import pallas as pl
from jax.experimental.pallas import tpu as pltpu
from jax.sharding import PartitionSpec as P

HEAD_DIM = 64
CAPACITY = 160
EPS = 1e-06
THETA = 10000.0
LANES = 128
BF = jnp.bfloat16
F4 = jnp.float32
TQ = 512
TK = 1024
VMEM_LIMIT = 56 * 1024 * 1024


def dot(a, b):
    return jnp.dot(a, b, preferred_element_type=F4)


def dot_nt(a, b):
    return lax.dot_general(a, b, (((1,), (1,)), ((), ())), preferred_element_type=F4)


def dot_tn(a, b):
    return lax.dot_general(a, b, (((0,), (0,)), ((), ())), preferred_element_type=F4)


def wt_gather(x):
    size = lax.axis_size("wt")
    return [x] + [
        lax.ppermute(x, "wt", [(i, (i - k) % size) for i in range(size)]) for k in range(1, size)
    ]


def wt_scatter(pieces):
    size = lax.axis_size("wt")
    total = pieces[0]
    for k in range(1, size):
        moved = lax.ppermute(pieces[k], "wt", [(i, (i + k) % size) for i in range(size)])
        total = total + moved.astype(total.dtype)
    return total


def wt_sum(x):
    if lax.axis_size("wt") == 2:
        return x + lax.ppermute(x, "wt", [(0, 1), (1, 0)])
    return lax.psum(x, "wt")


def ctx_sum(x):
    size = lax.axis_size("ctx")
    if size & (size - 1):
        return lax.psum(x, "ctx")
    by = 1
    while by < size:
        x = x + lax.ppermute(x, "ctx", [(i, i ^ by) for i in range(size)])
        by *= 2
    return x


def in_order(parts):
    size = len(parts)
    start = (size - lax.axis_index("wt")) % size
    return lax.dynamic_slice_in_dim(jnp.stack(parts + parts[:-1]), start, size, 0)


def lane_of(shape):
    return lax.broadcasted_iota(jnp.int32, shape, len(shape) - 1)


def pair_swap(a, b):
    low = lane_of(a.shape) < HEAD_DIM
    return (
        jnp.where(low, a, pltpu.roll(b, HEAD_DIM, 1)),
        jnp.where(low, pltpu.roll(a, HEAD_DIM, 1), b),
    )


def turn_halves(t):
    first = lane_of(t.shape) % HEAD_DIM < HEAD_DIM // 2
    return jnp.where(
        first,
        pltpu.roll(t, LANES - HEAD_DIM // 2, 1),
        pltpu.roll(t, HEAD_DIM // 2, 1),
    )


def params(count):
    return pltpu.CompilerParams(
        vmem_limit_bytes=VMEM_LIMIT, dimension_semantics=("arbitrary",) * count
    )


def whole(shape):
    return pl.BlockSpec(shape, lambda *i: (0,) * len(shape))


def head_units(seqs, heads, members, shift, s, rel):
    unit = s * heads + lax.rem(rel + shift, heads)
    return lax.rem(unit, members), lax.div(unit, members)


def project_kernel(heads, units, members, count, shift_ref, x_ref, gain_ref, cos_ref, sin_ref, *refs):
    w_refs = refs[: 3 * count]
    msg_ref, a1_ref = refs[3 * count :]
    seqs, rows, width = x_ref.shape
    chunk = rows // 2
    for s in range(seqs):
        x = x_ref[s].astype(F4)
        scale = lax.rsqrt(jnp.mean(x * x, axis=-1, keepdims=True) + EPS)
        a1_ref[s] = (x * scale * gain_ref[...]).astype(BF)
    if units * members > heads * seqs:
        msg_ref[...] = jnp.zeros_like(msg_ref)
    a1 = a1_ref[...].reshape(seqs * rows, width)
    cosine, sine = cos_ref[...], sin_ref[...]

    def rope(t):
        return t * cosine + turn_halves(t) * sine

    per = heads // count
    for k in range(count):
        query, key, value = (dot(a1, ref[...]) for ref in w_refs[3 * k : 3 * k + 3])
        for s in range(seqs):
            mine = slice(s * rows, (s + 1) * rows)
            for g in range(per // 2):
                part = slice(g * LANES, (g + 1) * LANES)
                pairs = pair_swap(rope(key[mine, part]), value[mine, part])
                turned = rope(query[mine, part])
                asked = pair_swap(turned[:chunk], turned[chunk:])
                for c in range(2):
                    chip, u = head_units(
                        seqs, heads, members, shift_ref[0], s, k * per + 2 * g + c
                    )
                    msg_ref[chip, 3 * u] = pairs[c][:chunk].astype(BF)
                    msg_ref[chip, 3 * u + 1] = pairs[c][chunk:].astype(BF)
                    msg_ref[chip, 3 * u + 2] = asked[c].astype(BF)


SMEM = pl.BlockSpec(memory_space=pltpu.SMEM)


def one_step(kernel, name, shift, arrays, shapes):
    return pl.pallas_call(
        kernel,
        grid=(1,),
        in_specs=[SMEM] + [whole(array.shape) for array in arrays],
        out_specs=[whole(shape.shape) for shape in shapes],
        out_shape=shapes,
        compiler_params=params(1),
        name=name,
    )(shift, *arrays)


def project(shift, x, gain, cosine, sine, parts, members, units):
    seqs, rows, width = x.shape
    count = len(parts)
    heads = sum(part[0].shape[1] for part in parts) // HEAD_DIM
    flat = [w for part in parts for w in part]
    return one_step(
        functools.partial(project_kernel, heads, units, members, count),
        "project",
        shift,
        [x, gain, cosine, sine, *flat],
        [
            jax.ShapeDtypeStruct((members, 3 * units, rows // 2, LANES), BF),
            jax.ShapeDtypeStruct((seqs, rows, width), BF),
        ],
    )


def turn_kernel(count, shift_ref, *refs):
    (a1_ref, *ins), (a1t_ref, *outs) = refs[: 1 + 4 * count], refs[1 + 4 * count :]
    a1t_ref[...] = a1_ref[...].T
    for k in range(count):
        inner = ins[4 * k].shape[1]
        for n in range(3):
            outs[2 * k][n * inner : (n + 1) * inner, :] = ins[4 * k + n][...].T
        outs[2 * k + 1][...] = ins[4 * k + 3][...].T


def turn(a1, parts, out_parts):
    rows, width = a1.shape
    ins = [a1]
    shapes = [jax.ShapeDtypeStruct((width, rows), BF)]
    for part, out_part in zip(parts, out_parts):
        ins += [*part, out_part]
        inner = out_part.shape[0]
        shapes += [
            jax.ShapeDtypeStruct((3 * inner, width), BF),
            jax.ShapeDtypeStruct((width, inner), BF),
        ]
    made = one_step(
        functools.partial(turn_kernel, len(parts)), "turn", jnp.zeros((1,), jnp.int32), ins, shapes
    )
    return made[0], list(made[1::2]), list(made[2::2])


def gather_keys(inv_ref, w, kv_refs, kv_s, members, chunk):
    size = len(kv_refs)
    for block in range(2 * members):
        half = 0 if block < members else 1
        chip = inv_ref[block if half == 0 else 2 * members - 1 - block]
        for k, ref in enumerate(kv_refs):
            core = lax.rem(w + k, size)
            start = pl.multiple_of(block * size * chunk + core * chunk, chunk)
            kv_s[pl.ds(start, chunk), :] = ref[chip, half]


def gather_rows(inv_ref, read, put, members, to_high):
    for block in range(2 * members):
        half = 0 if block < members else 1
        chip = inv_ref[block if half == 0 else 2 * members - 1 - block]
        rows = read(chip).astype(F4)
        if (half == 1) != to_high:
            rows = pltpu.roll(rows, HEAD_DIM, 1)
        low = lane_of(rows.shape) < HEAD_DIM
        rows = jnp.where(low, 0.0, rows) if to_high else jnp.where(low, rows, 0.0)
        put(block, rows)


def attend_kernel(members, size, inv_ref, len_ref, w_ref, *refs):
    kv_refs = refs[:size]
    o_ref, of_ref, stat_ref = refs[size : size + 3]
    kv_s, vt_s, q_s, o_s, s_s = refs[size + 3 :]
    u = pl.program_id(0)
    chunk = kv_refs[0].shape[2]
    own_rows = q_s.shape[0]
    slot = kv_s.shape[0]
    w = w_ref[0]
    length = len_ref[u]
    gather_keys(inv_ref, w, kv_refs, kv_s, members, chunk)

    def put(block, rows):
        q_s[block * chunk : (block + 1) * chunk, :] = rows * HEAD_DIM ** (-0.5)

    gather_rows(inv_ref, lambda chip: kv_refs[0][chip, 2], put, members, False)

    def flip(i, carry):
        tile = kv_s[pl.ds(pl.multiple_of(i * TK, TK), TK), :].astype(F4)
        vt_s[i] = tile.T[HEAD_DIM:].astype(BF)
        return carry

    lax.fori_loop(0, slot // TK, flip, 0)
    span = TQ * size

    def row_tile(t, carry):
        row = pl.multiple_of(t * TQ, TQ)
        qt = q_s[pl.ds(row, TQ), :].T.astype(BF)
        index = lax.broadcasted_iota(jnp.int32, (1, TQ), 1)
        place = t * span + (index // chunk) * (size * chunk) + w * chunk + index % chunk
        limit = jnp.minimum(place, length - 1)

        def first_step(masked, kt, top):
            start = pl.multiple_of(kt * TK, TK)
            scores = dot(kv_s[pl.ds(start, TK), :], qt)
            if masked:
                keys = kt * TK + lax.broadcasted_iota(jnp.int32, (TK, 1), 0)
                scores = jnp.where(keys <= limit, scores, -1e30)
            s_s[kt] = scores
            return jnp.maximum(top, jnp.max(scores.reshape(TK // 8, 8, TQ), axis=0))

        def second_step(kt, state):
            total, acc = state
            weights = jnp.exp(s_s[kt] - top)
            total = total + jnp.sum(weights.reshape(TK // 8, 8, TQ), axis=0)
            return total, acc + dot(vt_s[kt], weights.astype(BF))

        clear = jnp.minimum(t * span, length) // TK
        last = jnp.minimum(pl.cdiv((t + 1) * span, TK), pl.cdiv(length, TK))
        top = jnp.full((8, TQ), -1e30, F4)
        top = lax.fori_loop(0, clear, functools.partial(first_step, False), top)
        top = lax.fori_loop(clear, last, functools.partial(first_step, True), top)
        top = jnp.max(top, axis=0, keepdims=True)
        state = (jnp.zeros((8, TQ), F4), jnp.zeros((HEAD_DIM, TQ), F4))
        total, acc = lax.fori_loop(0, last, second_step, state)
        total = jnp.sum(total, axis=0, keepdims=True)
        result = acc / total
        of_ref[0, t] = result
        stat_ref[0, t, 0:1] = top
        stat_ref[0, t, 1:2] = 1.0 / total
        blank = jnp.zeros_like(result)
        first = 2 * t * TQ < own_rows
        both = jnp.concatenate(
            [jnp.where(first, result, blank), jnp.where(first, blank, result)], axis=0
        )
        o_s[pl.ds(row, TQ), :] = both.T
        return carry

    lax.fori_loop(0, own_rows // TQ, row_tile, 0)
    for b in range(members):
        other = 2 * members - 1 - b
        rows = (
            o_s[b * chunk : (b + 1) * chunk, :] + o_s[other * chunk : (other + 1) * chunk, :]
        )
        o_ref[inv_ref[b], 0] = rows.astype(BF)


def attend(inv, lengths, w, blocks, units):
    members, _, chunk, _ = blocks[0].shape
    size = len(blocks)
    slot = 2 * members * chunk * size
    rows = 2 * members * chunk
    spec = pl.BlockSpec((members, 3, chunk, LANES), lambda u, *_: (0, u, 0, 0))
    return pl.pallas_call(
        functools.partial(attend_kernel, members, size),
        grid_spec=pltpu.PrefetchScalarGridSpec(
            num_scalar_prefetch=3,
            grid=(units,),
            in_specs=[spec] * size,
            out_specs=[
                pl.BlockSpec((members, 1, chunk, LANES), lambda u, *_: (0, u, 0, 0)),
                pl.BlockSpec((1, rows // TQ, HEAD_DIM, TQ), lambda u, *_: (u, 0, 0, 0)),
                pl.BlockSpec((1, rows // TQ, 2, TQ), lambda u, *_: (u, 0, 0, 0)),
            ],
            scratch_shapes=[
                pltpu.VMEM((slot, LANES), BF),
                pltpu.VMEM((slot // TK, HEAD_DIM, TK), BF),
                pltpu.VMEM((rows, LANES), F4),
                pltpu.VMEM((rows, LANES), F4),
                pltpu.VMEM((slot // TK, TK, TQ), F4),
            ],
        ),
        out_shape=[
            jax.ShapeDtypeStruct((members, units, chunk, LANES), BF),
            jax.ShapeDtypeStruct((units, rows // TQ, HEAD_DIM, TQ), F4),
            jax.ShapeDtypeStruct((units, rows // TQ, 2, TQ), F4),
        ],
        compiler_params=params(1),
        name="attend",
    )(inv, lengths, w, *blocks)


def attend_back_kernel(members, size, inv_ref, len_ref, w_ref, *refs):
    kv_refs = refs[:size]
    do_ref, of_ref, stat_ref = refs[size : size + 3]
    dq_ref = refs[size + 3]
    dkv_refs = refs[size + 4 : 2 * size + 4]
    kv_s, kt_s, q_s, do_s, dq_s, dkv_s = refs[2 * size + 4 :]
    u = pl.program_id(0)
    chunk = kv_refs[0].shape[2]
    own_rows = q_s.shape[0]
    slot = kv_s.shape[0]
    w = w_ref[0]
    length = len_ref[u]
    gather_keys(inv_ref, w, kv_refs, kv_s, members, chunk)

    def put_q(block, rows):
        q_s[block * chunk : (block + 1) * chunk, :] = rows * HEAD_DIM ** (-0.5)

    def put_do(block, rows):
        do_s[block * chunk : (block + 1) * chunk, :] = rows

    gather_rows(inv_ref, lambda chip: kv_refs[0][chip, 2], put_q, members, False)
    gather_rows(inv_ref, lambda chip: do_ref[chip, 0], put_do, members, True)

    def flip(i, carry):
        tile = kv_s[pl.ds(pl.multiple_of(i * TK, TK), TK), :].astype(F4)
        kt_s[i] = tile.T[:HEAD_DIM].astype(BF)
        return carry

    lax.fori_loop(0, slot // TK, flip, 0)
    dkv_s[...] = jnp.zeros_like(dkv_s)
    dq_s[...] = jnp.zeros_like(dq_s)
    span = TQ * size

    def row_tile(t, carry):
        row = pl.multiple_of(t * TQ, TQ)
        q_rows = q_s[pl.ds(row, TQ), :]
        do_rows = do_s[pl.ds(row, TQ), :]
        qt, dot_ = q_rows.T, do_rows.T
        delta = jnp.sum(dot_[HEAD_DIM:] * of_ref[0, t], axis=0, keepdims=True)
        qt, dot_ = qt.astype(BF), dot_.astype(BF)
        stacked = jnp.concatenate([do_rows.astype(BF), q_rows.astype(BF)], axis=0)
        top, share = stat_ref[0, t, 0:1], stat_ref[0, t, 1:2]
        index = lax.broadcasted_iota(jnp.int32, (1, TQ), 1)
        place = t * span + (index // chunk) * (size * chunk) + w * chunk + index % chunk
        limit = jnp.minimum(place, length - 1)

        def step(masked, kt, dqt):
            start = pl.multiple_of(kt * TK, TK)
            kv = kv_s[pl.ds(start, TK), :]
            weights = jnp.exp(dot(kv, qt) - top) * share
            if masked:
                keys = kt * TK + lax.broadcasted_iota(jnp.int32, (TK, 1), 0)
                weights = jnp.where(keys <= limit, weights, 0.0)
            pulled = dot(kv, dot_)
            back = (weights * (pulled - delta)).astype(BF)
            dkv_s[pl.ds(start, TK), :] += dot(
                jnp.concatenate([weights.astype(BF), back], axis=1), stacked
            )
            return dqt + dot(kt_s[kt], back)

        clear = jnp.minimum(t * span, length) // TK
        last = jnp.minimum(pl.cdiv((t + 1) * span, TK), pl.cdiv(length, TK))
        dqt = jnp.zeros((HEAD_DIM, TQ), F4)
        dqt = lax.fori_loop(0, clear, functools.partial(step, False), dqt)
        dqt = lax.fori_loop(clear, last, functools.partial(step, True), dqt)
        dqt = dqt * HEAD_DIM ** (-0.5)
        blank = jnp.zeros_like(dqt)
        first = 2 * t * TQ < own_rows
        both = jnp.concatenate(
            [jnp.where(first, dqt, blank), jnp.where(first, blank, dqt)], axis=0
        )
        dq_s[pl.ds(row, TQ), :] = both.T
        return carry

    lax.fori_loop(0, jnp.minimum(pl.cdiv(length, span), own_rows // TQ), row_tile, 0)
    for b in range(members):
        other = 2 * members - 1 - b
        chip = inv_ref[b]
        rows = (
            dq_s[b * chunk : (b + 1) * chunk, :] + dq_s[other * chunk : (other + 1) * chunk, :]
        )
        dq_ref[chip, 0] = rows.astype(BF)
        for half, block in ((0, b), (1, other)):
            for k, ref in enumerate(dkv_refs):
                core = lax.rem(w + k, size)
                start = pl.multiple_of(block * size * chunk + core * chunk, chunk)
                ref[chip, half] = dkv_s[pl.ds(start, chunk), :].astype(ref.dtype)


def attend_back(inv, lengths, w, blocks, do_msg, kept, stats, units):
    members, _, chunk, _ = blocks[0].shape
    size = len(blocks)
    slot = 2 * members * chunk * size
    rows = 2 * members * chunk
    spec = pl.BlockSpec((members, 3, chunk, LANES), lambda u, *_: (0, u, 0, 0))
    one = pl.BlockSpec((members, 1, chunk, LANES), lambda u, *_: (0, u, 0, 0))
    two = pl.BlockSpec((members, 2, chunk, LANES), lambda u, *_: (0, u, 0, 0))
    return pl.pallas_call(
        functools.partial(attend_back_kernel, members, size),
        grid_spec=pltpu.PrefetchScalarGridSpec(
            num_scalar_prefetch=3,
            grid=(units,),
            in_specs=[spec] * size
            + [
                one,
                pl.BlockSpec((1, rows // TQ, HEAD_DIM, TQ), lambda u, *_: (u, 0, 0, 0)),
                pl.BlockSpec((1, rows // TQ, 2, TQ), lambda u, *_: (u, 0, 0, 0)),
            ],
            out_specs=[one] + [two] * size,
            scratch_shapes=[
                pltpu.VMEM((slot, LANES), BF),
                pltpu.VMEM((slot // TK, HEAD_DIM, TK), BF),
                pltpu.VMEM((rows, LANES), F4),
                pltpu.VMEM((rows, LANES), F4),
                pltpu.VMEM((rows, LANES), F4),
                pltpu.VMEM((slot, LANES), F4),
            ],
        ),
        out_shape=[jax.ShapeDtypeStruct((members, units, chunk, LANES), BF)]
        + [
            jax.ShapeDtypeStruct((members, 2 * units, chunk, LANES), BF) for k in range(size)
        ],
        compiler_params=params(1),
        name="attend_back",
    )(inv, lengths, w, *blocks, do_msg, kept, stats)


def mix_kernel(heads, count, shift_ref, o_ref, x_ref, gain_ref, *refs):
    w_refs = refs[:count]
    mixed_ref, state_ref, a2_ref = refs[count:]
    members, _, chunk, _ = o_ref.shape
    seqs, rows, width = x_ref.shape
    for s in range(seqs):
        for g in range(heads // 2):
            pair = []
            for c in range(2):
                chip, u = head_units(seqs, heads, members, shift_ref[0], s, 2 * g + c)
                pair.append(o_ref[chip, u].astype(F4))
            early, late = pair_swap(*pair)
            part = slice(g * LANES, (g + 1) * LANES)
            mixed_ref[s, :chunk, part] = early.astype(BF)
            mixed_ref[s, chunk:, part] = late.astype(BF)
    inner = heads * HEAD_DIM // count
    made = 0.0
    for k in range(count):
        mixed = mixed_ref[:, :, k * inner : (k + 1) * inner].reshape(seqs * rows, inner)
        made = made + dot(mixed, w_refs[k][...])
    for s in range(seqs):
        state = x_ref[s].astype(F4) + made[s * rows : (s + 1) * rows]
        state_ref[s] = state
        scale = lax.rsqrt(jnp.mean(state * state, axis=-1, keepdims=True) + EPS)
        a2_ref[s] = (state * scale * gain_ref[...]).astype(BF)


def mix(shift, o_msg, x, gain, parts):
    seqs, rows, width = x.shape
    inner = sum(part.shape[0] for part in parts)
    return one_step(
        functools.partial(mix_kernel, inner // HEAD_DIM, len(parts)),
        "mix",
        shift,
        [o_msg, x, gain, *parts],
        [
            jax.ShapeDtypeStruct((seqs, rows, inner), BF),
            jax.ShapeDtypeStruct((seqs, rows, width), F4),
            jax.ShapeDtypeStruct((seqs, rows, width), BF),
        ],
    )


def norm_back(values, gain, upstream):
    scale = lax.rsqrt(jnp.mean(values * values, axis=-1, keepdims=True) + EPS)
    unit = values * scale
    pulled = upstream * gain
    result = scale * (pulled - unit * jnp.mean(pulled * unit, axis=-1, keepdims=True))
    return result, jnp.sum(upstream * unit, axis=0, keepdims=True)


def unrotate_kernel(heads, per, k, shift_ref, msg_ref, cos_ref, sin_ref, at_ref, dqkv_ref, grad_ref):
    members, triple, chunk, _ = msg_ref.shape
    units = triple // 3
    seqs, rows, _ = dqkv_ref.shape
    cosine, sine = cos_ref[...], sin_ref[...]
    inner = per * HEAD_DIM

    def rope_back(grad):
        return grad * cosine - turn_halves(grad) * sine

    for s in range(seqs):
        for g in range(per // 2):
            pair, asked = [], []
            for c in range(2):
                chip, u = head_units(seqs, heads, members, shift_ref[0], s, k * per + 2 * g + c)
                both = [msg_ref[chip, 2 * u], msg_ref[chip, 2 * u + 1]]
                pair.append(jnp.concatenate(both, axis=0).astype(F4))
                asked.append(msg_ref[chip, 2 * units + u].astype(F4))
            key, value = pair_swap(*pair)
            query = jnp.concatenate(pair_swap(*asked), axis=0)
            at = g * LANES
            dqkv_ref[s, :, at : at + LANES] = rope_back(query).astype(BF)
            at = at + inner
            dqkv_ref[s, :, at : at + LANES] = rope_back(key).astype(BF)
            at = at + inner
            dqkv_ref[s, :, at : at + LANES] = value.astype(BF)
    made = dot(at_ref[...], dqkv_ref[...].reshape(seqs * rows, 3 * inner))
    grad_ref[...] = made.astype(grad_ref.dtype)


def unrotate(shift, msg, cosine, sine, a1_turned, seqs, heads, k, count):
    rows = 2 * msg.shape[2]
    width = a1_turned.shape[0]
    per = heads // count
    inner = per * HEAD_DIM
    return one_step(
        functools.partial(unrotate_kernel, heads, per, k),
        "unrotate",
        shift,
        [msg, cosine, sine, a1_turned],
        [
            jax.ShapeDtypeStruct((seqs, rows, 3 * inner), BF),
            jax.ShapeDtypeStruct((width, 3 * inner), BF),
        ],
    )


def unproject_kernel(count, shift_ref, x_ref, dstate_ref, gain_ref, *refs):
    dqkv_refs, w_refs = refs[:count], refs[count : 2 * count]
    dx_ref, dgain_ref = refs[2 * count :]
    seqs, rows, width = x_ref.shape
    made = 0.0
    for dqkv_ref, w_ref in zip(dqkv_refs, w_refs):
        made = made + dot(dqkv_ref[...].reshape(seqs * rows, -1), w_ref[...])
    total = jnp.zeros((1, width), F4)
    for s in range(seqs):
        pulled, dgain = norm_back(
            x_ref[s].astype(F4), gain_ref[...], made[s * rows : (s + 1) * rows]
        )
        total = total + dgain
        dx_ref[s] = (dstate_ref[s] + pulled).astype(BF)
    dgain_ref[...] = total


def unproject(shift, dqkv, x, dstate, gain, parts):
    seqs, rows, width = x.shape
    return one_step(
        functools.partial(unproject_kernel, len(parts)),
        "unproject",
        shift,
        [x, dstate, gain, *dqkv, *parts],
        [
            jax.ShapeDtypeStruct((seqs, rows, width), BF),
            jax.ShapeDtypeStruct((1, width), F4),
        ],
    )


def two_gates(picked):
    top = jnp.maximum(*picked)
    raised = [jnp.exp(value - top) for value in picked]
    total = raised[0] + raised[1]
    return [value / total for value in raised]


def slot_hits(info_ref, count):
    shape = (count, info_ref.shape[1])
    ids = lax.broadcasted_iota(jnp.int32, shape, 0) + pl.program_id(0) * count
    return ids == info_ref[0:1, :], ids == info_ref[1:2, :]


def dispatch_kernel(info_ref, *refs):
    *second_refs, out_ref = refs
    count, held, width = out_ref.shape
    part = second_refs[0].shape[0]
    one, two = slot_hits(info_ref, count * held)
    hits = (one | two).astype(BF)
    routed = 0.0
    for k, ref in enumerate(second_refs):
        routed = routed + dot(hits[:, k * part : (k + 1) * part], ref[...])
    out_ref[...] = routed.astype(BF).reshape(count, held, width)


def dispatch_early_kernel(info_ref, cot_ref, out_ref):
    count, held, wide = out_ref.shape
    width = cot_ref.shape[1]
    one, two = slot_hits(info_ref, count * held)
    hits = (one | two).astype(BF)
    out_ref[:, :, :width] = dot(hits, cot_ref[...]).astype(BF).reshape(count, held, width)
    other = jnp.where(one, info_ref[3:4, :], 0) + jnp.where(two, info_ref[2:3, :], 0)
    other = jnp.sum(other.astype(F4), axis=1, keepdims=True)
    other = jnp.broadcast_to(other, (count * held, wide - width)).astype(BF)
    out_ref[:, :, width:] = other.reshape(count, held, wide - width)


def dispatch(kernel, info, arrays, wide, experts, held, name):
    count = 4 if experts % 4 == 0 else 1
    return pl.pallas_call(
        kernel,
        grid=(experts // count,),
        in_specs=[whole(array.shape) for array in (info, *arrays)],
        out_specs=pl.BlockSpec((count, held, wide), lambda e: (e, 0, 0)),
        out_shape=jax.ShapeDtypeStruct((experts, held, wide), BF),
        compiler_params=params(1),
        name=name,
    )(info, *arrays)


def two_gates(picked):
    top = jnp.maximum(*picked)
    raised = [jnp.exp(value - top) for value in picked]
    total = raised[0] + raised[1]
    return [value / total for value in raised]


def take_back(info, home_ref, k, width):
    target = info[:, 2 * k : 2 * k + 2]
    ids = lax.broadcasted_iota(jnp.int32, (info.shape[0], home_ref.shape[0]), 1)
    hits = [ids == target[:, c : c + 1] for c in range(2)]
    made = [dot(hit.astype(BF), home_ref[:, :width]) for hit in hits]
    return [*made, dot((hits[0] | hits[1]).astype(BF), home_ref[:, width:])]


def first_part_kernel(info_ref, home_ref, out_ref):
    take, rows, triple = out_ref.shape
    width = triple // 3
    info = info_ref[...].reshape(take * rows, info_ref.shape[2])
    for n, part in enumerate(take_back(info, home_ref, 0, width)):
        out_ref[:, :, n * width : (n + 1) * width] = part.reshape(take, rows, width)


def first_part(info, home):
    seqs, rows, cols = info.shape
    width = home.shape[1] // 2
    take = max(1, min(seqs, 256 // rows))
    return pl.pallas_call(
        first_part_kernel,
        grid=(seqs // take,),
        in_specs=[pl.BlockSpec((take, rows, cols), lambda s: (s, 0, 0)), whole(home.shape)],
        out_specs=pl.BlockSpec((take, rows, 3 * width), lambda s: (s, 0, 0)),
        out_shape=jax.ShapeDtypeStruct((seqs, rows, 3 * width), F4),
        compiler_params=params(1),
        name="first_part",
    )(info, home)


def finish_kernel(
    heads, size, count, shift_ref, info_ref, second_ref, state_ref, cot_ref, gain_ref, *refs
):
    router_ref, turned_ref, *refs = refs
    home_refs, refs = refs[: size - 1], refs[size - 1 :]
    first_ref, dense_ref, *refs = refs
    w_refs = refs[:count]
    out_ref, dstate_ref, low_ref, logit_ref, msg_ref, dgain_ref = refs[count:]
    step = pl.program_id(0)
    take, rows, width = state_ref.shape
    lines = take * rows
    members, units, chunk, _ = msg_ref.shape
    experts = turned_ref.shape[0]
    info = info_ref[...].reshape(lines, info_ref.shape[2])
    chosen = [info[:, 2 * size + c : 2 * size + c + 1] for c in range(2)]
    logits = dot(second_ref[...].reshape(lines, width), router_ref[...])[:, :experts]
    names = lax.broadcasted_iota(jnp.int32, (lines, experts), 1)
    gates = two_gates(
        [jnp.sum(jnp.where(names == pick, logits, 0.0), axis=1, keepdims=True) for pick in chosen]
    )
    first = first_ref[...].reshape(lines, 3 * width)
    *made, back = [first[:, n * width : (n + 1) * width] for n in range(3)]
    for k, home_ref in enumerate(home_refs):
        more = take_back(info, home_ref, k + 1, width)
        made = [a + b for a, b in zip(made, more)]
        back = back + more[2]
    cot = cot_ref[...].reshape(lines, width).astype(F4)
    pulled = [jnp.sum(y * cot, axis=-1, keepdims=True) for y in made]
    middle = gates[0] * pulled[0] + gates[1] * pulled[1]
    logit = 0.0
    for c in range(2):
        logit = logit + jnp.where(names == chosen[c], gates[c] * (pulled[c] - middle), 0.0)
    logit = logit.astype(BF)
    logit_ref[...] = logit.reshape(take, rows, experts)
    back = back + dot(logit, turned_ref[...])
    branch = gates[0] * made[0] + gates[1] * made[1]
    dense = dense_ref[...].reshape(lines, 2 * width)
    branch = branch + dense[:, :width]
    back = back + dense[:, width:]
    state = state_ref[...].reshape(lines, width)
    out_ref[...] = (state + branch).astype(BF).reshape(take, rows, width)
    pulled, dgain = norm_back(state, gain_ref[...], back)
    dstate = cot + pulled
    dstate_ref[...] = dstate.reshape(take, rows, width)
    low = dstate.astype(BF)
    low_ref[...] = low.reshape(take, rows, width)
    seqs = take * pl.num_programs(0)

    @pl.when(step == 0)
    def _():
        dgain_ref[...] = jnp.zeros_like(dgain_ref)
        if members * units > heads * seqs:
            msg_ref[...] = jnp.zeros_like(msg_ref)

    dgain_ref[...] += dgain
    per = heads // count
    for k in range(count):
        mixed_back = dot(low, w_refs[k][...])
        for s in range(take):
            for g in range(per // 2):
                part = mixed_back[s * rows : (s + 1) * rows, g * LANES : (g + 1) * LANES]
                pair = pair_swap(part[:chunk], part[chunk:])
                for c in range(2):
                    chip, u = head_units(
                        seqs, heads, members, shift_ref[0], step * take + s, k * per + 2 * g + c
                    )
                    msg_ref[chip, u] = pair[c].astype(BF)


def finish(shift, info, second, state, cot, gain, router, turned, homes, first, dense, parts, members, units):
    seqs, rows, width = state.shape
    inner = sum(part.shape[1] for part in parts)
    experts = turned.shape[0]
    take = max(1, min(seqs, 256 // rows))
    msg = (members, units, rows // 2, LANES)
    some = lambda cols: pl.BlockSpec((take, rows, cols), lambda s: (s, 0, 0))
    return pl.pallas_call(
        functools.partial(finish_kernel, inner // HEAD_DIM, len(homes) + 1, len(parts)),
        grid=(seqs // take,),
        in_specs=[SMEM, some(info.shape[2]), some(width), some(width), some(width)]
        + [whole((1, width)), whole(router.shape), whole(turned.shape)]
        + [whole(home.shape) for home in homes]
        + [some(3 * width), some(2 * width)]
        + [whole(part.shape) for part in parts],
        out_specs=[some(width)] * 3 + [some(experts), whole(msg), whole((1, width))],
        out_shape=[
            jax.ShapeDtypeStruct((seqs, rows, width), BF),
            jax.ShapeDtypeStruct((seqs, rows, width), F4),
            jax.ShapeDtypeStruct((seqs, rows, width), BF),
            jax.ShapeDtypeStruct((seqs, rows, experts), BF),
            jax.ShapeDtypeStruct(msg, BF),
            jax.ShapeDtypeStruct((1, width), F4),
        ],
        compiler_params=params(1),
        name="finish",
    )(shift, info, second, state, cot, gain, router, turned, *homes, first, dense, *parts)


def place_kernel(copies, cuts, *refs):
    whole_refs = refs[cuts * copies :]
    blocks = []
    for n in range(cuts):
        total = refs[n * copies][...].astype(F4)
        for ref in refs[n * copies + 1 : (n + 1) * copies]:
            total = total + ref[...].astype(F4)
        blocks.append(total)
    total = jnp.concatenate(blocks, axis=-1)
    for n, out in enumerate(whole_refs):
        out[...] = untile(total, n)


def place(blocks, experts):
    members, rows, _ = blocks[0].shape
    hidden = sum(block.shape[2] for block in blocks) // 3
    copies = members // experts
    take = 2 if experts % 2 == 0 else 1
    return pl.pallas_call(
        functools.partial(place_kernel, copies, len(blocks)),
        grid=(experts // take,),
        in_specs=[
            pl.BlockSpec(
                (take, rows, block.shape[2]), lambda e, n=n: (n * experts // take + e, 0, 0)
            )
            for block in blocks
            for n in range(copies)
        ],
        out_specs=[pl.BlockSpec((take, rows, hidden), lambda e: (e, 0, 0))] * 3,
        out_shape=[jax.ShapeDtypeStruct((experts, rows, hidden), F4)] * 3,
        compiler_params=params(1),
        name="place",
    )(*[block for block in blocks for n in range(copies)])


def gated_kernel(count, tiles, routed, *refs):
    if routed:
        expert_ref, router_ref, early_ref, x_ref, *refs = refs
        d_ref = refs[3 * count]
    else:
        d_ref, x_ref, *refs = refs
    w_refs, (out_ref, hid_ref, acc_ref) = refs[: 3 * count], refs[-3:]
    step = pl.program_id(0)
    rows, width = x_ref.shape
    tile = hid_ref.shape[1] // 3
    take = min(256, rows)

    @pl.when(step == 0)
    def _():
        acc_ref[...] = jnp.zeros_like(acc_ref)
        if routed:
            logits = dot(x_ref[...], router_ref[...])
            names = lane_of(logits.shape)
            other = early_ref[:, width : width + 1].astype(F4).astype(jnp.int32)
            picked = [
                jnp.sum(jnp.where(names == name, logits, 0.0), axis=1, keepdims=True)
                for name in (expert_ref[0], other)
            ]
            gate = two_gates(picked)[0]
            d_ref[...] = (early_ref[:, :width].astype(F4) * gate).astype(BF)

    for k in range(count):

        @pl.when(step // tiles == k)
        def _(k=k):
            gate_w, up_w, down_w = w_refs[3 * k : 3 * k + 3]
            gate_t, up_t, down_t = gate_w[...].T, up_w[...].T, down_w[...].T
            for r in range(0, rows, take):
                mine = slice(r, r + take)
                x, d = x_ref[mine, :], d_ref[mine, :]
                gate, up, back = dot(x, gate_w[...]), dot(x, up_w[...]), dot(d, down_t)
                share = 1.0 / (1.0 + jnp.exp(-gate))
                silu = gate * share
                hidden = (silu * up).astype(BF)
                dup = (back * silu).astype(BF)
                dgate = (back * up * (share * (1.0 + gate * (1.0 - share)))).astype(BF)
                hid_ref[mine, :tile] = dgate
                hid_ref[mine, tile : 2 * tile] = dup
                hid_ref[mine, 2 * tile :] = hidden
                acc_ref[mine, :width] += dot(hidden, down_w[...])
                acc_ref[mine, width:] += dot(dgate, gate_t) + dot(dup, up_t)

    @pl.when(step == pl.num_programs(0) - 1)
    def _():
        out_ref[...] = acc_ref[...].astype(out_ref.dtype)


def tile_of(hidden):
    return min(512, hidden)


def gated(x, d, parts, kind, name, routed=()):
    rows = x.shape[0]
    width, hidden = parts[0][0].shape
    tile = tile_of(hidden)
    tiles = hidden // tile
    count = len(parts)
    flat, specs = [], []
    for k, part in enumerate(parts):
        at = lambda f, k=k: jnp.clip(f - k * tiles, 0, tiles - 1)
        cols = pl.BlockSpec((width, tile), lambda f, at=at: (0, at(f)))
        lines = pl.BlockSpec((tile, width), lambda f, at=at: (at(f), 0))
        flat += list(part)
        specs += [cols, cols, lines]
    ahead = [SMEM, whole(routed[1].shape)] if routed else []
    gated_out = [(whole((rows, width)), jax.ShapeDtypeStruct((rows, width), BF))] if routed else []
    return pl.pallas_call(
        functools.partial(gated_kernel, count, tiles, bool(routed)),
        grid=(count * tiles,),
        in_specs=ahead + [whole(d.shape), whole(x.shape)] + specs,
        out_specs=[spec for spec, _ in gated_out]
        + [whole((rows, 2 * width)), pl.BlockSpec((rows, 3 * tile), lambda f: (0, f))],
        out_shape=[shape for _, shape in gated_out]
        + [
            jax.ShapeDtypeStruct((rows, 2 * width), kind),
            jax.ShapeDtypeStruct((rows, 3 * count * hidden), BF),
        ],
        scratch_shapes=[pltpu.VMEM((rows, 2 * width), F4)],
        compiler_params=params(1),
        name=name,
    )(*routed, d, x, *flat)


def gated_grads_kernel(x_ref, d_ref, hid_ref, out_ref, xt_ref, dt_ref):
    tile = hid_ref.shape[1] // 3

    @pl.when(pl.program_id(0) == 0)
    def _():
        xt_ref[...] = x_ref[...].T
        dt_ref[...] = d_ref[...].T

    out_ref[:, : 2 * tile] = dot(xt_ref[...], hid_ref[:, : 2 * tile]).astype(BF)
    out_ref[:, 2 * tile :] = dot(dt_ref[...], hid_ref[:, 2 * tile :]).astype(BF)


def gated_grads(x, d, hid, k, count, name):
    rows, width = x.shape
    hidden = hid.shape[1] // 3 // count
    tile = tile_of(hidden)
    tiles = hidden // tile
    return pl.pallas_call(
        gated_grads_kernel,
        grid=(tiles,),
        in_specs=[
            whole(x.shape),
            whole(d.shape),
            pl.BlockSpec((rows, 3 * tile), lambda f: (0, k * tiles + f)),
        ],
        out_specs=pl.BlockSpec((width, 3 * tile), lambda f: (0, f)),
        out_shape=jax.ShapeDtypeStruct((width, 3 * hidden), BF),
        scratch_shapes=[pltpu.VMEM((width, rows), BF)] * 2,
        compiler_params=params(1),
        cost_estimate=pl.CostEstimate(
            flops=6 * rows * width * hidden,
            bytes_accessed=2 * (2 * rows * width + 3 * hidden * (rows + width)),
            transcendentals=0,
        ),
        name=name,
    )(x, d, hid)


def untile(array, n):
    hidden = array.shape[-1] // 3
    tile = tile_of(hidden)
    parts = [
        array[..., (3 * j + n) * tile : (3 * j + n + 1) * tile] for j in range(hidden // tile)
    ]
    return jnp.concatenate(parts, axis=-1)


def per_device(
    inputs,
    cotangent,
    lengths,
    block_pairs,
    routes,
    attn_gain,
    query_weight,
    key_weight,
    value_weight,
    out_weight,
    ffn_gain,
    router_weight,
    expert_gate,
    expert_up,
    expert_down,
    dense_gate,
    dense_up,
    dense_down,
):
    pair_rows, seqs, width = inputs.shape[1:]
    members, size = lax.axis_size("ctx"), lax.axis_size("wt")
    ctx, w = lax.axis_index("ctx"), lax.axis_index("wt")
    experts = expert_gate.shape[0]
    block = pair_rows // 2
    chunk = block // size
    rows = 2 * chunk * seqs
    inner = query_weight.shape[1] * size
    heads = inner // HEAD_DIM
    units = -(-(seqs * heads) // members)

    def rows_of(array, k):
        parted = array.reshape(2, size, chunk, seqs, -1)
        mine = lax.dynamic_index_in_dim(parted, (w + k) % size, 1, False)
        return mine.transpose(2, 0, 1, 3).reshape(seqs, 2 * chunk, -1)

    def places_of(k):
        pair = lax.dynamic_index_in_dim(block_pairs, ctx, 0, False)
        blocks = jnp.stack([pair, 2 * members - 1 - pair])
        core = (w + k) % size
        return (blocks[:, None] * block + core * chunk + jnp.arange(chunk)[None, :]).reshape(-1)

    x = rows_of(inputs[0], 0)
    half = HEAD_DIM // 2
    lane = jnp.arange(LANES)
    freqs = THETA ** (-(lane % half).astype(F4) / half)
    angles = places_of(0).astype(F4)[:, None] * freqs[None, :]
    cosine = jnp.cos(angles)
    sine = jnp.sin(angles) * jnp.where(lane % HEAD_DIM < half, -1.0, 1.0)[None, :]

    local = inner // size
    split = size == 2 and local % LANES == 0
    shift = (w * (heads // size) if split else jnp.zeros_like(w)).astype(jnp.int32)[None]
    own_qkv = [query_weight, key_weight, value_weight]
    if split:
        parts = list(zip(*[wt_gather(weight) for weight in own_qkv]))
        out_parts = wt_gather(out_weight)
    else:
        parts = [[lax.all_gather(weight, "wt", axis=1, tiled=True) for weight in own_qkv]]
        out_parts = [lax.all_gather(out_weight, "wt", axis=0, tiled=True)]
    x, cosine, sine = lax.optimization_barrier((x, cosine, sine))
    msg, a1 = project(shift, x, attn_gain[None], cosine, sine, parts, members, units)
    msg, cotangent, routes = lax.optimization_barrier((msg, cotangent, routes))
    got = lax.all_to_all(msg, "ctx", 0, 0, tiled=True)

    near = 4 if members % 4 == 0 else 1
    outer = members // near
    near_groups = [[o * near + i for i in range(near)] for o in range(outer)]
    far_groups = [[o * near + i for o in range(outer)] for i in range(near)]

    def by_steps(array):
        array = array.reshape(outer, near, width // members, -1).swapaxes(0, 1)
        return array.reshape(width, -1)

    def near_scatter(array):
        return lax.psum_scatter(
            array, "ctx", scatter_dimension=0, tiled=True, axis_index_groups=near_groups
        )

    def far_scatter(array):
        return lax.psum_scatter(
            array, "ctx", scatter_dimension=0, tiled=True, axis_index_groups=far_groups
        )

    a1_turned, back_parts, out_back = turn(a1.reshape(rows, width), parts, out_parts)
    a1_turned = by_steps(a1_turned)
    expert = ctx % experts
    expert_parts = list(
        zip(
            *[
                wt_gather(lax.dynamic_index_in_dim(weights, expert, 0, False))
                for weights in (expert_gate, expert_up, expert_down)
            ]
        )
    )
    total_rows = rows * size
    cots = []
    for k in range(size):
        valid = places_of(k)[None, :] < lengths[:, None]
        cots.append(
            jnp.where(valid[:, :, None], rows_of(cotangent[0], k), jnp.zeros((), BF)).reshape(
                rows, width
            )
        )
    cot = jnp.concatenate(cots)

    parted = routes[0].reshape(2, size, chunk, seqs, 2).transpose(1, 3, 0, 2, 4)
    chosen_all = parted.reshape(total_rows, 2)
    names = jnp.arange(experts, dtype=jnp.int32)
    picks_all = chosen_all[:, :, None] == names
    marks = jnp.any(picks_all, axis=1).astype(BF)
    index = jnp.arange(total_rows)
    before = dot((index[None, :] < index[:, None]).astype(BF), marks)
    order_all = jnp.sum(jnp.where(picks_all, before[:, None, :], 0.0), axis=-1).astype(jnp.int32)
    share = -(-CAPACITY // size)
    held = -(-share // 16) * 16

    def targets(chosen, order, core):
        inside = (order >= core * held) & (order < (core + 1) * held)
        return jnp.where(inside, chosen * held + order - core * held, -1)

    def own_first(array):
        pieces = array.reshape(size, rows, 2)
        pieces = jnp.concatenate([pieces, pieces[:-1]])
        return lax.dynamic_slice_in_dim(pieces, w, size, 0).reshape(total_rows, 2)

    chosen, order_here = own_first(chosen_all), own_first(order_all)
    target = targets(chosen, order_here, w)
    own_targets = [
        targets(chosen[:rows], order_here[:rows], (w + k) % size) for k in range(size)
    ]
    own_info = jnp.concatenate(own_targets + [chosen[:rows]], axis=1)
    own_info = own_info.reshape(seqs, 2 * chunk, -1)
    info = jnp.concatenate([target, chosen, jnp.zeros((total_rows, 4), jnp.int32)], axis=1).T
    router_wide = jnp.pad(router_weight, ((0, 0), (0, LANES - experts)))
    router_turned = router_weight.T
    inv = jnp.argsort(block_pairs).astype(jnp.int32)
    unit_slots = jnp.minimum((ctx + members * jnp.arange(units)) // heads, seqs - 1)
    unit_lengths = lengths[unit_slots]
    w_arg = w.astype(jnp.int32)[None]
    groups = None
    if members != experts:
        groups = [[g * experts + e for e in range(experts)] for g in range(members // experts)]
    swap = functools.partial(
        lax.all_to_all,
        axis_name="ctx",
        split_axis=0,
        concat_axis=0,
        axis_index_groups=groups,
        tiled=True,
    )

    early = dispatch(
        dispatch_early_kernel, info, [cot], width + LANES, experts, held, "dispatch_early"
    )
    (
        got,
        early,
        a1_turned,
        back_parts,
        out_back,
        expert_parts,
        cots,
        cot,
        own_info,
        info,
        router_wide,
        router_turned,
        inv,
        unit_lengths,
    ) = (
        lax.optimization_barrier(
            (
                got,
                early,
                a1_turned,
                back_parts,
                out_back,
                expert_parts,
                cots,
                cot,
                own_info,
                info,
                router_wide,
                router_turned,
                inv,
                unit_lengths,
            )
        )
    )

    blocks = wt_gather(got)
    early = swap(early)
    o_msg, kept, stats = attend(inv, unit_lengths, w_arg, blocks, units)
    o_msg, early = lax.optimization_barrier((o_msg, early))
    o_got = lax.all_to_all(o_msg, "ctx", 0, 0, tiled=True)
    mixed, state, second_own = mix(shift, o_got, x, ffn_gain[None], out_parts)

    seconds = wt_gather(second_own.reshape(rows, width))
    sent = dispatch(dispatch_kernel, info, seconds, width, experts, held, "dispatch")

    sent, seconds = lax.optimization_barrier((sent, seconds))
    second = jnp.concatenate(seconds)
    arrived = swap(sent)
    dense, dense_hid = gated(second, cot, [[dense_gate, dense_up, dense_down]], F4, "dense_branch")
    dense_grads = gated_grads(second, cot, dense_hid, 0, 1, "dense_grads")
    dense_grads = by_steps(dense_grads)
    denses = [dense[:rows]]
    for k in range(1, size):
        perm = [(i, (i + k) % size) for i in range(size)]
        denses.append(lax.ppermute(dense[k * rows : (k + 1) * rows], "wt", perm))
    arrived, denses, dense_grads = lax.optimization_barrier((arrived, denses, dense_grads))
    dense = denses[0]
    for part in denses[1:]:
        dense = dense + part
    dense_near = near_scatter(dense_grads)

    arrived = arrived.reshape(experts * held, width)
    dye, returned, hid = gated(
        arrived,
        early.reshape(experts * held, -1),
        expert_parts,
        BF,
        "expert_branch",
        (expert.astype(jnp.int32)[None], router_wide),
    )
    home = swap(returned.reshape(experts, held, 2 * width))
    hidden = expert_gate.shape[2]
    expert_sum = None
    for k in list(range(1, size)) + [0]:
        made = gated_grads(arrived, dye, hid, k, size, "expert_grads")
        if k:
            made = lax.ppermute(made, "wt", [(i, (i + k) % size) for i in range(size)])
        expert_sum = made.astype(F4) if expert_sum is None else expert_sum + made.astype(F4)
    expert_sum = expert_sum.astype(BF).reshape(members, width // members, 3 * hidden)
    cut = 3 * hidden // 2
    expert_sum = [expert_sum[:, :, :cut], expert_sum[:, :, cut:]]
    home, expert_sum, dense_near, dense = lax.optimization_barrier(
        (home, expert_sum, dense_near, dense)
    )
    dense_sum = far_scatter(dense_near)
    homes = wt_gather(home.reshape(experts * held, 2 * width))
    first = first_part(own_info, homes[0])

    own_cot = cots[0].reshape(seqs, 2 * chunk, width)
    dense = dense.reshape(seqs, 2 * chunk, 2 * width)
    output, dstate, dstate_low, logit_back, do_msg, ffn_grad = finish(
        shift,
        own_info,
        second_own,
        state,
        own_cot,
        ffn_gain[None],
        router_wide,
        router_turned,
        homes[1:],
        first,
        dense,
        out_back,
        members,
        units,
    )
    do_got = lax.all_to_all(do_msg, "ctx", 0, 0, tiled=True)

    def share_of(array, kinds, k):
        if split:
            return array[..., k * kinds * local : (k + 1) * kinds * local].reshape(rows, -1)
        cols = array.reshape(rows, kinds, size, local)
        return lax.dynamic_index_in_dim(cols, (w + k) % size, 2, False).reshape(rows, -1)

    def split_wt(left, right, kinds):
        pieces = []
        for k in range(size):
            made = dot_tn(left.reshape(rows, -1), share_of(right, kinds, k))
            pieces.append(made if k == 0 else made.astype(BF))
        return wt_scatter(pieces).astype(BF)

    router_grad = dot_tn(second_own.reshape(rows, width), logit_back.reshape(rows, experts))
    small = wt_sum(jnp.concatenate([ffn_grad.T, router_grad], axis=1))
    small_high = small.astype(BF)
    small_low = (small - small_high.astype(F4)).astype(BF)
    few = experts + 1
    blank = jnp.zeros((width, -(2 * few) % LANES), BF)
    out_msg = [split_wt(dstate_low, mixed, 1), small_high, small_low, blank]
    out_msg = by_steps(jnp.concatenate(out_msg, axis=1))
    do_got, out_msg, output, dense_sum, expert_sum = lax.optimization_barrier(
        (do_got, out_msg, output, dense_sum, expert_sum)
    )
    expert_got = [lax.all_to_all(expert_sum[0], "ctx", 0, 0, tiled=True)]
    out_near = near_scatter(out_msg)
    dq, *dkv = attend_back(inv, unit_lengths, w_arg, blocks, do_got, kept, stats, units)
    dq, dkv, expert_got, out_near = lax.optimization_barrier((dq, dkv, expert_got, out_near))
    out_sum = far_scatter(out_near)
    dkv = wt_scatter([dkv[0].astype(F4), *dkv[1:]]).astype(BF)
    grad_msg = jnp.concatenate([dkv, dq], axis=1)
    grad_got = lax.all_to_all(grad_msg, "ctx", 0, 0, tiled=True)
    grad_got, out_sum, expert_sum = lax.optimization_barrier((grad_got, out_sum, expert_sum))
    expert_got.append(lax.all_to_all(expert_sum[1], "ctx", 0, 0, tiled=True))
    count = len(parts)
    dqkv, last_msg = [None] * count, None
    for k in list(range(1, count)) + [0]:
        dqkv[k], made = unrotate(shift, grad_got, cosine, sine, a1_turned, seqs, heads, k, count)
        if k:
            made = lax.ppermute(made, "wt", [(i, (i + k) % size) for i in range(size)])
        last_msg = made.astype(F4) if last_msg is None else last_msg + made.astype(F4)
    if split:
        last_msg = last_msg.astype(BF)
    else:
        last_msg = by_steps(split_wt(a1, dqkv[0], 3))
    last_sum = far_scatter(near_scatter(last_msg))
    dx, attn_grad = unproject(shift, dqkv, x, dstate, attn_gain[None], back_parts)
    attn_grad = ctx_sum(wt_sum(attn_grad)).reshape(members, -1)
    attn_grad = lax.dynamic_index_in_dim(attn_grad, ctx, 0, False)
    expert_grads = place(expert_got, experts)
    last_sum = last_sum.astype(F4)
    out_sum = out_sum.astype(F4)
    tail = out_sum[:, local:]
    tail = tail[:, :few] + tail[:, few : 2 * few]

    def to_tokens(own):
        array = in_order(wt_gather(own)).reshape(size, seqs, 2, chunk, width)
        return array.transpose(2, 0, 3, 1, 4).reshape(inputs.shape)

    return (
        to_tokens(output),
        to_tokens(dx),
        attn_grad,
        *[last_sum[:, n * local : (n + 1) * local] for n in range(3)],
        out_sum[:, :local].T,
        tail[:, 0],
        tail[:, 1:],
        *expert_grads[:2],
        expert_grads[2].transpose(0, 2, 1),
        *[untile(dense_sum, n).astype(F4) for n in range(2)],
        untile(dense_sum, 2).astype(F4).T,
    )


def solution(mesh):
    placed = (
        P("ctx", None, None, None),
        P("ctx", None, None, None),
        P(),
        P(),
        P("ctx", None, None, None),
        P(),
        P(None, "wt"),
        P(None, "wt"),
        P(None, "wt"),
        P("wt", None),
        P(),
        P(),
        P(None, None, "wt"),
        P(None, None, "wt"),
        P(None, "wt", None),
        P(None, "wt"),
        P(None, "wt"),
        P("wt", None),
    )
    return jax.shard_map(
        per_device,
        mesh=mesh,
        in_specs=placed,
        out_specs=(
            P("ctx", None, None, None),
            P("ctx", None, None, None),
            P("ctx"),
            P("ctx", "wt"),
            P("ctx", "wt"),
            P("ctx", "wt"),
            P("wt", "ctx"),
            P("ctx"),
            P("ctx", None),
            P(None, "ctx", "wt"),
            P(None, "ctx", "wt"),
            P(None, "wt", "ctx"),
            P("ctx", "wt"),
            P("ctx", "wt"),
            P("wt", "ctx"),
        ),
        check_vma=False,
    )
```
